32 devices in a mesh: section: 4 (over y, x), dp: 8 (over z, core).
Axes of the slice: x: 2, y: 2, z: 4, core: 2. Of those that a mesh axis runs over, the one named last changes fastest.
Arguments:
- hidden_in: bfloat16 [8, 3, 128, 768], P('dp'), may hold values from -6 to 6
- cotangent: bfloat16 [8, 3, 128, 768], P('dp'), may hold values from -6 to 6
- doc_lengths: int32 [8, 3, 4], P('dp'), may hold values from 0 to 64, as said below
- attn_weight: bfloat16 [4, 768, 1536], P('section')
- up_weight: bfloat16 [4, 768, 1536], P('section'), may hold values from -0.21875 to 0.21875
- down_weight: bfloat16 [4, 1536, 768], P('section'), may hold values from -0.109375 to 0.109375
- up_bias: bfloat16 [4, 1536], P('section'), may hold values from -3 to 3
- down_bias: bfloat16 [4, 384], P('section'), may hold values from -3 to 3
- norm_gain: float32 [4, 768], P('section'), may hold values from 0.1 to 1.9
Outputs:
- section_outputs: bfloat16 [4, 8, 3, 128, 768], P('section', 'dp')
- input_grads: bfloat16 [4, 8, 3, 128, 768], P('section', 'dp')
- attn_weight_grad: float32 [4, 768, 1536], P('section', 'dp')
- up_weight_grad: float32 [4, 768, 1536], P('section', 'dp')
- down_weight_grad: float32 [4, 1536, 768], P('section', 'dp')
- up_bias_grad: float32 [4, 1536], P('section', 'dp')
- down_bias_grad: float32 [4, 384], P('section', 'dp')
- gain_grad: float32 [4, 768], P('section', 'dp')
The draws below stay inside these ranges and needn't reach their ends.
Inputs may be any that keep to these rules, and one draw needn't show every extreme that they name: `doc_lengths`: each row of 4 lengths sums to 64; in every replica one micro-batch, drawn from the seed, holds a single document of 64 positions.
All inputs are finite; a program needn't handle non-finite values.
Results may differ from the reference program's by a relative error of at most 0.02.
Values may be sent and summed in bfloat16 or wider, within the bound.
No kernel may reach another device: no remote copies, remote signals or barrier semaphores. Data moves between devices by JAX's collectives and lax.ppermute only.
A program may use at most 192 MiB of HBM per device.

```python
import jax
import jax.numpy as jnp
from jax import lax

D = 768
HEADS = 12
HEAD = 64
FF = 3072
BLOCK = 16
DOCS = 4
MICRO = 3
SEQ = 64
ROWS = 128
REPLICAS = 8
N_SECTION = 4


OUT_GAIN = 5.0


def draw_doc_lengths(key, part):
    key = jax.random.fold_in(key, 11)
    cut_key, pick_key = jax.random.split(key)
    cuts = jax.random.randint(cut_key, (REPLICAS, MICRO, DOCS - 1), 0, SEQ + 1)
    cuts = jnp.sort(cuts, axis=-1)
    lower = jnp.zeros((REPLICAS, MICRO, 1), jnp.int32)
    upper = jnp.full((REPLICAS, MICRO, 1), SEQ, jnp.int32)
    edges = jnp.concatenate([lower, cuts.astype(jnp.int32), upper], axis=-1)
    pieces = edges[..., 1:] - edges[..., :-1]
    chosen = jax.random.randint(pick_key, (REPLICAS, 1), 0, MICRO)
    single = (jnp.arange(DOCS) == 0).astype(jnp.int32) * SEQ
    whole = (jnp.arange(MICRO)[None, :] == chosen)[..., None]
    return jnp.where(whole, single[None, None, :], pieces).astype(jnp.int32)


def draw_attn_weight(key, part):
    key = jax.random.fold_in(key, 23)
    extent = (N_SECTION, D, 2 * D)
    column = jnp.arange(2 * D)[None, None, :]
    second = (jnp.arange(N_SECTION) % 2 == 1)[:, None, None]
    factor = jnp.where(second & (column >= D), OUT_GAIN, 1.0) / jnp.sqrt(jnp.float32(D))
    base = jax.random.normal(key, extent, jnp.float32)
    return (base * factor).astype(jnp.bfloat16)


def with_spikes(result, own_key, source, target, blocks, factor):
    owner, partner = [(jnp.arange(result.shape[axis_at]) // (result.shape[axis_at] // blocks)).reshape([-1 if axis == axis_at else 1 for axis in range(result.ndim)]) for axis_at in (source, target)]
    chosen = jax.random.permutation(own_key, blocks)[partner]
    strong = (owner == chosen) | (owner == (partner + blocks // 2) % blocks)
    return jnp.where(strong, factor * result, result)


def block_scale(rng, shape, cuts, smallest, top_value):
    level = 1.0
    for dim, parts in cuts:
        draws = jax.random.uniform(jax.random.fold_in(jax.random.fold_in(rng, 6), dim), (parts,), jnp.float32, smallest / len(cuts), top_value / len(cuts))
        level = level * jnp.repeat(jnp.exp(draws), shape[dim] // parts).reshape((-1,) + (1,) * (len(shape) - 1 - dim))
    return level


def noise(stream_key, dims, scale, reach, cuts=(), held_as=jnp.bfloat16):
    level = block_scale(stream_key, dims, cuts, -0.22, 0.18) if cuts else 1.0
    values = jax.random.normal(stream_key, dims, jnp.float32) * scale * level
    return jnp.minimum(jnp.maximum(values, -reach), reach).astype(held_as)


def heavy_noise(key, shape, deviation, reach, cuts, heavy, held_as=jnp.bfloat16):
    entries = deviation * jax.random.normal(key, shape, jnp.float32)
    if cuts:
        entries = entries * block_scale(key, shape, cuts, -0.22, 0.18)
    return jnp.clip(with_spikes(entries, jax.random.fold_in(key, 3), *heavy), -reach, reach).astype(held_as)


def setup_inputs(seed: int = 0) -> dict:
    splits = jax.random.split(jax.random.key(seed), 10)
    hidden_in = noise(splits[0], (REPLICAS, MICRO, ROWS, D), 1.0, 6.0, ((0, 8),))
    cotangent = heavy_noise(splits[1], (REPLICAS, MICRO, ROWS, D), 1.0, 6.0, ((0, 8),), (0, 3, 8, 2.0))
    doc_lengths = draw_doc_lengths(jax.random.fold_in(splits[9], 71), 0)
    attn_weight = draw_attn_weight(jax.random.fold_in(splits[9], 71), 0)
    up_weight = noise(splits[4], (N_SECTION, D, FF // 2), D ** -0.5, 0.21875, ((0, 4),))
    down_weight = noise(splits[5], (N_SECTION, FF // 2, D), FF ** -0.5, 0.109375, ((0, 4),))
    up_bias = noise(splits[6], (N_SECTION, FF // 2), 0.5, 3.0, ((0, 4),))
    down_bias = noise(splits[7], (N_SECTION, D // 2), 0.5, 3.0, ((0, 4),))
    norm_gain = jnp.clip(1.0 + 0.18 * jax.random.normal(splits[8], (N_SECTION, D), jnp.float32), 0.1, 1.9)
    return {"hidden_in": hidden_in, "cotangent": cotangent, "doc_lengths": doc_lengths, "attn_weight": attn_weight, "up_weight": up_weight, "down_weight": down_weight, "up_bias": up_bias, "down_bias": down_bias, "norm_gain": norm_gain}


EPSILON = 1e-05
MASKED = -1e+30
HIGH = lax.Precision.HIGHEST

@jax.custom_vjp
def low(v):
    return lax.optimization_barrier(v.astype(jnp.bfloat16)).astype(jnp.float32)

@jax.custom_vjp
def low_back(v):
    return v

def low_keep(v):
    return (low(v), None)

def low_pass(kept, grad):
    return (grad,)

def back_keep(v):
    return (v, None)

def back_low(kept, grad):
    return (low(grad),)
low.defvjp(low_keep, low_pass)
low_back.defvjp(back_keep, back_low)

def layer_norm(values, gain):
    mean = lax.optimization_barrier(jnp.mean(values, axis=-1, keepdims=True))
    centered = values - mean
    spread = lax.optimization_barrier(jnp.mean(centered * centered, axis=-1, keepdims=True))
    return centered * lax.rsqrt(spread + EPSILON) * gain

def row_layout(lengths, rows):
    half = rows // 2
    place = jnp.arange(rows, dtype=jnp.int32)
    clean = place >= half
    within = jnp.where(clean, place - half, place)
    ends = jnp.cumsum(lengths).astype(jnp.int32)
    passed = (within[:, None] >= ends[None, :]).astype(jnp.int32)
    document = lax.optimization_barrier(jnp.sum(passed, axis=1))
    start = lax.optimization_barrier(jnp.sum(passed * lengths[None, :], axis=1))
    offset = within - start
    return (document, offset // BLOCK, clean, offset)

def visible(query_side, key_side):
    query_doc, query_block, query_clean = query_side
    key_doc, key_block, key_clean = key_side
    same = query_doc[:, None] == key_doc[None, :]
    upto = key_block[None, :] <= query_block[:, None]
    before = key_block[None, :] < query_block[:, None]
    equal = key_block[None, :] == query_block[:, None]
    clean_key = key_clean[None, :]
    rule = jnp.where(query_clean[:, None], clean_key & upto, jnp.where(clean_key, before, equal))
    return same & rule

def rotation(offset):
    count = HEAD // 2
    freq = jnp.power(10000.0, -2.0 * jnp.arange(count, dtype=jnp.float32) / HEAD)
    angle = offset.astype(jnp.float32)[:, None] * freq[None, :]
    return (jnp.cos(angle)[:, None, :], jnp.sin(angle)[:, None, :])

def rotate(values, cosine, sine):
    count = values.shape[-1] // 2
    first = values[..., :count]
    second = values[..., count:]
    return jnp.concatenate([first * cosine - second * sine, second * cosine + first * sine], axis=-1)

def attend(stream, layout, mixing, gain):
    document, blocks, clean, offset = layout
    rows = stream.shape[0]
    cosine, sine = rotation(offset)
    normed = low(layer_norm(stream, gain))
    project = jnp.dot(normed, mixing[:, :3 * D], precision=HIGH)
    query = low(rotate(low_back(project[:, :D]).reshape(rows, HEADS, HEAD), cosine, sine))
    keys = low(rotate(low_back(project[:, D:2 * D]).reshape(rows, HEADS, HEAD), cosine, sine))
    values = low(low_back(project[:, 2 * D:])).reshape(rows, HEADS, HEAD)
    side = (document, blocks, clean)
    mask = visible(side, side)
    scores = jnp.einsum('qhd,khd->hqk', query, keys, precision=HIGH) * HEAD ** (-0.5)
    scores = low_back(jnp.where(mask[None], scores, MASKED))
    weights = low(jax.nn.softmax(scores, axis=-1))
    mixed = jnp.einsum('hqk,khd->qhd', weights, values, precision=HIGH).reshape(rows, D)
    mixed = low(low_back(mixed))
    return stream + jnp.einsum('tj,ij->ti', mixed, mixing[:, 3 * D:], precision=HIGH)

def feed(stream, upward, downward, up_shift, down_shift, gain):
    normed = low(layer_norm(stream, gain))
    before = low_back(jnp.dot(normed, upward, precision=HIGH) + up_shift)
    active = low(jax.nn.gelu(before, approximate=True))
    return stream + jnp.dot(active, downward, precision=HIGH) + down_shift

def micro_forward(params, stream, spare, lengths):
    attn_all, up_all, down_all, up_bias_all, down_bias_all, gains = params
    layout = row_layout(lengths, stream.shape[0])
    results = []
    for layer in range(N_SECTION // 2):
        lower = 2 * layer
        upper = 2 * layer + 1
        mixing = jnp.concatenate([attn_all[lower], attn_all[upper]], axis=1)
        stream = low_back(low(attend(stream, layout, mixing, gains[lower]) + spare[lower]))
        results.append(stream)
        upward = jnp.concatenate([up_all[lower], up_all[upper]], axis=1)
        downward = jnp.concatenate([down_all[lower], down_all[upper]], axis=0)
        up_shift = jnp.concatenate([up_bias_all[lower], up_bias_all[upper]], axis=0)
        down_shift = jnp.concatenate([down_bias_all[lower], down_bias_all[upper]], axis=0)
        stream = low_back(low(feed(stream, upward, downward, up_shift, down_shift, gains[upper]) + spare[upper]))
        results.append(stream)
    return (stream, jnp.stack(results))

def reference(hidden_in, cotangent, doc_lengths, attn_weight, up_weight, down_weight, up_bias, down_bias, norm_gain):
    batches = REPLICAS * MICRO
    stream_all = hidden_in.astype(jnp.float32).reshape(batches, ROWS, D)
    lengths_all = doc_lengths.reshape(batches, DOCS)
    params = (attn_weight.astype(jnp.float32), up_weight.astype(jnp.float32), down_weight.astype(jnp.float32), up_bias.astype(jnp.float32), down_bias.astype(jnp.float32), norm_gain.astype(jnp.float32))
    spare_all = jnp.zeros((batches, N_SECTION, ROWS, D), jnp.float32)

    def whole(stream_all, params, spare_all):

        def step(carry, item):
            stream, spare, lengths = item
            final, middle = micro_forward(params, stream, spare, lengths)
            return (carry, (final, middle))
        _, (finals, middles) = lax.scan(jax.checkpoint(step), jnp.zeros((), jnp.float32), (stream_all, spare_all, lengths_all))
        return (finals, middles)
    finals, pull, middles = jax.vjp(whole, stream_all, params, spare_all, has_aux=True)
    grad_stream, grad_params, grad_spare = pull(cotangent.astype(jnp.float32).reshape(batches, ROWS, D))
    section_outputs = jnp.transpose(middles, (1, 0, 2, 3)).reshape(N_SECTION, REPLICAS, MICRO, ROWS, D)
    gathered = jnp.stack([grad_stream, grad_spare[:, 0], grad_spare[:, 1], grad_spare[:, 2]], axis=0)
    input_grads = gathered.reshape(N_SECTION, REPLICAS, MICRO, ROWS, D)
    return (section_outputs.astype(jnp.bfloat16), input_grads.astype(jnp.bfloat16), grad_params[0], grad_params[1], grad_params[2], grad_params[3], grad_params[4], grad_params[5])
```

```python
import jax
import jax.numpy as jnp
from jax import lax
from jax.experimental import pallas as pl
from jax.experimental.pallas import tpu as pltpu
from jax.sharding import PartitionSpec as P

HEAD = 64
BLOCK = 16
EPSILON = 1e-05
MASKED = -1e30
LANES = 128
LINE = 4
F32 = jnp.float32
BF16 = jnp.bfloat16


def dot(left, right):
    return lax.dot_general(left, right, (((1,), (0,)), ((), ())), preferred_element_type=F32)


def dot_cols(left, right):
    return lax.dot_general(left, right, (((1,), (1,)), ((), ())), preferred_element_type=F32)


def dot_rows(left, right):
    return lax.dot_general(left, right, (((0,), (0,)), ((), ())), preferred_element_type=F32)


def normalized(values):
    mean = jnp.mean(values, axis=-1, keepdims=True)
    centered = values - mean
    spread = jnp.mean(centered * centered, axis=-1, keepdims=True)
    rstd = lax.rsqrt(spread + EPSILON)
    return centered * rstd, rstd


def norm_backward(values, gain, upstream, grad_normed):
    xhat, rstd = normalized(values)
    scaled = grad_normed * gain
    mean = jnp.mean(scaled, axis=-1, keepdims=True)
    along = jnp.mean(scaled * xhat, axis=-1, keepdims=True)
    grad_gain = jnp.sum(grad_normed * xhat, axis=0, keepdims=True)
    grad = upstream.astype(F32) + rstd * (scaled - mean - xhat * along)
    return grad.astype(BF16), grad_gain


def swap_halves(block):
    lane = lax.broadcasted_iota(jnp.int32, block.shape, 1)
    low = lax.rem(lane, HEAD) < HEAD // 2
    ahead = pltpu.roll(block, LANES - HEAD // 2, 1)
    behind = pltpu.roll(block, HEAD // 2, 1)
    return jnp.where(low, ahead, behind)


def side(lengths, rows, axis):
    place = lax.broadcasted_iota(jnp.int32, (rows, rows), axis)
    half = rows // 2
    clean = place >= half
    within = jnp.where(clean, place - half, place)
    document = jnp.zeros((rows, rows), jnp.int32)
    start = jnp.zeros((rows, rows), jnp.int32)
    end = jnp.int32(0)
    for length in lengths:
        end = end + length
        passed = (within >= end).astype(jnp.int32)
        document = document + passed
        start = start + passed * length
    return document, (within - start) // BLOCK, clean


def visible(lengths, rows):
    query_doc, query_block, query_clean = side(lengths, rows, 0)
    key_doc, key_block, key_clean = side(lengths, rows, 1)
    upto = key_block <= query_block
    before = key_block < query_block
    equal = key_block == query_block
    noisy = jnp.logical_not(query_clean)
    rule = (query_clean & key_clean & upto) | (
        noisy & ((key_clean & before) | (jnp.logical_not(key_clean) & equal))
    )
    return (query_doc == key_doc) & rule


def stacked(pair):
    lane = lax.broadcasted_iota(jnp.int32, pair.shape, 1)
    zero = jnp.zeros_like(pair)
    return jnp.concatenate(
        [jnp.where(lane < HEAD, pair, zero), jnp.where(lane < HEAD, zero, pair)], axis=0
    )


def merged(stack, rows):
    lane = lax.broadcasted_iota(jnp.int32, (rows, LANES), 1)
    return jnp.where(lane < HEAD, stack[:rows], stack[rows:])


def attend_kernel(micro, docs, keep, x, gain, lens, qk, ve, cosine, sine, *refs):
    if keep:
        partial, normed_out, q, k, v, mixed, chance = refs
    else:
        partial, q, k, v, mixed = refs
        normed_out, chance = None, None
    total, width = x.shape
    half = width // 2
    rows = total // micro
    xhat, _ = normalized(x[...].astype(F32))
    normed = (xhat * gain[...]).astype(BF16)
    if keep:
        normed_out[...] = normed
    values = dot(normed, ve[:, :half])
    v[...] = values.astype(BF16)
    cos, sin = cosine[...], sine[...]
    for low, target in ((0, q), (half, k)):
        wide = dot(normed, qk[:, low : low + half])
        for at in range(0, half, LANES):
            block = wide[:, at : at + LANES]
            target[:, at : at + LANES] = (block * cos + swap_halves(block) * sin).astype(BF16)
    for item in range(micro):
        spot = pl.ds(item * rows, rows)
        mask = visible([lens[item, j] for j in range(docs)], rows)
        mask = jnp.concatenate([mask, mask], axis=0)
        for pair in range(half // LANES):
            lanes = pl.ds(pair * LANES, LANES)
            scores = dot_cols(stacked(q[spot, lanes]), k[spot, lanes]) * HEAD ** (-0.5)
            scores = jnp.where(mask, scores, MASKED)
            peak = jnp.max(scores, axis=-1, keepdims=True)
            powers = jnp.exp(scores - peak)
            weights = powers / jnp.sum(powers, axis=-1, keepdims=True)
            if keep:
                chance[item * (half // LANES) + pair] = weights
            mixed[spot, lanes] = merged(dot(weights.astype(BF16), v[spot, lanes]), rows).astype(BF16)
    partial[...] = dot_cols(mixed[...], ve[:, half:])


def feed_kernel(keep, x, own, other, gain, up_mine, up_theirs, down_mine, down_theirs, shift, *refs):
    if keep:
        partial, stream, normed_out, active_mine, active_theirs, slope = refs
    else:
        partial, stream, active_mine, active_theirs = refs
        normed_out, slope = None, None
    rows, width = x.shape
    result = (x[...].astype(F32) + (own[...] + other[...])).astype(BF16)
    stream[...] = result
    xhat, _ = normalized(result.astype(F32))
    normed = (xhat * gain[...]).astype(BF16)
    if keep:
        normed_out[...] = normed
    scale = (2.0 / jnp.pi) ** 0.5
    piece = 256
    for index, (up, active) in enumerate(((up_mine, active_mine), (up_theirs, active_theirs))):
        for at in range(0, width, piece):
            before = dot(normed, up[:, at : at + piece])
            before = before + shift[:, index * width + at : index * width + at + piece]
            square = before * before
            bend = jnp.tanh(scale * before * (1.0 + 0.044715 * square))
            active[:, at : at + piece] = (0.5 * before * (1.0 + bend)).astype(BF16)
            if keep:
                inner = scale * (1.0 + 3 * 0.044715 * square)
                tilt = 0.5 * (1.0 + bend) + 0.5 * before * (1.0 - bend * bend) * inner
                slope[:, index * width + at : index * width + at + piece] = tilt.astype(BF16)
    partial[...] = dot(active_mine[...], down_mine[...]) + dot(active_theirs[...], down_theirs[...])


def feed_back_kernel(dz, slope, up_mine, up_theirs, down_mine, down_theirs, partial, back_mine, back_theirs, sums):
    rows, width = dz.shape
    upstream = dz[...]
    piece = 256
    totals = []
    for index, (down, back) in enumerate(((down_mine, back_mine), (down_theirs, back_theirs))):
        for at in range(0, width, piece):
            grad = dot_cols(upstream, down[at : at + piece, :])
            grad = grad * slope[:, index * width + at : index * width + at + piece].astype(F32)
            rounded = grad.astype(BF16)
            back[:, at : at + piece] = rounded
            sums[index : index + 1, at : at + piece] = jnp.sum(
                rounded.astype(F32), axis=0, keepdims=True
            )
    sums[2:3, :] = jnp.sum(upstream.astype(F32), axis=0, keepdims=True)
    sums[3:, :] = jnp.zeros((sums.shape[0] - 3, width), F32)
    partial[...] = dot_cols(back_mine[...], up_mine[...]) + dot_cols(back_theirs[...], up_theirs[...])


def attend_back_kernel(
    micro, x, gain, dz, own, other, qk, ve, q, k, v, mixed, chance, cosine, sine, flag,
    partial, grad, grad_gain, rhs, pay, dq, dk, dv, dmixed,
):
    total, width = x.shape
    half = width // 2
    rows = total // micro
    result, gain_sum = norm_backward(
        x[...].astype(F32), gain[...], dz[...], own[...] + other[...]
    )
    grad[...] = result
    grad_gain[...] = jnp.broadcast_to(gain_sum, grad_gain.shape)
    dmixed[...] = dot(result, ve[:, half:]).astype(BF16)
    cos, sin = cosine[...], sine[...]
    for item in range(micro):
        spot = pl.ds(item * rows, rows)
        turn, tilt = cos[item * rows : (item + 1) * rows], sin[item * rows : (item + 1) * rows]
        for pair in range(half // LANES):
            lanes = pl.ds(pair * LANES, LANES)
            weights = chance[item * (half // LANES) + pair]
            grads = stacked(dmixed[spot, lanes])
            queries = stacked(q[spot, lanes])
            dv[spot, lanes] = dot_rows(weights.astype(BF16), grads).astype(BF16)
            spread = dot_cols(grads, v[spot, lanes])
            inner = jnp.sum(weights * spread, axis=-1, keepdims=True)
            scores = (weights * (spread - inner)).astype(BF16)
            query_grad = merged(dot(scores, k[spot, lanes]), rows) * HEAD ** (-0.5)
            key_grad = dot_rows(scores, queries) * HEAD ** (-0.5)
            dq[spot, lanes] = (query_grad * turn - swap_halves(query_grad) * tilt).astype(BF16)
            dk[spot, lanes] = (key_grad * turn - swap_halves(key_grad) * tilt).astype(BF16)
    partial[...] = (
        dot_cols(dq[...], qk[:, :half]) + dot_cols(dk[...], qk[:, half:]) + dot_cols(dv[...], ve[:, :half])
    )
    if rhs is not None:
        even = flag[0] == 0
        rhs[:, :half] = jnp.where(even, dq[...], dv[...])
        rhs[:, half:] = jnp.where(even, dk[...], mixed[...])
        pay[:, :half] = jnp.where(even, dv[...], dq[...])
        pay[:, half:] = jnp.where(even, mixed[...], dk[...])


def norm_back_kernel(x, gain, dz, own, other, grad, grad_gain):
    result, gain_sum = norm_backward(
        x[...].astype(F32), gain[...], dz[...], own[...] + other[...]
    )
    grad[...] = result
    grad_gain[...] = jnp.broadcast_to(gain_sum, grad_gain.shape)


def pair_kernel(left_a, right_a, left_b, right_b, out):
    out[...] = (dot_rows(left_a[...], right_a[...]) + dot_rows(left_b[...], right_b[...])).astype(BF16)


def attend_weight_kernel(left_a, left_b, right_a, right_b, far_a, far_b, out):
    half = right_a.shape[1] // 2
    out[:, :half] = (
        dot_rows(left_a[...], right_a[:, :half]) + dot_rows(left_b[...], right_b[:, :half])
    ).astype(BF16)
    out[:, half:] = (
        dot_rows(far_a[...], right_a[:, half:]) + dot_rows(far_b[...], right_b[:, half:])
    ).astype(BF16)


VECTOR = pl.BlockSpec(memory_space=pltpu.VMEM)
SCALAR = pl.BlockSpec(memory_space=pltpu.SMEM)


def call(kernel, args, outs, flops, scratch=(), name=None):
    outs = [jax.ShapeDtypeStruct(shape, dtype) for shape, dtype in outs]
    moved = sum(a.size * a.dtype.itemsize for a in args) + sum(
        o.size * jnp.dtype(o.dtype).itemsize for o in outs
    )
    return pl.pallas_call(
        kernel,
        out_shape=outs,
        in_specs=[SCALAR if a.dtype == jnp.int32 else VECTOR for a in args],
        out_specs=[VECTOR] * len(outs),
        scratch_shapes=list(scratch),
        compiler_params=pltpu.CompilerParams(vmem_limit_bytes=48 * 1024 * 1024),
        cost_estimate=pl.CostEstimate(flops=int(flops), bytes_accessed=int(moved), transcendentals=0),
        name=name,
    )(*args)


def swap_section(x):
    return lax.ppermute(x, "section", [(i, i ^ 1) for i in range(lax.axis_size("section"))])


def swap_core(x):
    return lax.ppermute(x, "dp", [(i, i ^ 1) for i in range(lax.axis_size("dp"))])


def to_layer(x, step):
    count = lax.axis_size("section")
    route = [(i, i + step) for i in range(count) if 0 <= i + step < count]
    return lax.ppermute(x, "section", route)


def swap_lead(x):
    count = lax.axis_size("dp")
    route = [
        (s * count + d, (s ^ 1) * count + d)
        for s in range(lax.axis_size("section"))
        for d in range(count)
        if d % 2 == s % 2
    ]
    return lax.ppermute(x, ("section", "dp"), route)


def line_sum(parts, z, chips):
    def piece(index):
        return lax.dynamic_index_in_dim(parts, jnp.clip(index, 0, chips - 1), 0, keepdims=False)

    right, left = None, None
    for step in range(chips - 1):
        send_right = piece(chips - 1 - step + z)
        send_left = piece(step - (chips - 1) + z)
        if step:
            send_right = (send_right.astype(F32) + right.astype(F32)).astype(BF16)
            send_left = (send_left.astype(F32) + left.astype(F32)).astype(BF16)
        right = lax.ppermute(
            send_right, "dp", [(2 * i + c, 2 * i + 2 + c) for i in range(step + 1) for c in (0, 1)]
        )
        left = lax.ppermute(
            send_left,
            "dp",
            [(2 * (chips - 1 - i) + c, 2 * (chips - 2 - i) + c) for i in range(step + 1) for c in (0, 1)],
        )
    return piece(z).astype(F32) + right.astype(F32) + left.astype(F32)


def replica_sum(parts, z, chips):
    if chips <= LINE:
        return line_sum(parts, z, chips)
    groups = [[2 * i + c for i in range(chips)] for c in (0, 1)]
    return lax.psum_scatter(
        parts, "dp", scatter_dimension=0, axis_index_groups=groups, tiled=False
    ).astype(F32)


def rotation_tables(lengths, rows):
    half = rows // 2
    place = jnp.arange(rows, dtype=jnp.int32)
    within = jnp.where(place >= half, place - half, place)
    ends = jnp.cumsum(lengths, axis=1)
    passed = (within[None, :, None] >= ends[:, None, :]).astype(jnp.int32)
    offset = (within[None] - jnp.sum(passed * lengths[:, None, :], axis=2)).reshape(-1)
    count = HEAD // 2
    freq = jnp.power(10000.0, -2.0 * jnp.arange(count, dtype=F32) / HEAD)
    angle = offset.astype(F32)[:, None] * freq[None, :]
    cosine, sine = jnp.cos(angle), jnp.sin(angle)
    cosine = jnp.concatenate([cosine] * (LANES // count), axis=1)
    sine = jnp.concatenate([-sine, sine] * (LANES // HEAD), axis=1)
    return cosine, sine


def body(
    hidden_in,
    cotangent,
    doc_lengths,
    attn_weight,
    up_weight,
    down_weight,
    up_bias,
    down_bias,
    norm_gain,
):
    section = lax.axis_index("section")
    replica = lax.axis_index("dp")
    chips = lax.axis_size("dp") // 2
    part, layer = section % 2, section // 2
    core, z = replica % 2, replica // 2
    even, lead, first = part == 0, core == part, layer == 0
    micro, rows, width = hidden_in.shape[1:]
    docs = doc_lengths.shape[2]
    total, half = micro * rows, width // 2
    hidden = up_weight.shape[2]
    flag = part.reshape(1)
    blocks = micro * (half // LANES)

    def columns(x, at, size):
        return lax.dynamic_slice_in_dim(x, at, size, axis=1)

    def by_part(mine, theirs, axis):
        return jnp.where(
            even, jnp.concatenate([mine, theirs], axis), jnp.concatenate([theirs, mine], axis)
        )

    def by_core(mine, theirs, axis):
        return jnp.where(
            core == 0, jnp.concatenate([mine, theirs], axis), jnp.concatenate([theirs, mine], axis)
        )

    attn_mine = jnp.concatenate(
        [columns(attn_weight[0], core * half, half), columns(attn_weight[0], width + core * half, half)],
        axis=1,
    )
    up_mine = columns(up_weight[0], core * width, width)
    down_mine = lax.dynamic_slice_in_dim(down_weight[0], core * width, width, axis=0)
    shift_mine = lax.dynamic_slice_in_dim(up_bias[0], core * width, width, axis=0).astype(F32)
    small = jnp.concatenate([shift_mine, down_bias[0].astype(F32), norm_gain[0]])
    hidden_other, cotangent_other, lengths_other = swap_core(
        (hidden_in[0], cotangent[0], doc_lengths[0])
    )
    small_theirs = swap_section(small)
    attn_theirs = swap_section(attn_mine)
    up_theirs = swap_section(up_mine)
    down_theirs = swap_section(down_mine)

    stream_0 = jnp.where(lead, hidden_in[0], hidden_other).reshape(total, width)
    upstream_0 = jnp.where(lead, cotangent[0], cotangent_other).reshape(total, width)
    lengths = jnp.where(lead, doc_lengths[0], lengths_other)
    cosine, sine = rotation_tables(lengths, rows)
    qk = jnp.where(even, attn_mine, attn_theirs)
    ve = jnp.where(even, attn_theirs, attn_mine)
    shift = jnp.concatenate([shift_mine, small_theirs[:width]])[None]
    down_shift = by_part(small[width : width + half], small_theirs[width : width + half], 0)[None]
    gain_mine, gain_theirs = small[width + half :][None], small_theirs[width + half :][None]
    gain_attn = jnp.where(even, gain_mine, gain_theirs)
    gain_feed = jnp.where(even, gain_theirs, gain_mine)

    wide = (total, width)
    narrow = (total, half)
    matmul = 2.0 * total * width * width

    def attend(stream, keep):
        outs = [(wide, F32)]
        if keep:
            outs += [(wide, BF16)]
        outs += [(narrow, BF16)] * 4
        if keep:
            outs += [((blocks, 2 * rows, rows), F32)]
        return call(
            lambda *refs: attend_kernel(micro, docs, keep, *refs),
            (stream, gain_attn, lengths, qk, ve, cosine, sine),
            outs,
            2 * matmul,
            name="attend",
        )

    def feed(stream, own, other, keep):
        outs = [(wide, F32), (wide, BF16)]
        if keep:
            outs += [(wide, BF16)]
        outs += [(wide, BF16)] * 2
        if keep:
            outs += [((total, 2 * width), BF16)]
        return call(
            lambda *refs: feed_kernel(keep, *refs),
            (stream, own, other, gain_feed, up_mine, up_theirs, down_mine, down_theirs, shift),
            outs,
            4 * matmul,
            name="feed",
        )

    def finish(stream, own, other):
        return (stream.astype(F32) + ((own + other) + down_shift)).astype(BF16)

    def forward(stream, keep):
        attended = attend(stream, keep)
        fed = feed(stream, attended[0], swap_core(attended[0]), keep)
        result = finish(fed[1], fed[0], swap_core(fed[0]))
        return result, attended[1:], fed[1:]

    stream_2, _, _ = forward(stream_0, False)
    arrived = to_layer(columns(stream_2, core * half, half), 2)
    arrived = by_core(arrived, swap_core(arrived), 1)
    stream = jnp.where(first, stream_0, arrived)
    last, attended, fed = forward(stream, True)
    normed_attn, q, k, v, mixed, chance = attended
    middle, normed_feed, active_mine, active_theirs, slope = fed

    pay = jnp.concatenate(
        [
            columns(normed_attn, core * half, half),
            columns(normed_feed, core * half, half),
            active_theirs,
        ],
        axis=1,
    )
    pay = swap_section(pay)
    across = swap_core(jnp.concatenate([pay, active_mine], axis=1))
    far_attn = by_core(pay[:, :half], across[:, :half], 1)
    far_feed = by_core(pay[:, half:width], across[:, half:width], 1)
    far_active = by_core(pay[:, width:], across[:, width : 2 * width], 1)
    near_active = by_core(active_mine, across[:, 2 * width :], 1)

    outputs = jnp.where(even, middle, last)
    outputs = jnp.where(lead, outputs, swap_lead(jnp.where(even, last, middle)))

    def feed_back(upstream):
        return call(
            feed_back_kernel,
            (upstream, slope, up_mine, up_theirs, down_mine, down_theirs),
            [(wide, F32), (wide, BF16), (wide, BF16), ((8, width), F32)],
            4 * matmul,
            name="feed_back",
        )

    def attend_back(upstream, own, other, keep):
        outs = [(wide, F32), (wide, BF16), ((8, width), F32)]
        if keep:
            outs += [(wide, BF16), (wide, BF16)]

        def kernel(*refs):
            count = 15 + (5 if keep else 3)
            given, scratch = refs[:count], refs[count:]
            if not keep:
                given = given + (None, None)
            attend_back_kernel(micro, *given, *scratch)

        return call(
            kernel,
            (middle, gain_feed, upstream, own, other, qk, ve, q, k, v, mixed, chance, cosine, sine, flag),
            outs,
            2 * matmul,
            scratch=[pltpu.VMEM(narrow, BF16)] * 4,
            name="attend_back",
        )

    def norm_back(upstream, own, other):
        return call(
            norm_back_kernel,
            (stream, gain_attn, upstream, own, other),
            [(wide, BF16), ((8, width), F32)],
            0,
            name="norm_back",
        )

    def backward(upstream, keep):
        back = feed_back(upstream)
        attended = attend_back(upstream, back[0], swap_core(back[0]), keep)
        result = norm_back(attended[1], attended[0], swap_core(attended[0]))
        return result, attended[1:], back[1:]

    (grad_2, _), _, _ = backward(upstream_0, False)
    arrived = to_layer(columns(grad_2, core * half, half), -2)
    upstream_half = jnp.where(first, arrived, columns(upstream_0, core * half, half))
    upstream = by_core(upstream_half, swap_core(upstream_half), 1)
    far_upstream = swap_section(upstream_half)

    def weight(args, shape, name):
        return call(pair_kernel, args, [(shape, BF16)], 2 * matmul, name=name)[0]

    down_grad = weight(
        (near_active, upstream_half, far_active, far_upstream), (hidden, half), "down_weight"
    )
    down_sum = replica_sum(down_grad.reshape(chips, hidden // chips, half), z, chips)

    (grad_0, gain_attn_grad), attended, back = backward(upstream, True)
    grad_1, gain_feed_grad, rhs, pay = attended
    back_mine, back_theirs, sums = back
    far_back = swap_section(back_theirs)
    up_grad = weight((normed_feed, back_mine, far_feed, far_back), (width, width), "up_weight")
    up_sum = replica_sum(up_grad.reshape(chips, width // chips, width), z, chips)

    far_grad = swap_section(columns(grad_1, core * half, half))
    far_grad = by_core(far_grad, swap_core(far_grad), 1)
    far_rhs = swap_section(pay)
    attn_grad = call(
        attend_weight_kernel,
        (
            normed_attn,
            far_attn,
            rhs,
            far_rhs,
            jnp.where(even, normed_attn, grad_1),
            jnp.where(even, far_attn, far_grad),
        ),
        [((width, width), BF16)],
        2 * matmul,
        name="attend_weight",
    )[0]

    down_shift_halves = sums[2].reshape(2, half)
    mine = jnp.where(even, down_shift_halves[0], down_shift_halves[1])
    theirs = jnp.where(even, down_shift_halves[1], down_shift_halves[0])
    gain_near = jnp.where(even, gain_attn_grad[0], gain_feed_grad[0])
    gain_far = jnp.where(even, gain_feed_grad[0], gain_attn_grad[0])
    small = swap_section(jnp.concatenate([sums[1], theirs, gain_far]))
    up_part = sums[0] + small[:width]
    zero = jnp.zeros_like(up_part)
    up_part = by_core(up_part, zero, 0)
    vector = jnp.concatenate(
        [
            up_part.reshape(chips, -1),
            (mine + small[width : width + half]).reshape(chips, -1),
            (gain_near + small[width + half :]).reshape(chips, -1),
        ],
        axis=1,
    )
    span = vector.shape[1]
    vector = jnp.pad(vector, ((0, 0), (0, width - span)))[:, None].astype(BF16)
    vector = jnp.pad(vector, ((0, 0), (0, 15), (0, 0)))
    attn_parts = jnp.concatenate([attn_grad.reshape(chips, width // chips, width), vector], axis=1)
    attn_sum = replica_sum(attn_parts, z, chips)
    vector = attn_sum[width // chips]
    attn_sum = attn_sum[: width // chips]

    def shares(x):
        size = x.shape[0] // 2
        kept = lax.dynamic_slice_in_dim(x, core * size, size, axis=0)
        given = lax.dynamic_slice_in_dim(x, (1 - core) * size, size, axis=0)
        return kept, given

    kept, given = zip(*[shares(x) for x in (attn_sum, up_sum, down_sum)])
    others = swap_core(tuple(given) + (vector,))
    attn_out = jnp.concatenate(
        [by_core(kept[0][:, :half], others[0][:, :half], 1), by_core(kept[0][:, half:], others[0][:, half:], 1)],
        axis=1,
    )
    up_out = by_core(kept[1], others[1], 1)
    down_out = by_core(kept[2], others[2], 1)

    def own_share(x):
        size = x.shape[0] // 2
        return lax.dynamic_slice_in_dim(x, core * size, size, axis=0)

    cut_a = hidden // chips
    cut_b = cut_a + half // chips
    cut_c = cut_b + width // chips
    up_shift_out = own_share(vector[:cut_a] + others[3][:cut_a])
    down_shift_out = own_share(vector[cut_a:cut_b])
    gain_out = own_share(vector[cut_b:cut_c])

    grads = jnp.where(even, grad_0, grad_1)
    grads = jnp.where(lead, grads, swap_lead(jnp.where(even, grad_1, grad_0)))
    shape = (1, 1, micro, rows, width)
    return (
        outputs.reshape(shape),
        grads.reshape(shape),
        attn_out[None],
        up_out[None],
        down_out[None],
        up_shift_out[None],
        down_shift_out[None],
        gain_out[None],
    )


def solution(mesh):
    in_specs = (
        P("dp", None, None, None),
        P("dp", None, None, None),
        P("dp", None, None),
        P("section", None, None),
        P("section", None, None),
        P("section", None, None),
        P("section", None),
        P("section", None),
        P("section", None),
    )
    out_specs = (
        P("section", "dp", None, None, None),
        P("section", "dp", None, None, None),
        P("section", "dp", None),
        P("section", "dp", None),
        P("section", "dp", None),
        P("section", "dp"),
        P("section", "dp"),
        P("section", "dp"),
    )
    return jax.shard_map(body, mesh=mesh, in_specs=in_specs, out_specs=out_specs, check_vma=False)
```

```python
import jax
import jax.numpy as jnp
from jax import lax
from jax.experimental import pallas as pl
from jax.experimental.pallas import tpu as pltpu
from jax.sharding import PartitionSpec as P

HEAD = 64
BLOCK = 16
EPSILON = 1e-05
MASKED = -1e30
LANES = 128
LINE = 4
EXTRA = 16
F32 = jnp.float32
BF16 = jnp.bfloat16
PART, NEAR, CORE, LEAD, FIRST, HIGH = range(6)


def dot(left, right):
    return lax.dot_general(left, right, (((1,), (0,)), ((), ())), preferred_element_type=F32)


def dot_cols(left, right):
    return lax.dot_general(left, right, (((1,), (1,)), ((), ())), preferred_element_type=F32)


def dot_rows(left, right):
    return lax.dot_general(left, right, (((0,), (0,)), ((), ())), preferred_element_type=F32)


def normalized(values):
    mean = jnp.mean(values, axis=-1, keepdims=True)
    centered = values - mean
    spread = jnp.mean(centered * centered, axis=-1, keepdims=True)
    rstd = lax.rsqrt(spread + EPSILON)
    return centered * rstd, rstd


def norm_backward(values, gain, upstream, grad_normed):
    xhat, rstd = normalized(values)
    scaled = grad_normed * gain
    mean = jnp.mean(scaled, axis=-1, keepdims=True)
    along = jnp.mean(scaled * xhat, axis=-1, keepdims=True)
    grad_gain = jnp.sum(grad_normed * xhat, axis=0, keepdims=True)
    grad = upstream.astype(F32) + rstd * (scaled - mean - xhat * along)
    return grad.astype(BF16), grad_gain


def joined(own, other):
    return jnp.concatenate([a[...].astype(F32) + b[...].astype(F32) for a, b in zip(own, other)], axis=0)


def scatter(value, pieces):
    rows = pieces[0].shape[0]
    for index, piece in enumerate(pieces):
        piece[...] = value[index * rows : (index + 1) * rows].astype(BF16)


def lanes_of(spot, half):
    return pl.ds(pl.multiple_of(spot[CORE] * half, LANES), half)


def swap_halves(block):
    lane = lax.broadcasted_iota(jnp.int32, block.shape, 1)
    low = lax.rem(lane, HEAD) < HEAD // 2
    ahead = pltpu.roll(block, LANES - HEAD // 2, 1)
    behind = pltpu.roll(block, HEAD // 2, 1)
    return jnp.where(low, ahead, behind)


def stacked(pair):
    lane = lax.broadcasted_iota(jnp.int32, pair.shape, 1)
    zero = jnp.zeros_like(pair)
    return jnp.concatenate(
        [jnp.where(lane < HEAD, pair, zero), jnp.where(lane < HEAD, zero, pair)], axis=0
    )


def merged(stack, rows):
    lane = lax.broadcasted_iota(jnp.int32, (rows, LANES), 1)
    return jnp.where(lane < HEAD, stack[:rows], stack[rows:])


def visible(table, at, rows, total):
    low = table[at : at + rows, 2 * LANES : 2 * LANES + 1]
    high = table[at : at + rows, 2 * LANES + 1 : 2 * LANES + 2]
    same = table[at : at + rows, 2 * LANES + 2 : 2 * LANES + 3]
    clean = table[total : total + 1, at : at + rows]
    noisy = table[total + 1 : total + 2, at : at + rows]
    return ((clean >= low) & (clean <= high)) | (noisy == same)


VECTOR = pl.BlockSpec(memory_space=pltpu.VMEM)
SCALAR = pl.BlockSpec(memory_space=pltpu.SMEM)
ANYWHERE = pl.BlockSpec(memory_space=pl.ANY)


def call(kernel, args, outs, scratch=(), name=None):
    return pl.pallas_call(
        kernel,
        out_shape=[jax.ShapeDtypeStruct(shape, dtype) for shape, dtype in outs],
        in_specs=[SCALAR if x.dtype == jnp.int32 else VECTOR for x in args],
        out_specs=[VECTOR] * len(outs),
        scratch_shapes=list(scratch),
        compiler_params=pltpu.CompilerParams(vmem_limit_bytes=8 * 1024 * 1024),
        name=name,
    )(*args)


GAIN_ATTN, GAIN_FEED, DOWN_SHIFT, SHIFT = range(4)


def cut_kernel(places, spot, *refs):
    count = len(places)
    arrays, outs, sems = refs[: -count - 1], refs[-count - 1 : -1], refs[-1]
    copies = []
    for index, (number, place) in enumerate(places):
        row, column = place(spot)
        rows, columns = outs[index].shape
        lines = pl.ds(pl.multiple_of(row, 16), rows)
        lanes = pl.ds(pl.multiple_of(column, LANES), columns)
        copies.append(
            pltpu.make_async_copy(arrays[number].at[0, lines, lanes], outs[index], sems.at[index])
        )
    for copy in copies:
        copy.start()
    for copy in copies:
        copy.wait()


def cut(spot, arrays, places, shapes, name):
    return pl.pallas_call(
        lambda *refs: cut_kernel(places, *refs),
        out_shape=[jax.ShapeDtypeStruct(shape, BF16) for shape in shapes],
        in_specs=[SCALAR] + [ANYWHERE] * len(arrays),
        out_specs=[VECTOR] * len(shapes),
        scratch_shapes=[pltpu.SemaphoreType.DMA((len(shapes),))],
        name=name,
    )(spot, *arrays)


def attend_kernel(micro, keep, arrived, *refs):
    if arrived:
        mine, theirs, before, *refs = refs
    else:
        mine, theirs, *refs = refs
    params, spot, table, *refs = refs
    held, refs = refs[:4], refs[4:]
    partial, stream, refs = refs[:micro], refs[micro], refs[micro + 1 :]
    if keep:
        normed_out, q, k, v, mixed, chance = refs
    else:
        q, k, v, mixed = refs
    total, width = stream.shape
    half = width // 2
    rows = total // micro
    if arrived:
        low = jnp.where(spot[CORE] == 0, mine[...], theirs[...])
        high = jnp.where(spot[CORE] == 0, theirs[...], mine[...])
        x = jnp.where(spot[FIRST] == 1, before[...], jnp.concatenate([low, high], axis=1))
    else:
        x = jnp.where(spot[LEAD] == 1, mine[...], theirs[...])
    stream[...] = x
    xhat, _ = normalized(x.astype(F32))
    normed = (xhat * params[GAIN_ATTN : GAIN_ATTN + 1, :width]).astype(BF16)
    if keep:
        normed_out[...] = normed
    v[...] = dot(normed, held[2][...]).astype(BF16)
    cos, sin = table[:total, :LANES], table[:total, LANES : 2 * LANES]
    for index, target in ((0, q), (1, k)):
        wide = dot(normed, held[index][...])
        for at in range(0, half, LANES):
            block = wide[:, at : at + LANES]
            target[:, at : at + LANES] = (block * cos + swap_halves(block) * sin).astype(BF16)
    for item in range(micro):
        place = pl.ds(item * rows, rows)
        mask = visible(table, item * rows, rows, total)
        mask = jnp.concatenate([mask, mask], axis=0)
        for pair in range(half // LANES):
            lanes = pl.ds(pair * LANES, LANES)
            scores = dot_cols(stacked(q[place, lanes]), k[place, lanes]) * HEAD ** (-0.5)
            scores = jnp.where(mask, scores, MASKED)
            peak = jnp.max(scores, axis=-1, keepdims=True)
            powers = jnp.exp(scores - peak)
            weights = powers / jnp.sum(powers, axis=-1, keepdims=True)
            if keep:
                chance[item * (half // LANES) + pair] = weights
            mixed[place, lanes] = merged(dot(weights.astype(BF16), v[place, lanes]), rows).astype(BF16)
    scatter(dot_cols(mixed[...], held[3][...]), partial)


def feed_up(x, own, other, params, held, stream, normed_out, active, slope):
    width = x.shape[1]
    result = (x[...].astype(F32) + joined(own, other)).astype(BF16)
    stream[...] = result
    xhat, _ = normalized(result.astype(F32))
    normed = (xhat * params[GAIN_FEED : GAIN_FEED + 1, :width]).astype(BF16)
    if normed_out is not None:
        normed_out[...] = normed
    scale = (2.0 / jnp.pi) ** 0.5
    piece = 2 * LANES
    for index in (0, 1):
        for at in range(0, width, piece):
            wide = pl.ds(index * width + at, piece)
            before = dot(normed, held[index][:, at : at + piece]) + params[SHIFT : SHIFT + 1, wide]
            square = before * before
            bend = jnp.tanh(scale * before * (1.0 + 0.044715 * square))
            active[index][:, at : at + piece] = (0.5 * before * (1.0 + bend)).astype(BF16)
            if slope is not None:
                inner = scale * (1.0 + 3 * 0.044715 * square)
                tilt = 0.5 * (1.0 + bend) + 0.5 * before * (1.0 - bend * bend) * inner
                slope[:, wide] = tilt.astype(BF16)


def feed_up_kernel(micro, x, *refs):
    own, other, refs = refs[:micro], refs[micro : 2 * micro], refs[2 * micro :]
    params, up_mine, up_theirs, stream, mine, theirs = refs
    feed_up(x, own, other, params, (up_mine, up_theirs), stream, None, (mine, theirs), None)


def feed_down_kernel(mine, theirs, down_mine, down_theirs, *partial):
    scatter(dot(mine[...], down_mine[...]) + dot(theirs[...], down_theirs[...]), partial)


def feed_kernel(micro, x, *refs):
    own, other, refs = refs[:micro], refs[micro : 2 * micro], refs[2 * micro :]
    params, spot, up_mine, up_theirs, down_mine, down_theirs, normed_attn, mixed, *refs = refs
    partial, refs = refs[:micro], refs[micro:]
    stream, normed, mine, slope, pay, theirs = refs
    width = x.shape[1]
    half = width // 2
    feed_up(x, own, other, params, (up_mine, up_theirs), stream, normed, (mine, theirs), slope)
    scatter(dot(mine[...], down_mine[...]) + dot(theirs[...], down_theirs[...]), partial)
    lanes = lanes_of(spot, half)
    pay[:, :half] = normed_attn[:, lanes]
    pay[:, half:width] = mixed[...]
    pay[:, width : width + half] = normed[:, lanes]
    pay[:, width + half :] = theirs[...]


def finish_kernel(micro, stream, *refs):
    own, other, refs = refs[:micro], refs[micro : 2 * micro], refs[2 * micro :]
    params, spot, part, result = refs
    width = stream.shape[1]
    shift = params[DOWN_SHIFT : DOWN_SHIFT + 1, :width]
    result[...] = (stream[...].astype(F32) + (joined(own, other) + shift)).astype(BF16)
    part[...] = result[:, lanes_of(spot, part.shape[1])]


def last_kernel(micro, stream, *refs):
    own, other, refs = refs[:micro], refs[micro : 2 * micro], refs[2 * micro :]
    params, spot, mine, theirs = refs
    width = stream.shape[1]
    shift = params[DOWN_SHIFT : DOWN_SHIFT + 1, :width]
    middle = stream[...]
    result = (middle.astype(F32) + (joined(own, other) + shift)).astype(BF16)
    mine[...] = jnp.where(spot[PART] == 0, middle, result)
    theirs[...] = jnp.where(spot[PART] == 0, result, middle)


def feed_back_kernel(micro, arrived, *refs):
    if arrived:
        half_mine, half_theirs, before, *refs = refs
    else:
        whole_mine, whole_theirs, *refs = refs
    slope, spot, up_mine, up_theirs, down_mine, down_theirs, *refs = refs
    partial, upstream, refs = refs[:micro], refs[micro], refs[micro + 1 :]
    if arrived:
        mine, theirs, sums = refs
    else:
        mine, theirs = refs
    rows, width = upstream.shape
    if arrived:
        low = jnp.where(spot[CORE] == 0, half_mine[...], half_theirs[...])
        high = jnp.where(spot[CORE] == 0, half_theirs[...], half_mine[...])
        dz = jnp.where(spot[FIRST] == 1, jnp.concatenate([low, high], axis=1), before[...])
        sums[2:3, :] = jnp.sum(dz.astype(F32), axis=0, keepdims=True)
        sums[3:, :] = jnp.zeros((sums.shape[0] - 3, width), F32)
    else:
        dz = jnp.where(spot[LEAD] == 1, whole_mine[...], whole_theirs[...])
    upstream[...] = dz
    piece = 2 * LANES
    for index, (down, back) in enumerate(((down_mine, mine), (down_theirs, theirs))):
        for at in range(0, width, piece):
            grad = dot_cols(dz, down[at : at + piece, :])
            grad = grad * slope[:, index * width + at : index * width + at + piece].astype(F32)
            rounded = grad.astype(BF16)
            back[:, at : at + piece] = rounded
            if arrived:
                sums[index : index + 1, at : at + piece] = jnp.sum(
                    rounded.astype(F32), axis=0, keepdims=True
                )
    scatter(dot_cols(mine[...], up_mine[...]) + dot_cols(theirs[...], up_theirs[...]), partial)


def attend_back_kernel(micro, keep, dz, *refs):
    own, other, refs = refs[:micro], refs[micro : 2 * micro], refs[2 * micro :]
    x, params, chance, v, k, q, mixed, table, spot, *refs = refs
    held, refs = refs[:4], refs[4:]
    partial, refs = refs[:micro], refs[micro:]
    grad, *refs = refs
    if keep:
        grad_gain, rhs_a, rhs_b, pay_a, pay_b, *refs = refs
    dq, dk, dv, dmixed = refs
    total, width = x.shape
    half = width // 2
    rows = total // micro
    gain = params[GAIN_FEED : GAIN_FEED + 1, :width]
    result, gain_sum = norm_backward(x[...].astype(F32), gain, dz[...], joined(own, other))
    grad[...] = result
    if keep:
        grad_gain[...] = jnp.broadcast_to(gain_sum, grad_gain.shape)
    dmixed[...] = dot(result, held[3][...]).astype(BF16)
    for item in range(micro):
        place = pl.ds(item * rows, rows)
        turn = table[item * rows : (item + 1) * rows, :LANES]
        tilt = table[item * rows : (item + 1) * rows, LANES : 2 * LANES]
        for pair in range(half // LANES):
            lanes = pl.ds(pair * LANES, LANES)
            weights = chance[item * (half // LANES) + pair]
            grads = stacked(dmixed[place, lanes])
            queries = stacked(q[place, lanes])
            dv[place, lanes] = dot_rows(weights.astype(BF16), grads).astype(BF16)
            spread = dot_cols(grads, v[place, lanes])
            inner = jnp.sum(weights * spread, axis=-1, keepdims=True)
            scores = (weights * (spread - inner)).astype(BF16)
            query_grad = merged(dot(scores, k[place, lanes]), rows) * HEAD ** (-0.5)
            key_grad = dot_rows(scores, queries) * HEAD ** (-0.5)
            dq[place, lanes] = (query_grad * turn - swap_halves(query_grad) * tilt).astype(BF16)
            dk[place, lanes] = (key_grad * turn - swap_halves(key_grad) * tilt).astype(BF16)
    if keep:
        even = spot[PART] == 0
        rhs_a[...] = jnp.where(even, dq[...], dv[...])
        rhs_b[...] = jnp.where(even, dk[...], mixed[...])
        pay_a[...] = jnp.where(even, dv[...], dq[...])
        pay_b[...] = jnp.where(even, grad[:, lanes_of(spot, half)], dk[...])
    scatter(
        dot_cols(dq[...], held[0][...]) + dot_cols(dk[...], held[1][...]) + dot_cols(dv[...], held[2][...]),
        partial,
    )


def norm_back_kernel(micro, dz, *refs):
    own, other, refs = refs[:micro], refs[micro : 2 * micro], refs[2 * micro :]
    x, params, spot, grad, part = refs
    gain = params[GAIN_ATTN : GAIN_ATTN + 1, : x.shape[1]]
    result, _ = norm_backward(x[...].astype(F32), gain, dz[...], joined(own, other))
    grad[...] = result
    part[...] = grad[:, lanes_of(spot, part.shape[1])]


def norm_end_kernel(micro, dz, *refs):
    own, other, refs = refs[:micro], refs[micro : 2 * micro], refs[2 * micro :]
    x, params, sums, gain_feed, spot, mine, theirs, kept, given = refs
    width = x.shape[1]
    half = width // 2
    gain = params[GAIN_ATTN : GAIN_ATTN + 1, :width]
    upstream = dz[...]
    result, gain_sum = norm_backward(x[...].astype(F32), gain, upstream, joined(own, other))
    even = spot[PART] == 0
    mine[...] = jnp.where(even, result, upstream)
    theirs[...] = jnp.where(even, upstream, result)
    far_gain = gain_feed[0:1]
    low, high = sums[2:3, :half], sums[2:3, half:]
    zero = jnp.zeros((1, half), F32)
    for out, row, take_low, gains in (
        (kept, 0, even, jnp.where(even, gain_sum, far_gain)),
        (given, 1, jnp.logical_not(even), jnp.where(even, far_gain, gain_sum)),
    ):
        out[0:1, :] = sums[row : row + 1, :]
        out[1:2, :] = jnp.concatenate([jnp.where(take_low, low, high), zero], axis=1)
        out[2:3, :] = gains
        out[3:, :] = jnp.zeros((out.shape[0] - 3, width), F32)


def halves(spot, size):
    return [(pl.ds(pl.multiple_of(at * size, LANES), size), at) for at in (spot[CORE], 1 - spot[CORE])]


def deal(grad, half, spot, kept, given):
    pairs, size = kept.shape[0], kept.shape[1]
    for i in range(pairs // 2):
        low = grad[2 * i * size : (2 * i + 1) * size]
        high = grad[(2 * i + 1) * size : (2 * i + 2) * size]
        place = half * (pairs // 2) + i
        kept[place] = jnp.where(spot[NEAR] == 0, low, high).astype(BF16)
        given[place] = jnp.where(spot[NEAR] == 0, high, low).astype(BF16)


def down_weight_kernel(near, near_other, far, far_other, dz, far_dz, spot, kept, given):
    width = near.shape[1]
    at = far.shape[1] - width
    lefts = ((near, far), (near_other, far_other))
    for (left, far_left), (_, half) in zip(lefts, halves(spot, width)):
        grad = dot_rows(left[...], dz[...]) + dot_rows(far_left[:, at:], far_dz[...])
        deal(grad, half, spot, kept, given)


def up_weight_kernel(near, far, far_other, back, far_back, spot, kept, given):
    size = near.shape[1] // 2
    for left, (lines, half) in zip((far, far_other), halves(spot, size)):
        far_left = left[:, 2 * size : 3 * size]
        grad = dot_rows(near[:, lines], back[...]) + dot_rows(far_left, far_back[...])
        deal(grad, half, spot, kept, given)


def attend_weight_a_kernel(near, far, far_other, right, far_right, mine, theirs, spot, kept, given):
    size = near.shape[1] // 2
    kept, given, kept_vector, given_vector = [
        x.at[:, at] for at in (pl.ds(0, kept.shape[1] - EXTRA), pl.ds(kept.shape[1] - EXTRA, EXTRA)) for x in (kept, given)
    ]
    for left, (lines, half) in zip((far, far_other), halves(spot, size)):
        grad = dot_rows(near[:, lines], right[...]) + dot_rows(left[:, :size], far_right[...])
        deal(grad, half, spot, kept, given)
    total = mine[...] + theirs[...]
    chips = 2 * kept.shape[0]
    parts = []
    for chip in range(chips):
        rows = []
        held = [spot[CORE] == i for i in (0, 1)]
        each = 2 * total.shape[1] // chips
        first = chip * each % total.shape[1]
        units = jnp.where(held[chip * each // total.shape[1]], total[0:1, first : first + each], 0.0)
        rows = [units]
        for row, all_of in ((1, size), (2, 2 * size)):
            each = all_of // chips
            rows.append(total[row : row + 1, chip * each : (chip + 1) * each])
        rows = [jnp.pad(x, ((0, 0), (0, size - x.shape[1]))) for x in rows]
        parts.append(jnp.concatenate(rows + [jnp.zeros((EXTRA - 3, size), F32)], axis=0))
    for i in range(chips // 2):
        low, high = parts[2 * i], parts[2 * i + 1]
        kept_vector[i] = jnp.where(spot[NEAR] == 0, low, high).astype(BF16)
        given_vector[i] = jnp.where(spot[NEAR] == 0, high, low).astype(BF16)


def attend_weight_b_kernel(
    near, grad_in, far, far_other, right, far_right, far_right_other, spot, kept, given
):
    size = near.shape[1] // 2
    even = spot[PART] == 0
    rights = jnp.where(even, far_right[...], far[:, size : 2 * size])
    lefts = ((far, far_right), (far_other, far_right_other))
    for (left, back), (lines, half) in zip(lefts, halves(spot, size)):
        grad = dot_rows(jnp.where(even, near[:, lines], grad_in[:, lines]), right[...])
        grad += dot_rows(jnp.where(even, left[:, :size], back[...]), rights)
        deal(grad, half, spot, kept, given)


def fold_kernel(kept, received, spot, out, given):
    low = kept[0].astype(F32) + received[0].astype(F32)
    high = kept[1].astype(F32) + received[1].astype(F32)
    out[0] = jnp.where(spot[HIGH] == 0, low, high)
    given[0] = jnp.where(spot[HIGH] == 0, high, low).astype(BF16)


def close_kernel(extra, kept, received, spot, out, given):
    size = out.shape[0] - extra
    total = kept[0] + received[0].astype(F32)
    low, high = total[:size], total[size : 2 * size]
    out[:size] = jnp.where(spot[CORE] == 0, low, high)
    given[:size] = jnp.where(spot[CORE] == 0, high, low)
    if extra:
        out[size:] = total[2 * size :]
        given[size:] = total[2 * size :]


def swap_section(x):
    return lax.ppermute(x, "section", [(i, i ^ 1) for i in range(lax.axis_size("section"))])


def swap_layer(x):
    return lax.ppermute(x, "section", [(i, i ^ 2) for i in range(lax.axis_size("section"))])


def swap_core(x):
    return lax.ppermute(x, "dp", [(i, i ^ 1) for i in range(lax.axis_size("dp"))])


def swap_chip(x, distance):
    return lax.ppermute(x, "dp", [(i, i ^ (2 * distance)) for i in range(lax.axis_size("dp"))])


def after(x, *others):
    return lax.optimization_barrier((x,) + others)[0]


def replica_sum(kept, given, z, chips):
    if chips > LINE:
        pair = jnp.where(z % 2 == 0, jnp.stack([kept, given], 1), jnp.stack([given, kept], 1))
        groups = [[2 * i + c for i in range(chips)] for c in (0, 1)]
        return lax.psum_scatter(
            pair.reshape(chips, *kept.shape[1:]),
            "dp",
            scatter_dimension=0,
            axis_index_groups=groups,
            tiled=False,
        ).astype(F32)
    distance = 1
    while True:
        total = kept.astype(F32) + swap_chip(given, distance).astype(F32)
        if total.shape[0] == 1:
            return total[0]
        distance *= 2
        bit = z // distance % 2
        pairs = total.reshape(total.shape[0] // 2, 2, *total.shape[1:])
        given = lax.dynamic_index_in_dim(pairs, 1 - bit, 1, keepdims=False).astype(given.dtype)
        kept = lax.dynamic_index_in_dim(pairs, bit, 1, keepdims=False)


def rotation_and_mask(lengths, rows):
    half = rows // 2
    place = jnp.arange(rows, dtype=jnp.int32)
    clean = (place >= half)[None]
    within = jnp.where(place >= half, place - half, place)
    ends = jnp.cumsum(lengths, axis=1)
    passed = (within[None, :, None] >= ends[:, None, :]).astype(jnp.int32)
    document = jnp.sum(passed, axis=2)
    offset = within[None] - jnp.sum(passed * lengths[:, None, :], axis=2)
    count = HEAD // 2
    freq = jnp.power(10000.0, -2.0 * jnp.arange(count, dtype=F32) / HEAD)
    angle = offset.reshape(-1).astype(F32)[:, None] * freq[None, :]
    cosine, sine = jnp.cos(angle), jnp.sin(angle)
    span = half // BLOCK + 1
    block = document * span + offset // BLOCK
    low = document * span
    high = jnp.where(clean, block, block - 1)
    same = jnp.where(clean, -1, block)
    total = offset.size
    codes = jnp.stack([x.reshape(-1) for x in (low, high, same)], axis=1).astype(F32)
    codes = jnp.pad(codes, ((0, 0), (0, LANES - 3)))
    keys = jnp.stack([jnp.where(clean, block, -2).reshape(-1), jnp.where(clean, -2, block).reshape(-1)])
    keys = jnp.pad(keys.astype(F32), ((0, 6), (0, max(0, 3 * LANES - total))))
    table = jnp.concatenate(
        [cosine] * (LANES // count) + [-sine, sine] * (LANES // HEAD) + [codes], axis=1
    )
    table = jnp.pad(table, ((0, 0), (0, keys.shape[1] - table.shape[1])))
    return jnp.concatenate([table, keys], axis=0)


def body(
    hidden_in,
    cotangent,
    doc_lengths,
    attn_weight,
    up_weight,
    down_weight,
    up_bias,
    down_bias,
    norm_gain,
):
    section = lax.axis_index("section")
    replica = lax.axis_index("dp")
    chips = lax.axis_size("dp") // 2
    part, layer = section % 2, section // 2
    core, z = replica % 2, replica // 2
    near = z % 2
    even, lead, first = part == 0, core == part, layer == 0
    micro, rows, width = hidden_in.shape[1:]
    total, half = micro * rows, width // 2
    hidden = up_weight.shape[2]
    blocks = micro * (half // LANES)
    spot = jnp.stack(
        [part, near, core, lead.astype(jnp.int32), first.astype(jnp.int32), z // 2 % 2]
    ).astype(jnp.int32)

    def columns(x, at, size):
        return lax.dynamic_slice_in_dim(x, at, size, axis=1)

    def by_part(mine, theirs, axis):
        return jnp.where(
            even, jnp.concatenate([mine, theirs], axis), jnp.concatenate([theirs, mine], axis)
        )

    def by_core(mine, theirs, axis):
        return jnp.where(
            core == 0, jnp.concatenate([mine, theirs], axis), jnp.concatenate([theirs, mine], axis)
        )

    wide, narrow = ((total, width), BF16), ((total, half), BF16)
    pieces = [((rows, width), BF16)] * micro
    vectors = ((8, width), F32)

    shift_mine = lax.dynamic_slice_in_dim(up_bias[0], core * width, width, axis=0).astype(F32)
    small = jnp.concatenate([shift_mine, down_bias[0].astype(F32), norm_gain[0]])
    def given(at, array, place, shape, name):
        return cut(at, (array,), [(0, place)], [shape], name)[0]

    attn_given = given(
        spot,
        attn_weight,
        lambda spot: (0, spot[NEAR] * width + spot[CORE] * half),
        (width, half),
        "cut_attn",
    )
    up_given = given(
        after(spot, attn_given),
        up_weight,
        lambda spot: (spot[NEAR] * half, spot[CORE] * width),
        (half, width),
        "cut_up",
    )
    attn_near, up_near = swap_section(attn_given), swap_section(up_given)
    down_given = given(
        after(spot, attn_near),
        down_weight,
        lambda spot: (spot[CORE] * width + spot[NEAR] * half, 0),
        (half, width),
        "cut_down",
    )
    down_near = swap_section(down_given)
    attn_next, up_next = swap_chip(attn_near, 1), swap_chip(up_near, 1)
    attn_own = cut(
        after(spot, up_given),
        (attn_weight,),
        [(0, lambda spot, i=i: (0, i * width + spot[CORE] * half)) for i in (0, 1)],
        [(width, half)] * 2,
        "cut_own",
    )
    hidden_in, cotangent, doc_lengths, small = lax.optimization_barrier(
        (hidden_in, cotangent, doc_lengths, small, up_given)
    )[:4]
    hidden_in, cotangent = hidden_in.reshape(wide[0]), cotangent.reshape(wide[0])
    hidden_other, lengths_other = swap_core((hidden_in, doc_lengths[0]))
    small_theirs = swap_section(small)
    table = rotation_and_mask(jnp.where(lead, doc_lengths[0], lengths_other), rows)
    down_shift = by_part(small[width : width + half], small_theirs[width : width + half], 0)
    gains = [jnp.pad(x[width + half :], (0, width)) for x in (small, small_theirs)]
    params = jnp.stack(
        [
            jnp.where(even, gains[0], gains[1]),
            jnp.where(even, gains[1], gains[0]),
            jnp.pad(down_shift, (0, width)),
            jnp.concatenate([shift_mine, small_theirs[:width]]),
        ]
    )
    params = jnp.pad(params, ((0, 4), (0, 0)))

    def ordered(mine, theirs):
        low, high = jnp.where(near == 0, mine, theirs), jnp.where(near == 0, theirs, mine)
        return jnp.concatenate([low, high], axis=0)

    low, high = jnp.where(near == 0, attn_near, attn_next), jnp.where(near == 0, attn_next, attn_near)
    attn = (
        jnp.where(even, attn_own[0], low),
        jnp.where(even, attn_own[1], high),
        jnp.where(even, low, attn_own[0]),
        jnp.where(even, high, attn_own[1]),
    )

    def attend(streams, keep):
        arrived = len(streams) == 3
        outs, scratch = pieces + [wide], [pltpu.VMEM(*narrow)] * 4
        if keep:
            outs, scratch = outs + [wide] + [narrow] * 4 + [((blocks, 2 * rows, rows), F32)], ()
        out = call(
            lambda *refs: attend_kernel(micro, keep, arrived, *refs),
            (*streams, params, spot, table, *attn),
            outs,
            scratch,
            "attend",
        )
        return out[:micro], out[micro:]

    own_part, (stream_0,) = attend((hidden_in, hidden_other), False)
    down_next = swap_chip(after(down_near, own_part[0]), 1)
    feed_own = cut(
        after(spot, own_part[0]),
        (up_weight, down_weight),
        [(0, lambda spot: (0, spot[CORE] * width)), (1, lambda spot: (spot[CORE] * width, 0))],
        [(width, width)] * 2,
        "cut_feed",
    )
    ups = (feed_own[0], ordered(up_near, up_next))
    downs = (feed_own[1], ordered(down_near, down_next))
    middle, *active = call(
        lambda *refs: feed_up_kernel(micro, *refs),
        (stream_0, *own_part, *swap_core(own_part), params, *ups),
        [wide] * 3,
        name="feed_up",
    )
    own_part = call(feed_down_kernel, (*active, *downs), pieces, name="feed_down")
    arrived = call(
        lambda *refs: finish_kernel(micro, *refs),
        (middle, *own_part, *swap_core(own_part), params, spot),
        [narrow],
        [pltpu.VMEM(*wide)],
        "finish",
    )[0]
    arrived = swap_layer(arrived)
    own_part, kept = attend((arrived, swap_core(arrived), stream_0), True)
    stream, normed_attn, q, k, v, mixed, chance = kept
    out = call(
        lambda *refs: feed_kernel(micro, *refs),
        (stream, *own_part, *swap_core(own_part), params, spot, *ups, *downs, normed_attn, mixed),
        pieces + [wide] * 3 + [((total, 2 * width), BF16), ((total, 2 * width + half), BF16)],
        [pltpu.VMEM(*wide)],
        "feed",
    )
    fed, (middle, normed_feed, active_mine, slope, pay) = out[:micro], out[micro:]
    far = swap_section(pay)

    def feed_back(upstreams):
        arrived = len(upstreams) == 3
        outs, scratch = pieces + [wide], [pltpu.VMEM(*wide)] * 2
        if arrived:
            outs, scratch = outs + [wide, wide, vectors], ()
        out = call(
            lambda *refs: feed_back_kernel(micro, arrived, *refs),
            (*upstreams, slope, spot, *ups, *downs),
            outs,
            scratch,
            "feed_back",
        )
        return out[:micro], out[micro:]

    def attend_back(upstream, own, other, params, keep):
        outs = pieces + [wide]
        if keep:
            outs += [vectors] + [narrow] * 4
        out = call(
            lambda *refs: attend_back_kernel(micro, keep, *refs),
            (upstream, *own, *other, middle, params, chance, v, k, q, mixed, table, spot, *attn),
            outs,
            [pltpu.VMEM(*narrow)] * 4,
            "attend_back",
        )
        return out[:micro], out[micro:]

    cotangent_other = swap_core(after(cotangent, arrived))
    own_part, (upstream_0,) = feed_back((cotangent, cotangent_other))
    own_part, (grad,) = attend_back(upstream_0, own_part, swap_core(own_part), params, False)
    grad_2, arrived = call(
        lambda *refs: norm_back_kernel(micro, *refs),
        (grad, *own_part, *swap_core(own_part), stream, params, spot),
        [wide, narrow],
        name="norm_back",
    )
    arrived = swap_layer(arrived)
    upstream_half = jnp.where(first, arrived, columns(upstream_0, core * half, half))
    far_upstream = swap_section(upstream_half)
    active_other = swap_core(after(active_mine, grad_2))

    def weight(kernel, args, shape, name, extra=0):
        outs = [((chips // 2, shape[0] // chips + extra, shape[1]), BF16)] * 2
        return call(kernel, (*args, spot), outs, name=name)

    def folded(grad, *others):
        kept, given = grad
        if chips != LINE:
            return replica_sum(kept, given, z, chips)
        received = after(swap_chip(given, 1), *others)
        part = (1, *kept.shape[1:])
        return call(fold_kernel, (kept, received, spot), [(part, F32), (part, BF16)], name="fold")

    def closed(fold, *others, extra=0):
        if chips != LINE:
            size = (fold.shape[0] - extra) // 2
            mine = lax.dynamic_slice_in_dim(fold, core * size, size, axis=0)
            theirs = lax.dynamic_slice_in_dim(fold, (1 - core) * size, size, axis=0)
            mine, theirs = [jnp.concatenate([x, fold[2 * size :]], axis=0) for x in (mine, theirs)]
            return mine, swap_core(theirs)
        kept, given = fold
        received = after(swap_chip(given, 2), *others)
        part = (((kept.shape[1] + extra) // 2, kept.shape[2]), F32)
        mine, theirs = call(
            lambda *refs: close_kernel(extra, *refs), (kept, received, spot), [part] * 2, name="close"
        )
        return mine, swap_core(theirs)

    def first_of(x):
        return x if chips != LINE else x[0]

    outputs, outputs_given = call(
        lambda *refs: last_kernel(micro, *refs),
        (middle, *fed, *swap_core([after(x, grad_2) for x in fed]), params, spot),
        [wide, wide],
        name="last",
    )
    own_part, back = feed_back(
        (upstream_half, swap_core(upstream_half), after(upstream_0, outputs_given))
    )
    upstream, back_mine, back_theirs, sums = back
    far = after(far, upstream)
    far_other = swap_core(far)
    far_back = swap_section(back_theirs)
    *own_part, far_upstream = lax.optimization_barrier((*own_part, far_upstream))
    down_grad = weight(
        down_weight_kernel,
        (active_mine, active_other, far, far_other, upstream_half, far_upstream),
        (hidden, half),
        "down_weight",
    )
    own_part, back = attend_back(
        upstream, own_part, swap_core(own_part), after(params, down_grad[0]), True
    )
    grad_1, gain_feed_grad, rhs_a, rhs_b, pay_a, pay_b = back
    far_rhs_a, far_rhs_b = swap_section(pay_a), swap_section(pay_b)
    grads, grads_given, vector, vector_given = call(
        lambda *refs: norm_end_kernel(micro, *refs),
        (
            grad_1,
            *own_part,
            *swap_core(own_part),
            stream,
            params,
            sums,
            gain_feed_grad,
            spot,
        ),
        [wide, wide, vectors, vectors],
        name="norm_end",
    )
    vector_theirs = swap_section(vector_given)
    up_grad = weight(
        up_weight_kernel,
        (normed_feed, far, far_other, back_mine, after(far_back, grads)),
        (width, width),
        "up_weight",
    )
    down_fold = folded(down_grad, up_grad[0])
    attn_grad_a = weight(
        attend_weight_a_kernel,
        (
            normed_attn,
            far,
            far_other,
            rhs_a,
            after(far_rhs_a, first_of(down_fold)),
            vector,
            vector_theirs,
        ),
        (width, half),
        "attend_weight_a",
        EXTRA,
    )
    far_rhs_b = after(far_rhs_b, attn_grad_a[0])
    attn_grad_b = weight(
        attend_weight_b_kernel,
        (normed_attn, grad_1, far, far_other, rhs_b, far_rhs_b, swap_core(far_rhs_b)),
        (width, half),
        "attend_weight_b",
    )
    up_fold = folded(up_grad, attn_grad_b[0])
    attn_fold_a = folded(attn_grad_a, first_of(up_fold))
    down_sum = closed(down_fold, first_of(attn_fold_a))
    attn_fold_b = folded(attn_grad_b, down_sum[0])
    up_sum = closed(up_fold, first_of(attn_fold_b))
    attn_sum_a = closed(attn_fold_a, up_sum[0], extra=EXTRA)
    attn_sum_b = closed(attn_fold_b, attn_sum_a[0])
    vector, vector_other = [x[width // chips // 2 :] for x in attn_sum_a]
    attn_sum_a = [x[: width // chips // 2] for x in attn_sum_a]

    def own_share(x, total):
        size = total // (2 * chips)
        return lax.dynamic_slice_in_dim(x, core * size, size, axis=0)

    up_shift_out = own_share(vector[0] + vector_other[0], hidden)
    down_shift_out = own_share(vector[1], half)
    gain_out = own_share(vector[2], width)

    attn_out = jnp.concatenate([by_core(*attn_sum_a, 1), by_core(*attn_sum_b, 1)], axis=1)
    up_out, down_out = by_core(*up_sum, 1), by_core(*down_sum, 1)

    outputs = jnp.where(lead, outputs, swap_section(outputs_given))
    grads = jnp.where(lead, grads, swap_section(grads_given))
    shape = (1, 1, micro, rows, width)
    return (
        outputs.reshape(shape),
        grads.reshape(shape),
        attn_out[None],
        up_out[None],
        down_out[None],
        up_shift_out[None],
        down_shift_out[None],
        gain_out[None],
    )


def solution(mesh):
    in_specs = (
        P("dp", None, None, None),
        P("dp", None, None, None),
        P("dp", None, None),
        P("section", None, None),
        P("section", None, None),
        P("section", None, None),
        P("section", None),
        P("section", None),
        P("section", None),
    )
    out_specs = (
        P("section", "dp", None, None, None),
        P("section", "dp", None, None, None),
        P("section", "dp", None),
        P("section", "dp", None),
        P("section", "dp", None),
        P("section", "dp"),
        P("section", "dp"),
        P("section", "dp"),
    )
    return jax.shard_map(body, mesh=mesh, in_specs=in_specs, out_specs=out_specs, check_vma=False)
```

```python
import jax
import jax.numpy as jnp
from jax import lax
from jax.experimental import pallas as pl
from jax.experimental.pallas import tpu as pltpu
from jax.sharding import PartitionSpec as P

HEAD = 64
BLOCK = 16
EPSILON = 1e-05
MASKED = -1e30
LANES = 128
LINE = 4
EXTRA = 16
F32 = jnp.float32
BF16 = jnp.bfloat16
PART, NEAR, CORE, LEAD, FIRST, HIGH = range(6)


def dot(left, right):
    return lax.dot_general(left, right, (((1,), (0,)), ((), ())), preferred_element_type=F32)


def dot_cols(left, right):
    return lax.dot_general(left, right, (((1,), (1,)), ((), ())), preferred_element_type=F32)


def dot_rows(left, right):
    return lax.dot_general(left, right, (((0,), (0,)), ((), ())), preferred_element_type=F32)


def normalized(values):
    mean = jnp.mean(values, axis=-1, keepdims=True)
    centered = values - mean
    spread = jnp.mean(centered * centered, axis=-1, keepdims=True)
    rstd = lax.rsqrt(spread + EPSILON)
    return centered * rstd, rstd


def norm_backward(values, gain, upstream, grad_normed):
    xhat, rstd = normalized(values)
    scaled = grad_normed * gain
    mean = jnp.mean(scaled, axis=-1, keepdims=True)
    along = jnp.mean(scaled * xhat, axis=-1, keepdims=True)
    grad_gain = jnp.sum(grad_normed * xhat, axis=0, keepdims=True)
    grad = upstream.astype(F32) + rstd * (scaled - mean - xhat * along)
    return grad.astype(BF16), grad_gain


def joined(own, other):
    return jnp.concatenate([a[...].astype(F32) + b[...].astype(F32) for a, b in zip(own, other)], axis=0)


def where():
    section, replica = lax.axis_index("section"), lax.axis_index("dp")
    part, core, z = section % 2, replica % 2, replica // 2
    lead = (part == core).astype(jnp.int32)
    first = (section < 2).astype(jnp.int32)
    return part, z % 2, core, lead, first, z // 2 % 2


def scatter(value, pieces):
    rows = pieces[0].shape[0]
    for index, piece in enumerate(pieces):
        piece[...] = value[index * rows : (index + 1) * rows].astype(BF16)


def lanes_of(spot, half):
    return pl.ds(pl.multiple_of(spot[CORE] * half, LANES), half)


def swap_halves(block):
    lane = lax.broadcasted_iota(jnp.int32, block.shape, 1)
    low = lax.rem(lane, HEAD) < HEAD // 2
    ahead = pltpu.roll(block, LANES - HEAD // 2, 1)
    behind = pltpu.roll(block, HEAD // 2, 1)
    return jnp.where(low, ahead, behind)


def stacked(pair):
    lane = lax.broadcasted_iota(jnp.int32, pair.shape, 1)
    zero = jnp.zeros_like(pair)
    return jnp.concatenate(
        [jnp.where(lane < HEAD, pair, zero), jnp.where(lane < HEAD, zero, pair)], axis=0
    )


def merged(stack, rows):
    lane = lax.broadcasted_iota(jnp.int32, (rows, LANES), 1)
    return jnp.where(lane < HEAD, stack[:rows], stack[rows:])


def visible(table, at, rows, total):
    low = table[at : at + rows, 2 * LANES : 2 * LANES + 1]
    high = table[at : at + rows, 2 * LANES + 1 : 2 * LANES + 2]
    same = table[at : at + rows, 2 * LANES + 2 : 2 * LANES + 3]
    clean = table[total : total + 1, at : at + rows]
    noisy = table[total + 1 : total + 2, at : at + rows]
    return ((clean >= low) & (clean <= high)) | (noisy == same)


VECTOR = pl.BlockSpec(memory_space=pltpu.VMEM)
ANYWHERE = pl.BlockSpec(memory_space=pl.ANY)


def call(kernel, args, outs, scratch=(), name=None):
    return pl.pallas_call(
        kernel,
        out_shape=[jax.ShapeDtypeStruct(shape, dtype) for shape, dtype in outs],
        in_specs=[VECTOR] * len(args),
        out_specs=[VECTOR] * len(outs),
        scratch_shapes=list(scratch),
        compiler_params=pltpu.CompilerParams(vmem_limit_bytes=8 * 1024 * 1024),
        name=name,
    )(*args)


GAIN_ATTN, GAIN_FEED, DOWN_SHIFT, SHIFT = range(4)


def cut_kernel(places, *refs):
    spot = where()
    count = len(places)
    refs = refs[1:]
    arrays, outs, sems = refs[: -count - 1], refs[-count - 1 : -1], refs[-1]
    copies = []
    for index, (number, place) in enumerate(places):
        row, column = place(spot)
        rows, columns = outs[index].shape
        lines = pl.ds(pl.multiple_of(row, 16), rows)
        lanes = pl.ds(pl.multiple_of(column, LANES), columns)
        copies.append(
            pltpu.make_async_copy(arrays[number].at[0, lines, lanes], outs[index], sems.at[index])
        )
    for copy in copies:
        copy.start()
    for copy in copies:
        copy.wait()


def cut(before, arrays, places, shapes, name):
    before = arrays[0] if before is None else before
    return pl.pallas_call(
        lambda *refs: cut_kernel(places, *refs),
        out_shape=[jax.ShapeDtypeStruct(shape, BF16) for shape in shapes],
        in_specs=[ANYWHERE] * (1 + len(arrays)),
        out_specs=[VECTOR] * len(shapes),
        scratch_shapes=[pltpu.SemaphoreType.DMA((len(shapes),))],
        name=name,
    )(before, *arrays)


def attend_kernel(micro, keep, arrived, *refs):
    if arrived:
        mine, theirs, before, *refs = refs
    else:
        mine, theirs, *refs = refs
    params, table, *refs = refs
    spot = where()
    held, refs = refs[:4], refs[4:]
    partial, stream, refs = refs[:micro], refs[micro], refs[micro + 1 :]
    if keep:
        normed_out, q, k, v, mixed, chance = refs
    else:
        q, k, v, mixed = refs
    total, width = stream.shape
    half = width // 2
    rows = total // micro
    if arrived:
        low = jnp.where(spot[CORE] == 0, mine[...], theirs[...])
        high = jnp.where(spot[CORE] == 0, theirs[...], mine[...])
        x = jnp.where(spot[FIRST] == 1, before[...], jnp.concatenate([low, high], axis=1))
    else:
        x = jnp.where(spot[LEAD] == 1, mine[...], theirs[...])
    stream[...] = x
    xhat, _ = normalized(x.astype(F32))
    normed = (xhat * params[GAIN_ATTN : GAIN_ATTN + 1, :width]).astype(BF16)
    if keep:
        normed_out[...] = normed
    v[...] = dot(normed, held[2][...]).astype(BF16)
    cos, sin = table[:total, :LANES], table[:total, LANES : 2 * LANES]
    for index, target in ((0, q), (1, k)):
        wide = dot(normed, held[index][...])
        for at in range(0, half, LANES):
            block = wide[:, at : at + LANES]
            target[:, at : at + LANES] = (block * cos + swap_halves(block) * sin).astype(BF16)
    for item in range(micro):
        place = pl.ds(item * rows, rows)
        mask = visible(table, item * rows, rows, total)
        mask = jnp.concatenate([mask, mask], axis=0)
        for pair in range(half // LANES):
            lanes = pl.ds(pair * LANES, LANES)
            scores = dot_cols(stacked(q[place, lanes]), k[place, lanes]) * HEAD ** (-0.5)
            scores = jnp.where(mask, scores, MASKED)
            peak = jnp.max(scores, axis=-1, keepdims=True)
            powers = jnp.exp(scores - peak)
            weights = powers / jnp.sum(powers, axis=-1, keepdims=True)
            if keep:
                chance[item * (half // LANES) + pair] = weights
            mixed[place, lanes] = merged(dot(weights.astype(BF16), v[place, lanes]), rows).astype(BF16)
    scatter(dot_cols(mixed[...], held[3][...]), partial)


def feed_up(x, own, other, params, held, stream, normed_out, active, slope):
    width = x.shape[1]
    result = (x[...].astype(F32) + joined(own, other)).astype(BF16)
    stream[...] = result
    xhat, _ = normalized(result.astype(F32))
    normed = (xhat * params[GAIN_FEED : GAIN_FEED + 1, :width]).astype(BF16)
    if normed_out is not None:
        normed_out[...] = normed
    scale = (2.0 / jnp.pi) ** 0.5
    piece = 2 * LANES
    for index in (0, 1):
        for at in range(0, width, piece):
            wide = pl.ds(index * width + at, piece)
            before = dot(normed, held[index][:, at : at + piece]) + params[SHIFT : SHIFT + 1, wide]
            square = before * before
            bend = jnp.tanh(scale * before * (1.0 + 0.044715 * square))
            active[index][:, at : at + piece] = (0.5 * before * (1.0 + bend)).astype(BF16)
            if slope is not None:
                inner = scale * (1.0 + 3 * 0.044715 * square)
                tilt = 0.5 * (1.0 + bend) + 0.5 * before * (1.0 - bend * bend) * inner
                slope[:, wide] = tilt.astype(BF16)


def feed_up_kernel(micro, x, *refs):
    own, other, refs = refs[:micro], refs[micro : 2 * micro], refs[2 * micro :]
    params, up_mine, up_theirs, down_mine, stream, theirs, total, mine = refs
    feed_up(x, own, other, params, (up_mine, up_theirs), stream, None, (mine, theirs), None)
    total[...] = dot(mine[...], down_mine[...])


def feed_down_kernel(total, theirs, near, following, *partial):
    spot = where()
    half = near.shape[0]
    first = pl.ds(pl.multiple_of(spot[NEAR] * half, LANES), half)
    second = pl.ds(pl.multiple_of((1 - spot[NEAR]) * half, LANES), half)
    result = total[...] + dot(theirs[:, first], near[...]) + dot(theirs[:, second], following[...])
    scatter(result, partial)


def feed_kernel(micro, x, *refs):
    own, other, refs = refs[:micro], refs[micro : 2 * micro], refs[2 * micro :]
    params, up_mine, up_theirs, down_mine, down_theirs, normed_attn, mixed, *refs = refs
    spot = where()
    partial, refs = refs[:micro], refs[micro:]
    stream, normed, mine, slope, pay, pay_attn, theirs = refs
    width = x.shape[1]
    half = width // 2
    feed_up(x, own, other, params, (up_mine, up_theirs), stream, normed, (mine, theirs), slope)
    scatter(dot(mine[...], down_mine[...]) + dot(theirs[...], down_theirs[...]), partial)
    lanes = lanes_of(spot, half)
    pay[:, :half] = normed[:, lanes]
    pay[:, half:] = theirs[...]
    pay_attn[:, :half] = normed_attn[:, lanes]
    pay_attn[:, half:] = mixed[...]


def finish_kernel(micro, stream, *refs):
    own, other, refs = refs[:micro], refs[micro : 2 * micro], refs[2 * micro :]
    params, part, result = refs
    spot = where()
    width = stream.shape[1]
    shift = params[DOWN_SHIFT : DOWN_SHIFT + 1, :width]
    result[...] = (stream[...].astype(F32) + (joined(own, other) + shift)).astype(BF16)
    part[...] = result[:, lanes_of(spot, part.shape[1])]


def last_kernel(micro, stream, *refs):
    own, other, refs = refs[:micro], refs[micro : 2 * micro], refs[2 * micro :]
    params, mine, theirs = refs
    spot = where()
    width = stream.shape[1]
    shift = params[DOWN_SHIFT : DOWN_SHIFT + 1, :width]
    middle = stream[...]
    result = (middle.astype(F32) + (joined(own, other) + shift)).astype(BF16)
    mine[...] = jnp.where(spot[PART] == 0, middle, result)
    theirs[...] = jnp.where(spot[PART] == 0, result, middle)


def feed_back_kernel(micro, arrived, *refs):
    if arrived:
        half_mine, half_theirs, before, *refs = refs
    else:
        whole_mine, whole_theirs, *refs = refs
    slope, up_mine, up_theirs, down_mine, down_theirs, *refs = refs
    spot = where()
    partial, upstream, refs = refs[:micro], refs[micro], refs[micro + 1 :]
    if arrived:
        mine, theirs, sums = refs
    else:
        mine, theirs = refs
    rows, width = upstream.shape
    if arrived:
        low = jnp.where(spot[CORE] == 0, half_mine[...], half_theirs[...])
        high = jnp.where(spot[CORE] == 0, half_theirs[...], half_mine[...])
        dz = jnp.where(spot[FIRST] == 1, jnp.concatenate([low, high], axis=1), before[...])
        sums[2:3, :] = jnp.sum(dz.astype(F32), axis=0, keepdims=True)
        sums[3:, :] = jnp.zeros((sums.shape[0] - 3, width), F32)
    else:
        dz = jnp.where(spot[LEAD] == 1, whole_mine[...], whole_theirs[...])
    upstream[...] = dz
    piece = 2 * LANES
    for index, (down, back) in enumerate(((down_mine, mine), (down_theirs, theirs))):
        for at in range(0, width, piece):
            grad = dot_cols(dz, down[at : at + piece, :])
            grad = grad * slope[:, index * width + at : index * width + at + piece].astype(F32)
            rounded = grad.astype(BF16)
            back[:, at : at + piece] = rounded
            if arrived:
                sums[index : index + 1, at : at + piece] = jnp.sum(
                    rounded.astype(F32), axis=0, keepdims=True
                )
    scatter(dot_cols(mine[...], up_mine[...]) + dot_cols(theirs[...], up_theirs[...]), partial)


def attend_back_kernel(micro, keep, dz, *refs):
    own, other, refs = refs[:micro], refs[micro : 2 * micro], refs[2 * micro :]
    x, params, chance, v, k, q, mixed, table, *refs = refs
    spot = where()
    held, refs = refs[:4], refs[4:]
    given = micro + 2 if keep else micro
    partial, refs = refs[:given], refs[given:]
    grad, *refs = refs
    if keep:
        vector, rhs_a, rhs_b, pay_a, pay_b, *refs = refs
        stream, sums, *partial = partial
    dq, dk, dv, dmixed = refs
    total, width = x.shape
    half = width // 2
    rows = total // micro
    gain = params[GAIN_FEED : GAIN_FEED + 1, :width]
    result, gain_sum = norm_backward(x[...].astype(F32), gain, dz[...], joined(own, other))
    grad[...] = result
    dmixed[...] = dot(result, held[3][...]).astype(BF16)
    for item in range(micro):
        place = pl.ds(item * rows, rows)
        turn = table[item * rows : (item + 1) * rows, :LANES]
        tilt = table[item * rows : (item + 1) * rows, LANES : 2 * LANES]
        for pair in range(half // LANES):
            lanes = pl.ds(pair * LANES, LANES)
            weights = chance[item * (half // LANES) + pair]
            grads = stacked(dmixed[place, lanes])
            queries = stacked(q[place, lanes])
            dv[place, lanes] = dot_rows(weights.astype(BF16), grads).astype(BF16)
            spread = dot_cols(grads, v[place, lanes])
            inner = jnp.sum(weights * spread, axis=-1, keepdims=True)
            scores = (weights * (spread - inner)).astype(BF16)
            query_grad = merged(dot(scores, k[place, lanes]), rows) * HEAD ** (-0.5)
            key_grad = dot_rows(scores, queries) * HEAD ** (-0.5)
            dq[place, lanes] = (query_grad * turn - swap_halves(query_grad) * tilt).astype(BF16)
            dk[place, lanes] = (key_grad * turn - swap_halves(key_grad) * tilt).astype(BF16)
    if keep:
        even = spot[PART] == 0
        rhs_a[...] = jnp.where(even, dq[...], dv[...])
        rhs_b[...] = jnp.where(even, dk[...], mixed[...])
        pay_a[...] = jnp.where(even, dv[...], dq[...])
        pay_b[:total] = jnp.where(even, grad[:, lanes_of(spot, half)], dk[...])
    back = dot_cols(dq[...], held[0][...]) + dot_cols(dk[...], held[1][...])
    back += dot_cols(dv[...], held[2][...])
    scatter(back, partial)
    if keep:
        xhat, _ = normalized(stream[...].astype(F32))
        attn_gain = jnp.sum(back * xhat, axis=0, keepdims=True)
        zero = jnp.zeros((1, half), F32)
        alone = spot[CORE] == 0
        feed_gain = jnp.where(alone, gain_sum, 0.0)
        low = jnp.where(alone, sums[2:3, :half], zero)
        high = jnp.where(alone, sums[2:3, half:], zero)
        mine = (sums[0:1, :], jnp.where(even, low, high), jnp.where(even, attn_gain, feed_gain))
        theirs = (sums[1:2, :], jnp.where(even, high, low), jnp.where(even, feed_gain, attn_gain))
        vector[...] = rows_of(mine, half)
        wide = rows_of(theirs, half)
        above = wide.astype(BF16)
        pay_b[total : total + EXTRA] = above
        pay_b[total + EXTRA :] = (wide - above.astype(F32)).astype(BF16)


def rows_of(vectors, half):
    units, features, gain = vectors
    rows = [units[:, :half], units[:, half:], features, gain[:, :half], gain[:, half:]]
    return jnp.concatenate(rows + [jnp.zeros((EXTRA - len(rows), half), F32)], axis=0)


def norm_back_kernel(micro, dz, *refs):
    own, other, refs = refs[:micro], refs[micro : 2 * micro], refs[2 * micro :]
    x, params, grad, part = refs
    spot = where()
    gain = params[GAIN_ATTN : GAIN_ATTN + 1, : x.shape[1]]
    result, _ = norm_backward(x[...].astype(F32), gain, dz[...], joined(own, other))
    grad[...] = result
    part[...] = grad[:, lanes_of(spot, part.shape[1])]


def norm_end_kernel(micro, dz, *refs):
    own, other, refs = refs[:micro], refs[micro : 2 * micro], refs[2 * micro :]
    x, params, mine, theirs = refs
    spot = where()
    gain = params[GAIN_ATTN : GAIN_ATTN + 1, : x.shape[1]]
    upstream = dz[...]
    result, _ = norm_backward(x[...].astype(F32), gain, upstream, joined(own, other))
    even = spot[PART] == 0
    mine[...] = jnp.where(even, result, upstream)
    theirs[...] = jnp.where(even, upstream, result)


def halves(spot, size):
    return [(pl.ds(pl.multiple_of(at * size, LANES), size), at) for at in (spot[CORE], 1 - spot[CORE])]


def deal(grad, half, spot, kept, given):
    pairs, size = kept.shape[0], kept.shape[1]
    for i in range(pairs // 2):
        low = grad[2 * i * size : (2 * i + 1) * size]
        high = grad[(2 * i + 1) * size : (2 * i + 2) * size]
        place = half * (pairs // 2) + i
        kept[place] = jnp.where(spot[NEAR] == 0, low, high).astype(BF16)
        given[place] = jnp.where(spot[NEAR] == 0, high, low).astype(BF16)


def down_weight_kernel(near, near_other, far, far_other, dz, far_dz, kept, given):
    spot = where()
    width = near.shape[1]
    at = far.shape[1] - width
    lefts = ((near, far), (near_other, far_other))
    for (left, far_left), (_, half) in zip(lefts, halves(spot, width)):
        grad = dot_rows(left[...], dz[...]) + dot_rows(far_left[:, at:], far_dz[...])
        deal(grad, half, spot, kept, given)


def up_weight_kernel(near, far, far_other, back, far_back, kept, given):
    spot = where()
    size = near.shape[1] // 2
    for left, (lines, half) in zip((far, far_other), halves(spot, size)):
        grad = dot_rows(near[:, lines], back[...]) + dot_rows(left[:, :size], far_back[...])
        deal(grad, half, spot, kept, given)


def attend_weight_a_kernel(near, far, far_other, right, far_right, kept, given):
    spot = where()
    size = near.shape[1] // 2
    for left, (lines, half) in zip((far, far_other), halves(spot, size)):
        grad = dot_rows(near[:, lines], right[...]) + dot_rows(left[:, :size], far_right[...])
        deal(grad, half, spot, kept, given)


def attend_weight_b_kernel(
    near, grad_in, far, far_other, right, far_right, far_right_other, vector, kept, given
):
    spot = where()
    size = near.shape[1] // 2
    rows = near.shape[0]
    below = kept.shape[1] - EXTRA
    even = spot[PART] == 0
    rights = jnp.where(even, far_right[:rows], far[:, size:])
    lefts = ((far, far_right), (far_other, far_right_other))
    for (left, back), (lines, half) in zip(lefts, halves(spot, size)):
        grad = dot_rows(jnp.where(even, near[:, lines], grad_in[:, lines]), right[...])
        grad += dot_rows(jnp.where(even, left[:, :size], back[:rows]), rights)
        deal(grad, half, spot, kept.at[:, :below], given.at[:, :below])
    total = vector[...] + far_right[rows : rows + EXTRA].astype(F32) + far_right[rows + EXTRA :].astype(F32)
    chips = 2 * kept.shape[0]
    spans = ((0, 4 * size), (2, size), (3, 2 * size))
    parts = []
    for chip in range(chips):
        lines = []
        for row, extent in spans:
            each = extent // chips
            at = chip * each
            if row == 0:
                mine = spot[CORE] == at // (2 * size)
                at %= 2 * size
            piece = total[row + at // size : row + at // size + 1, at % size : at % size + each]
            piece = jnp.where(mine, piece, 0.0) if row == 0 else piece
            lines.append(jnp.pad(piece, ((0, 0), (0, size - each))))
        parts.append(jnp.concatenate(lines + [jnp.zeros((EXTRA - len(lines), size), F32)], axis=0))
    for i in range(chips // 2):
        low, high = parts[2 * i], parts[2 * i + 1]
        kept[i, below:] = jnp.where(spot[NEAR] == 0, low, high).astype(BF16)
        given[i, below:] = jnp.where(spot[NEAR] == 0, high, low).astype(BF16)


def fold_kernel(kept, received, out, given):
    spot = where()
    low = kept[0].astype(F32) + received[0].astype(F32)
    high = kept[1].astype(F32) + received[1].astype(F32)
    out[0] = jnp.where(spot[HIGH] == 0, low, high)
    given[0] = jnp.where(spot[HIGH] == 0, high, low).astype(BF16)


def close_kernel(extra, kept, received, out, given):
    spot = where()
    size = out.shape[0] - extra
    total = kept[0] + received[0].astype(F32)
    low, high = total[:size], total[size : 2 * size]
    out[:size] = jnp.where(spot[CORE] == 0, low, high)
    given[:size] = jnp.where(spot[CORE] == 0, high, low)
    if extra:
        out[size:] = total[2 * size :]
        given[size:] = total[2 * size :]


def swap_section(x):
    return lax.ppermute(x, "section", [(i, i ^ 1) for i in range(lax.axis_size("section"))])


def swap_layer(x):
    return lax.ppermute(x, "section", [(i, i ^ 2) for i in range(lax.axis_size("section"))])


def swap_core(x):
    return lax.ppermute(x, "dp", [(i, i ^ 1) for i in range(lax.axis_size("dp"))])


def swap_chip(x, distance):
    return lax.ppermute(x, "dp", [(i, i ^ (2 * distance)) for i in range(lax.axis_size("dp"))])


def after(x, *others):
    return lax.optimization_barrier((x,) + others)[0]


def replica_sum(kept, given, z, chips):
    if chips > LINE:
        pair = jnp.where(z % 2 == 0, jnp.stack([kept, given], 1), jnp.stack([given, kept], 1))
        groups = [[2 * i + c for i in range(chips)] for c in (0, 1)]
        return lax.psum_scatter(
            pair.reshape(chips, *kept.shape[1:]),
            "dp",
            scatter_dimension=0,
            axis_index_groups=groups,
            tiled=False,
        ).astype(F32)
    distance = 1
    while True:
        total = kept.astype(F32) + swap_chip(given, distance).astype(F32)
        if total.shape[0] == 1:
            return total[0]
        distance *= 2
        bit = z // distance % 2
        pairs = total.reshape(total.shape[0] // 2, 2, *total.shape[1:])
        given = lax.dynamic_index_in_dim(pairs, 1 - bit, 1, keepdims=False).astype(given.dtype)
        kept = lax.dynamic_index_in_dim(pairs, bit, 1, keepdims=False)


def rotation_and_mask(lengths, rows):
    half = rows // 2
    place = jnp.arange(rows, dtype=jnp.int32)
    clean = (place >= half)[None]
    within = jnp.where(place >= half, place - half, place)
    ends = jnp.cumsum(lengths, axis=1)
    passed = (within[None, :, None] >= ends[:, None, :]).astype(jnp.int32)
    document = jnp.sum(passed, axis=2)
    offset = within[None] - jnp.sum(passed * lengths[:, None, :], axis=2)
    count = HEAD // 2
    freq = jnp.power(10000.0, -2.0 * jnp.arange(count, dtype=F32) / HEAD)
    angle = offset.reshape(-1).astype(F32)[:, None] * freq[None, :]
    cosine, sine = jnp.cos(angle), jnp.sin(angle)
    span = half // BLOCK + 1
    block = document * span + offset // BLOCK
    low = document * span
    high = jnp.where(clean, block, block - 1)
    same = jnp.where(clean, -1, block)
    total = offset.size
    codes = jnp.stack([x.reshape(-1) for x in (low, high, same)], axis=1).astype(F32)
    codes = jnp.pad(codes, ((0, 0), (0, LANES - 3)))
    keys = jnp.stack([jnp.where(clean, block, -2).reshape(-1), jnp.where(clean, -2, block).reshape(-1)])
    keys = jnp.pad(keys.astype(F32), ((0, 6), (0, max(0, 3 * LANES - total))))
    table = jnp.concatenate(
        [cosine] * (LANES // count) + [-sine, sine] * (LANES // HEAD) + [codes], axis=1
    )
    table = jnp.pad(table, ((0, 0), (0, keys.shape[1] - table.shape[1])))
    return jnp.concatenate([table, keys], axis=0)


def body(
    hidden_in,
    cotangent,
    doc_lengths,
    attn_weight,
    up_weight,
    down_weight,
    up_bias,
    down_bias,
    norm_gain,
):
    section = lax.axis_index("section")
    replica = lax.axis_index("dp")
    chips = lax.axis_size("dp") // 2
    part, layer = section % 2, section // 2
    core, z = replica % 2, replica // 2
    near = z % 2
    even, lead, first = part == 0, core == part, layer == 0
    micro, rows, width = hidden_in.shape[1:]
    total, half = micro * rows, width // 2
    hidden = up_weight.shape[2]
    blocks = micro * (half // LANES)

    def columns(x, at, size):
        return lax.dynamic_slice_in_dim(x, at, size, axis=1)

    def by_part(mine, theirs, axis):
        return jnp.where(
            even, jnp.concatenate([mine, theirs], axis), jnp.concatenate([theirs, mine], axis)
        )

    def by_core(mine, theirs, axis):
        return jnp.where(
            core == 0, jnp.concatenate([mine, theirs], axis), jnp.concatenate([theirs, mine], axis)
        )

    wide, narrow = ((total, width), BF16), ((total, half), BF16)
    pieces = [((rows, width), BF16)] * micro
    vectors = ((8, width), F32)

    shift_mine = lax.dynamic_slice_in_dim(up_bias[0], core * width, width, axis=0).astype(F32)
    small = jnp.concatenate([shift_mine, down_bias[0].astype(F32), norm_gain[0]])
    def given(at, array, place, shape, name):
        return cut(at, (array,), [(0, place)], [shape], name)[0]

    attn_given = given(
        None,
        attn_weight,
        lambda spot: (0, spot[NEAR] * width + spot[CORE] * half),
        (width, half),
        "cut_attn",
    )
    up_given = given(
        attn_given,
        up_weight,
        lambda spot: (spot[NEAR] * half, spot[CORE] * width),
        (half, width),
        "cut_up",
    )
    attn_near, up_near = swap_section(attn_given), swap_section(up_given)
    down_given = given(
        attn_near,
        down_weight,
        lambda spot: (spot[CORE] * width + spot[NEAR] * half, 0),
        (half, width),
        "cut_down",
    )
    down_near = swap_section(down_given)
    attn_next, up_next = swap_chip(attn_near, 1), swap_chip(up_near, 1)
    attn_own = cut(
        up_given,
        (attn_weight,),
        [(0, lambda spot, i=i: (0, i * width + spot[CORE] * half)) for i in (0, 1)],
        [(width, half)] * 2,
        "cut_own",
    )
    feed_own = cut(
        down_given,
        (up_weight, down_weight),
        [(0, lambda spot: (0, spot[CORE] * width)), (1, lambda spot: (spot[CORE] * width, 0))],
        [(width, width)] * 2,
        "cut_feed",
    )
    hidden_in, cotangent, doc_lengths, small = lax.optimization_barrier(
        (hidden_in, cotangent, doc_lengths, small, up_given)
    )[:4]
    hidden_in, cotangent = hidden_in.reshape(wide[0]), cotangent.reshape(wide[0])
    hidden_other, lengths_other = swap_core((hidden_in, doc_lengths[0]))
    small_theirs = after(swap_section(small), attn_next)
    table = rotation_and_mask(jnp.where(lead, doc_lengths[0], lengths_other), rows)
    down_shift = by_part(small[width : width + half], small_theirs[width : width + half], 0)
    gains = [jnp.pad(x[width + half :], (0, width)) for x in (small, small_theirs)]
    params = jnp.stack(
        [
            jnp.where(even, gains[0], gains[1]),
            jnp.where(even, gains[1], gains[0]),
            jnp.pad(down_shift, (0, width)),
            jnp.concatenate([shift_mine, small_theirs[:width]]),
        ]
    )
    params = jnp.pad(params, ((0, 4), (0, 0)))

    def ordered(mine, theirs):
        low, high = jnp.where(near == 0, mine, theirs), jnp.where(near == 0, theirs, mine)
        return jnp.concatenate([low, high], axis=0)

    low, high = jnp.where(near == 0, attn_near, attn_next), jnp.where(near == 0, attn_next, attn_near)
    attn = (
        jnp.where(even, attn_own[0], low),
        jnp.where(even, attn_own[1], high),
        jnp.where(even, low, attn_own[0]),
        jnp.where(even, high, attn_own[1]),
    )

    def attend(streams, keep):
        arrived = len(streams) == 3
        outs, scratch = pieces + [wide], [pltpu.VMEM(*narrow)] * 4
        if keep:
            outs, scratch = outs + [wide] + [narrow] * 4 + [((blocks, 2 * rows, rows), F32)], ()
        out = call(
            lambda *refs: attend_kernel(micro, keep, arrived, *refs),
            (*streams, params, table, *attn),
            outs,
            scratch,
            "attend",
        )
        return out[:micro], out[micro:]

    own_part, (stream_0,) = attend((hidden_in, hidden_other), False)
    down_next = swap_chip(after(down_near, own_part[0]), 1)
    ups = (feed_own[0], ordered(up_near, up_next))
    middle, *active = call(
        lambda *refs: feed_up_kernel(micro, *refs),
        (stream_0, *own_part, *swap_core(own_part), params, *ups, feed_own[1]),
        [wide] * 2 + [(wide[0], F32)],
        [pltpu.VMEM(*wide)],
        name="feed_up",
    )
    own_part = call(
        feed_down_kernel, (active[1], active[0], down_near, down_next), pieces, name="feed_down"
    )
    arrived = call(
        lambda *refs: finish_kernel(micro, *refs),
        (middle, *own_part, *swap_core(own_part), params),
        [narrow],
        [pltpu.VMEM(*wide)],
        "finish",
    )[0]
    downs = (feed_own[1], ordered(after(down_near, arrived), down_next))
    arrived = after(swap_layer(arrived), downs[1])
    own_part, kept = attend((arrived, swap_core(arrived), stream_0), True)
    stream, normed_attn, q, k, v, mixed, chance = kept
    out = call(
        lambda *refs: feed_kernel(micro, *refs),
        (stream, *own_part, *swap_core(own_part), params, *ups, *downs, normed_attn, mixed),
        pieces + [wide] * 3 + [((total, 2 * width), BF16), ((total, width + half), BF16), wide],
        [pltpu.VMEM(*wide)],
        "feed",
    )
    fed, (middle, normed_feed, active_mine, slope, pay, pay_attn) = out[:micro], out[micro:]
    far = swap_section(pay)

    def feed_back(upstreams):
        arrived = len(upstreams) == 3
        outs, scratch = pieces + [wide], [pltpu.VMEM(*wide)] * 2
        if arrived:
            outs, scratch = outs + [wide, wide, vectors], ()
        out = call(
            lambda *refs: feed_back_kernel(micro, arrived, *refs),
            (*upstreams, slope, *ups, *downs),
            outs,
            scratch,
            "feed_back",
        )
        return out[:micro], out[micro:]

    def attend_back(upstream, own, other, params, keep):
        outs = pieces + [wide]
        more = ()
        if keep:
            outs += [((EXTRA, half), F32)] + [narrow] * 3 + [((total + 2 * EXTRA, half), BF16)]
            more = keep
        out = call(
            lambda *refs: attend_back_kernel(micro, bool(keep), *refs),
            (upstream, *own, *other, middle, params, chance, v, k, q, mixed, table, *attn, *more),
            outs,
            [pltpu.VMEM(*narrow)] * 4,
            "attend_back",
        )
        return out[:micro], out[micro:]

    cotangent_other = swap_core(after(cotangent, arrived))
    own_part, (upstream_0,) = feed_back((cotangent, cotangent_other))
    own_part, (grad,) = attend_back(upstream_0, own_part, swap_core(own_part), params, ())
    grad_2, arrived = call(
        lambda *refs: norm_back_kernel(micro, *refs),
        (grad, *own_part, *swap_core(own_part), stream, params),
        [wide, narrow],
        name="norm_back",
    )
    arrived = swap_layer(arrived)
    upstream_half = jnp.where(first, arrived, columns(upstream_0, core * half, half))
    far_upstream = swap_section(upstream_half)
    upstream_other = swap_core(upstream_half)
    far_attn = swap_section(after(pay_attn, grad_2))
    far, active_mine = lax.optimization_barrier((far, active_mine, upstream_half))[:2]
    active_other, far_other = swap_core((active_mine, far))

    def weight(kernel, args, shape, name, extra=0):
        outs = [((chips // 2, shape[0] // chips + extra, shape[1]), BF16)] * 2
        return call(kernel, args, outs, name=name)

    def folded(grad, *others):
        kept, given = grad
        if chips != LINE:
            return replica_sum(kept, given, z, chips)
        received = after(swap_chip(given, 1), *others)
        part = (1, *kept.shape[1:])
        return call(fold_kernel, (kept, received), [(part, F32), (part, BF16)], name="fold")

    def closed(fold, *others, extra=0):
        if chips != LINE:
            size = (fold.shape[0] - extra) // 2
            mine = lax.dynamic_slice_in_dim(fold, core * size, size, axis=0)
            theirs = lax.dynamic_slice_in_dim(fold, (1 - core) * size, size, axis=0)
            mine, theirs = [jnp.concatenate([x, fold[2 * size :]], axis=0) for x in (mine, theirs)]
            return mine, swap_core(theirs)
        kept, given = fold
        received = after(swap_chip(given, 2), *others)
        part = (((kept.shape[1] + extra) // 2, kept.shape[2]), F32)
        mine, theirs = call(
            lambda *refs: close_kernel(extra, *refs), (kept, received), [part] * 2, name="close"
        )
        return mine, swap_core(theirs)

    def first_of(x):
        return x if chips != LINE else x[0]

    own_part, back = feed_back((upstream_half, upstream_other, upstream_0))
    upstream, back_mine, back_theirs, sums = back
    far_back = swap_section(back_theirs)
    *own_part, far_attn = lax.optimization_barrier((*own_part, far_attn))
    own_part, back = attend_back(upstream, own_part, swap_core(own_part), params, (stream, sums))
    grad_1, vector, rhs_a, rhs_b, pay_a, pay_b = back
    far_rhs_a, far_rhs_b = swap_section(pay_a), swap_section(pay_b)
    far_attn_other = swap_core(after(far_attn, grad_1))
    down_grad = weight(
        down_weight_kernel,
        (active_mine, active_other, far, far_other, upstream_half, after(far_upstream, grad_1)),
        (hidden, half),
        "down_weight",
    )
    up_grad = weight(
        up_weight_kernel,
        (normed_feed, far, far_other, back_mine, after(far_back, down_grad[0])),
        (width, width),
        "up_weight",
    )
    down_fold = folded(down_grad, up_grad[0])
    grads, grads_given = call(
        lambda *refs: norm_end_kernel(micro, *refs),
        (grad_1, *own_part, *swap_core(own_part), stream, after(params, first_of(down_fold))),
        [wide, wide],
        name="norm_end",
    )
    attn_grad_a = weight(
        attend_weight_a_kernel,
        (
            normed_attn,
            far_attn,
            far_attn_other,
            rhs_a,
            after(far_rhs_a, grads),
        ),
        (width, half),
        "attend_weight_a",
    )
    far_rhs_b = after(far_rhs_b, attn_grad_a[0])
    attn_grad_b = weight(
        attend_weight_b_kernel,
        (
            normed_attn,
            grad_1,
            far_attn,
            far_attn_other,
            rhs_b,
            far_rhs_b,
            swap_core(far_rhs_b),
            vector,
        ),
        (width, half),
        "attend_weight_b",
        EXTRA,
    )
    outputs, outputs_given = call(
        lambda *refs: last_kernel(micro, *refs),
        (middle, *fed, *swap_core([after(x, attn_grad_b[0]) for x in fed]), params),
        [wide, wide],
        name="last",
    )
    grads_given = after(grads_given, attn_grad_b[0])
    outputs = jnp.where(lead, outputs, swap_section(outputs_given))
    grads = jnp.where(lead, grads, swap_section(grads_given))
    up_fold = folded(up_grad, attn_grad_b[0])
    attn_fold_a = folded(attn_grad_a, first_of(up_fold))
    down_sum = closed(down_fold, first_of(attn_fold_a))
    attn_fold_b = folded(attn_grad_b, down_sum[0])
    up_sum = closed(up_fold, first_of(attn_fold_b))
    attn_sum_a = closed(attn_fold_a, up_sum[0], outputs)
    attn_sum_b = closed(attn_fold_b, attn_sum_a[0], extra=EXTRA)
    vector, vector_other = [x[width // chips // 2 :] for x in attn_sum_b]
    attn_sum_b = [x[: width // chips // 2] for x in attn_sum_b]

    def own_share(x, total):
        size = total // (2 * chips)
        return lax.dynamic_slice_in_dim(x, core * size, size, axis=0)

    vector = vector + vector_other
    up_shift_out = own_share(vector[0], hidden)
    down_shift_out = own_share(vector[1], half)
    gain_out = own_share(vector[2], width)

    attn_out = jnp.concatenate([by_core(*attn_sum_a, 1), by_core(*attn_sum_b, 1)], axis=1)
    up_out, down_out = by_core(*up_sum, 1), by_core(*down_sum, 1)

    shape = (1, 1, micro, rows, width)
    return (
        outputs.reshape(shape),
        grads.reshape(shape),
        attn_out[None],
        up_out[None],
        down_out[None],
        up_shift_out[None],
        down_shift_out[None],
        gain_out[None],
    )


def solution(mesh):
    in_specs = (
        P("dp", None, None, None),
        P("dp", None, None, None),
        P("dp", None, None),
        P("section", None, None),
        P("section", None, None),
        P("section", None, None),
        P("section", None),
        P("section", None),
        P("section", None),
    )
    out_specs = (
        P("section", "dp", None, None, None),
        P("section", "dp", None, None, None),
        P("section", "dp", None),
        P("section", "dp", None),
        P("section", "dp", None),
        P("section", "dp"),
        P("section", "dp"),
        P("section", "dp"),
    )
    return jax.shard_map(body, mesh=mesh, in_specs=in_specs, out_specs=out_specs, check_vma=False)
```

```python
import types

import jax
import jax.numpy as jnp
import numpy as np
from jax import lax
from jax.experimental import pallas as pl
from jax.experimental.pallas import tpu as pltpu
from jax.sharding import PartitionSpec as P

HEAD = 64
BLOCK = 16
EPSILON = 1e-05
MASKED = -1e30
LANES = 128
LINE = 4
EXTRA = 16
F32 = jnp.float32
BF16 = jnp.bfloat16
PART, NEAR, CORE, LEAD, FIRST, HIGH = range(6)


def dot(left, right):
    return lax.dot_general(left, right, (((1,), (0,)), ((), ())), preferred_element_type=F32)


def dot_cols(left, right):
    return lax.dot_general(left, right, (((1,), (1,)), ((), ())), preferred_element_type=F32)


def dot_rows(left, right):
    return lax.dot_general(left, right, (((0,), (0,)), ((), ())), preferred_element_type=F32)


def normalized(values):
    mean = jnp.mean(values, axis=-1, keepdims=True)
    centered = values - mean
    spread = jnp.mean(centered * centered, axis=-1, keepdims=True)
    rstd = lax.rsqrt(spread + EPSILON)
    return centered * rstd, rstd


def norm_backward(values, gain, upstream, grad_normed):
    xhat, rstd = normalized(values)
    scaled = grad_normed * gain
    mean = jnp.mean(scaled, axis=-1, keepdims=True)
    along = jnp.mean(scaled * xhat, axis=-1, keepdims=True)
    grad_gain = jnp.sum(grad_normed * xhat, axis=0, keepdims=True)
    grad = upstream.astype(F32) + rstd * (scaled - mean - xhat * along)
    return grad.astype(BF16), grad_gain


def joined(own, other):
    return jnp.concatenate([a[...].astype(F32) + b[...].astype(F32) for a, b in zip(own, other)], axis=0)


def where():
    section, replica = lax.axis_index("section"), lax.axis_index("dp")
    part, core, z = section % 2, replica % 2, replica // 2
    lead = (part == core).astype(jnp.int32)
    first = (section < 2).astype(jnp.int32)
    return part, z % 2, core, lead, first, z // 2 % 2


def scatter(value, pieces):
    rows = pieces[0].shape[0]
    for index, piece in enumerate(pieces):
        piece[...] = value[index * rows : (index + 1) * rows].astype(BF16)


def lanes_of(spot, half):
    return pl.ds(pl.multiple_of(spot[CORE] * half, LANES), half)


def swap_halves(block):
    lane = lax.broadcasted_iota(jnp.int32, block.shape, 1)
    low = lax.rem(lane, HEAD) < HEAD // 2
    ahead = pltpu.roll(block, LANES - HEAD // 2, 1)
    behind = pltpu.roll(block, HEAD // 2, 1)
    return jnp.where(low, ahead, behind)


def stacked(pair):
    lane = lax.broadcasted_iota(jnp.int32, pair.shape, 1)
    zero = jnp.zeros_like(pair)
    return jnp.concatenate(
        [jnp.where(lane < HEAD, pair, zero), jnp.where(lane < HEAD, zero, pair)], axis=0
    )


def merged(stack, rows):
    lane = lax.broadcasted_iota(jnp.int32, (rows, LANES), 1)
    return jnp.where(lane < HEAD, stack[:rows], stack[rows:])


def visible(table, at, rows, total):
    low = table[at : at + rows, 2 * LANES : 2 * LANES + 1]
    high = table[at : at + rows, 2 * LANES + 1 : 2 * LANES + 2]
    same = table[at : at + rows, 2 * LANES + 2 : 2 * LANES + 3]
    clean = table[total : total + 1, at : at + rows]
    noisy = table[total + 1 : total + 2, at : at + rows]
    return ((clean >= low) & (clean <= high)) | (noisy == same)


VECTOR = pl.BlockSpec(memory_space=pltpu.VMEM)
ANYWHERE = pl.BlockSpec(memory_space=pl.ANY)


def call(kernel, args, outs, scratch=(), name=None, held=()):
    count = len(args)

    def wrapped(*refs):
        kernel(*refs[:count], *refs[count + len(held) :])

    return pl.pallas_call(
        wrapped,
        out_shape=[jax.ShapeDtypeStruct(shape, dtype) for shape, dtype in outs],
        in_specs=[VECTOR] * (count + len(held)),
        out_specs=[VECTOR] * len(outs),
        scratch_shapes=list(scratch),
        compiler_params=pltpu.CompilerParams(vmem_limit_bytes=8 * 1024 * 1024),
        name=name,
    )(*args, *held)


GAIN_ATTN, GAIN_FEED, DOWN_SHIFT, SHIFT = range(4)


def cut_kernel(places, *refs):
    spot = where()
    count = len(places)
    refs = refs[1:]
    arrays, outs, sems = refs[: -count - 1], refs[-count - 1 : -1], refs[-1]
    copies = []
    for index, (number, place) in enumerate(places):
        row, column = place(spot)
        rows, columns = outs[index].shape
        lines = pl.ds(pl.multiple_of(row, 16), rows)
        lanes = pl.ds(pl.multiple_of(column, LANES), columns)
        copies.append(
            pltpu.make_async_copy(arrays[number].at[0, lines, lanes], outs[index], sems.at[index])
        )
    for copy in copies:
        copy.start()
    for copy in copies:
        copy.wait()


def cut(before, arrays, places, shapes, name):
    before = arrays[0] if before is None else before
    return pl.pallas_call(
        lambda *refs: cut_kernel(places, *refs),
        out_shape=[jax.ShapeDtypeStruct(shape, BF16) for shape in shapes],
        in_specs=[ANYWHERE] * (1 + len(arrays)),
        out_specs=[VECTOR] * len(shapes),
        scratch_shapes=[pltpu.SemaphoreType.DMA((len(shapes),))],
        compiler_params=pltpu.CompilerParams(vmem_limit_bytes=8 * 1024 * 1024),
        name=name,
    )(before, *arrays)


def table_kernel(micro, mine, theirs, turns, out):
    total = out.shape[0] - 8
    rows = total // micro
    half = rows // 2
    span = half // BLOCK + 1
    lead = where()[LEAD] == 1

    def layout(item, shape, axis):
        place = lax.broadcasted_iota(jnp.int32, shape, axis)
        clean = place >= half
        within = jnp.where(clean, place - half, place)
        document, begin = jnp.zeros(shape, jnp.int32), jnp.zeros(shape, jnp.int32)
        end = jnp.int32(0)
        for j in range(mine.shape[1]):
            length = jnp.where(lead, mine[item, j], theirs[item, j])
            end = end + length
            passed = (within >= end).astype(jnp.int32)
            document = document + passed
            begin = begin + passed * length
        offset = within - begin
        return clean, offset, document * span, document * span + offset // BLOCK

    for item in range(micro):
        at = pl.ds(item * rows, rows)
        clean, offset, low, block = layout(item, (rows, LANES), 0)
        lane = lax.broadcasted_iota(jnp.int32, (rows, LANES), 1)
        chosen = (offset[:, :half] == lane[:, :half]).astype(F32)
        out[at, : 2 * LANES] = lax.dot_general(
            chosen,
            turns[...],
            (((1,), (0,)), ((), ())),
            precision=lax.Precision.HIGHEST,
            preferred_element_type=F32,
        )
        high, same = jnp.where(clean, block, block - 1), jnp.where(clean, -1, block)
        codes = jnp.where(lane == 0, low, jnp.where(lane == 1, high, same))
        out[at, 2 * LANES : 3 * LANES] = codes.astype(F32)
        clean, _, _, block = layout(item, (8, rows), 1)
        row = lax.broadcasted_iota(jnp.int32, (8, rows), 0)
        keys = jnp.where(clean == (row == 0), block, -2)
        out[total:, at] = keys.astype(F32)


def attend_kernel(micro, keep, arrived, *refs):
    if arrived:
        mine, theirs, before, *refs = refs
    else:
        mine, theirs, *refs = refs
    params, table, *refs = refs
    spot = where()
    held, refs = refs[:4], refs[4:]
    partial, stream, refs = refs[:micro], refs[micro], refs[micro + 1 :]
    if keep:
        normed_out, q, k, v, mixed, chance, pay = refs
    else:
        q, k, v, mixed = refs
    total, width = stream.shape
    half = width // 2
    rows = total // micro
    if arrived:
        low = jnp.where(spot[CORE] == 0, mine[...], theirs[...])
        high = jnp.where(spot[CORE] == 0, theirs[...], mine[...])
        x = jnp.where(spot[FIRST] == 1, before[...], jnp.concatenate([low, high], axis=1))
    else:
        x = jnp.where(spot[LEAD] == 1, mine[...], theirs[...])
    stream[...] = x
    xhat, _ = normalized(x.astype(F32))
    normed = (xhat * params[GAIN_ATTN : GAIN_ATTN + 1, :width]).astype(BF16)
    if keep:
        normed_out[...] = normed
    v[...] = dot(normed, held[2][...]).astype(BF16)
    cos, sin = table[:total, :LANES], table[:total, LANES : 2 * LANES]
    for index, target in ((0, q), (1, k)):
        wide = dot(normed, held[index][...])
        for at in range(0, half, LANES):
            block = wide[:, at : at + LANES]
            target[:, at : at + LANES] = (block * cos + swap_halves(block) * sin).astype(BF16)
    for item in range(micro):
        place = pl.ds(item * rows, rows)
        mask = visible(table, item * rows, rows, total)
        mask = jnp.concatenate([mask, mask], axis=0)
        for pair in range(half // LANES):
            lanes = pl.ds(pair * LANES, LANES)
            scores = dot_cols(stacked(q[place, lanes]), k[place, lanes]) * HEAD ** (-0.5)
            scores = jnp.where(mask, scores, MASKED)
            peak = jnp.max(scores, axis=-1, keepdims=True)
            powers = jnp.exp(scores - peak)
            weights = powers / jnp.sum(powers, axis=-1, keepdims=True)
            if keep:
                chance[item * (half // LANES) + pair] = weights
            mixed[place, lanes] = merged(dot(weights.astype(BF16), v[place, lanes]), rows).astype(BF16)
    scatter(dot_cols(mixed[...], held[3][...]), partial)
    if keep:
        pay[:, :half] = normed_out[:, lanes_of(spot, half)]
        pay[:, half:] = mixed[...]


def feed_up(x, own, other, params, held, stream, normed_out, active, slope):
    width = x.shape[1]
    result = (x[...].astype(F32) + joined(own, other)).astype(BF16)
    stream[...] = result
    xhat, _ = normalized(result.astype(F32))
    normed = (xhat * params[GAIN_FEED : GAIN_FEED + 1, :width]).astype(BF16)
    normed_out[...] = normed
    scale = (2.0 / jnp.pi) ** 0.5
    piece = 2 * LANES
    for index in (0, 1):
        for at in range(0, width, piece):
            wide = pl.ds(index * width + at, piece)
            lanes = pl.ds(at, piece)
            if index == 0 or len(held) == 2:
                before = dot(normed, held[index][:, lanes])
            else:
                first, second = ends(where(), width, width // 2)
                before = dot(normed_out[:, first], held[1][:, lanes])
                before += dot(normed_out[:, second], held[2][:, lanes])
            before = before + params[SHIFT : SHIFT + 1, wide]
            square = before * before
            bend = jnp.tanh(scale * before * (1.0 + 0.044715 * square))
            active[index][:, at : at + piece] = (0.5 * before * (1.0 + bend)).astype(BF16)
            if slope is not None:
                inner = scale * (1.0 + 3 * 0.044715 * square)
                tilt = 0.5 * (1.0 + bend) + 0.5 * before * (1.0 - bend * bend) * inner
                slope[:, wide] = tilt.astype(BF16)


def feed_up_kernel(micro, x, *refs):
    own, other, refs = refs[:micro], refs[micro : 2 * micro], refs[2 * micro :]
    params, up_mine, up_near, up_next, down_mine, stream, theirs, total, mine, normed = refs
    ups = (up_mine, up_near, up_next)
    feed_up(x, own, other, params, ups, stream, normed, (mine, theirs), None)
    total[...] = dot(mine[...], down_mine[...])


def ends(spot, width, size):
    return [pl.ds(pl.multiple_of(at * (width - size), LANES), size) for at in (spot[NEAR], 1 - spot[NEAR])]


def feed_down_kernel(total, theirs, near, middle, following, *partial):
    size, width = near.shape
    first, second = ends(where(), width, size)
    result = total[...] + dot(theirs[:, size : width - size], middle[...])
    result += dot(theirs[:, first], near[...]) + dot(theirs[:, second], following[...])
    scatter(result, partial)


def feed_kernel(micro, x, *refs):
    own, other, refs = refs[:micro], refs[micro : 2 * micro], refs[2 * micro :]
    params, up_mine, up_theirs, down_mine, down_theirs, *refs = refs
    spot = where()
    partial, refs = refs[:micro], refs[micro:]
    stream, normed, mine, slope, pay, theirs = refs
    width = x.shape[1]
    half = width // 2
    feed_up(x, own, other, params, (up_mine, up_theirs), stream, normed, (mine, theirs), slope)
    scatter(dot(mine[...], down_mine[...]) + dot(theirs[...], down_theirs[...]), partial)
    lanes = lanes_of(spot, half)
    pay[:, :half] = normed[:, lanes]
    pay[:, half:] = theirs[...]


def finish_kernel(micro, stream, *refs):
    own, other, refs = refs[:micro], refs[micro : 2 * micro], refs[2 * micro :]
    params, part, result = refs
    spot = where()
    width = stream.shape[1]
    shift = params[DOWN_SHIFT : DOWN_SHIFT + 1, :width]
    result[...] = (stream[...].astype(F32) + (joined(own, other) + shift)).astype(BF16)
    part[...] = result[:, lanes_of(spot, part.shape[1])]


def last_kernel(micro, stream, *refs):
    own, other, refs = refs[:micro], refs[micro : 2 * micro], refs[2 * micro :]
    params, mine, theirs = refs
    spot = where()
    width = stream.shape[1]
    shift = params[DOWN_SHIFT : DOWN_SHIFT + 1, :width]
    middle = stream[...]
    result = (middle.astype(F32) + (joined(own, other) + shift)).astype(BF16)
    mine[...] = jnp.where(spot[PART] == 0, middle, result)
    theirs[...] = jnp.where(spot[PART] == 0, result, middle)


def feed_back_kernel(micro, arrived, *refs):
    if arrived:
        half_mine, half_theirs, *refs = refs
    else:
        whole_mine, whole_theirs, *refs = refs
    slope, up_mine, up_theirs, down_mine, down_theirs, *refs = refs
    spot = where()
    partial, upstream, refs = refs[:micro], refs[micro], refs[micro + 1 :]
    if arrived:
        mine, theirs, sums = refs
    else:
        mine, theirs = refs
    rows, width = upstream.shape
    if arrived:
        low = jnp.where(spot[CORE] == 0, half_mine[...], half_theirs[...])
        high = jnp.where(spot[CORE] == 0, half_theirs[...], half_mine[...])
        dz = jnp.concatenate([low, high], axis=1)
        sums[2:3, :] = jnp.sum(dz.astype(F32), axis=0, keepdims=True)
        sums[3:, :] = jnp.zeros((sums.shape[0] - 3, width), F32)
    else:
        dz = jnp.where(spot[LEAD] == 1, whole_mine[...], whole_theirs[...])
    upstream[...] = dz
    piece = 2 * LANES
    for index, (down, back) in enumerate(((down_mine, mine), (down_theirs, theirs))):
        for at in range(0, width, piece):
            grad = dot_cols(dz, down[at : at + piece, :])
            grad = grad * slope[:, index * width + at : index * width + at + piece].astype(F32)
            rounded = grad.astype(BF16)
            back[:, at : at + piece] = rounded
            if arrived:
                sums[index : index + 1, at : at + piece] = jnp.sum(
                    rounded.astype(F32), axis=0, keepdims=True
                )
    scatter(dot_cols(mine[...], up_mine[...]) + dot_cols(theirs[...], up_theirs[...]), partial)


def attend_back_kernel(micro, keep, dz, *refs):
    own, other, refs = refs[:micro], refs[micro : 2 * micro], refs[2 * micro :]
    x, params, chance, v, k, q, mixed, table, *refs = refs
    spot = where()
    held, refs = refs[:4], refs[4:]
    given = micro + 2 if keep else micro
    partial, refs = refs[:given], refs[given:]
    grad, *refs = refs
    if keep:
        vector, rhs_a, rhs_b, pay_a, pay_b, *refs = refs
        stream, sums, *partial = partial
    dq, dk, dv, dmixed = refs
    total, width = x.shape
    half = width // 2
    rows = total // micro
    gain = params[GAIN_FEED : GAIN_FEED + 1, :width]
    result, gain_sum = norm_backward(x[...].astype(F32), gain, dz[...], joined(own, other))
    grad[...] = result
    dmixed[...] = dot(result, held[3][...]).astype(BF16)
    for item in range(micro):
        place = pl.ds(item * rows, rows)
        turn = table[item * rows : (item + 1) * rows, :LANES]
        tilt = table[item * rows : (item + 1) * rows, LANES : 2 * LANES]
        for pair in range(half // LANES):
            lanes = pl.ds(pair * LANES, LANES)
            weights = chance[item * (half // LANES) + pair]
            grads = stacked(dmixed[place, lanes])
            queries = stacked(q[place, lanes])
            dv[place, lanes] = dot_rows(weights.astype(BF16), grads).astype(BF16)
            spread = dot_cols(grads, v[place, lanes])
            inner = jnp.sum(weights * spread, axis=-1, keepdims=True)
            scores = (weights * (spread - inner)).astype(BF16)
            query_grad = merged(dot(scores, k[place, lanes]), rows) * HEAD ** (-0.5)
            key_grad = dot_rows(scores, queries) * HEAD ** (-0.5)
            dq[place, lanes] = (query_grad * turn - swap_halves(query_grad) * tilt).astype(BF16)
            dk[place, lanes] = (key_grad * turn - swap_halves(key_grad) * tilt).astype(BF16)
    if keep:
        even = spot[PART] == 0
        rhs_a[...] = jnp.where(even, dq[...], dv[...])
        rhs_b[...] = jnp.where(even, dk[...], mixed[...])
        pay_a[...] = jnp.where(even, dv[...], dq[...])
        pay_b[:total] = jnp.where(even, grad[:, lanes_of(spot, half)], dk[...])
    back = dot_cols(dq[...], held[0][...]) + dot_cols(dk[...], held[1][...])
    back += dot_cols(dv[...], held[2][...])
    scatter(back, partial)
    if keep:
        xhat, _ = normalized(stream[...].astype(F32))
        attn_gain = jnp.sum(back * xhat, axis=0, keepdims=True)
        zero = jnp.zeros((1, half), F32)
        alone = spot[CORE] == 0
        feed_gain = jnp.where(alone, gain_sum, 0.0)
        low = jnp.where(alone, sums[2:3, :half], zero)
        high = jnp.where(alone, sums[2:3, half:], zero)
        mine = (sums[0:1, :], jnp.where(even, low, high), jnp.where(even, attn_gain, feed_gain))
        theirs = (sums[1:2, :], jnp.where(even, high, low), jnp.where(even, feed_gain, attn_gain))
        vector[...] = rows_of(split(mine), half)
        wide = rows_of(split(theirs), half)
        above = wide.astype(BF16)
        pay_b[total : total + EXTRA] = above
        pay_b[total + EXTRA :] = (wide - above.astype(F32)).astype(BF16)


def split(vectors):
    units, features, gain = vectors
    half = features.shape[1]
    return units[:, :half], units[:, half:], features, gain[:, :half], gain[:, half:]


def rows_of(vectors, width):
    rows = [jnp.pad(x, ((0, 0), (0, width - x.shape[1]))) for x in vectors]
    return jnp.concatenate(rows + [jnp.zeros((EXTRA - len(rows), width), F32)], axis=0)


def norm_back_kernel(micro, dz, *refs):
    own, other, refs = refs[:micro], refs[micro : 2 * micro], refs[2 * micro :]
    x, params, grad, part = refs
    spot = where()
    gain = params[GAIN_ATTN : GAIN_ATTN + 1, : x.shape[1]]
    result, _ = norm_backward(x[...].astype(F32), gain, dz[...], joined(own, other))
    grad[...] = result
    part[...] = grad[:, lanes_of(spot, part.shape[1])]


def norm_end_kernel(micro, dz, *refs):
    own, other, refs = refs[:micro], refs[micro : 2 * micro], refs[2 * micro :]
    x, params, mine, theirs = refs
    spot = where()
    gain = params[GAIN_ATTN : GAIN_ATTN + 1, : x.shape[1]]
    upstream = dz[...]
    result, _ = norm_backward(x[...].astype(F32), gain, upstream, joined(own, other))
    even = spot[PART] == 0
    mine[...] = jnp.where(even, result, upstream)
    theirs[...] = jnp.where(even, upstream, result)


def halves(spot, size):
    return [(pl.ds(pl.multiple_of(at * size, LANES), size), at) for at in (spot[CORE], 1 - spot[CORE])]


def deal(grad, half, spot, kept, given):
    pairs, size = kept.shape[0], kept.shape[1]
    for i in range(pairs // 2):
        low = grad[2 * i * size : (2 * i + 1) * size]
        high = grad[(2 * i + 1) * size : (2 * i + 2) * size]
        place = half * (pairs // 2) + i
        kept[place] = jnp.where(spot[NEAR] == 0, low, high).astype(BF16)
        given[place] = jnp.where(spot[NEAR] == 0, high, low).astype(BF16)


def down_weight_kernel(near, near_other, far, far_other, dz, far_dz, *outs):
    spot = where()
    width = near.shape[1]
    at = far.shape[1] - width
    lefts = ((near, far), (near_other, far_other))
    for (left, far_left), (_, half) in zip(lefts, halves(spot, width)):
        grad = dot_rows(left[...], dz[...]) + dot_rows(far_left[:, at:], far_dz[...])
        deal(grad, half, spot, *outs)


def up_weight_kernel(near, far, far_other, back, far_back, kept, given):
    spot = where()
    size = near.shape[1] // 2
    for left, (lines, half) in zip((far, far_other), halves(spot, size)):
        grad = dot_rows(near[:, lines], back[...]) + dot_rows(left[:, :size], far_back[...])
        deal(grad, half, spot, kept, given)


def attend_weight_a_kernel(near, far, far_other, right, far_right, kept, given):
    spot = where()
    size = near.shape[1] // 2
    for left, (lines, half) in zip((far, far_other), halves(spot, size)):
        grad = dot_rows(near[:, lines], right[...]) + dot_rows(left[:, :size], far_right[...])
        deal(grad, half, spot, kept, given)


def attend_weight_b_kernel(
    near, grad_in, far, far_other, right, far_right, far_right_other, vector, kept, given
):
    spot = where()
    size = near.shape[1] // 2
    rows = near.shape[0]
    below = kept.shape[1] - EXTRA
    even = spot[PART] == 0
    rights = jnp.where(even, far_right[:rows], far[:, size:])
    lefts = ((far, far_right), (far_other, far_right_other))
    for (left, back), (lines, half) in zip(lefts, halves(spot, size)):
        grad = dot_rows(jnp.where(even, near[:, lines], grad_in[:, lines]), right[...])
        grad += dot_rows(jnp.where(even, left[:, :size], back[:rows]), rights)
        deal(grad, half, spot, kept.at[:, :below], given.at[:, :below])
    total = vector[...] + far_right[rows : rows + EXTRA].astype(F32) + far_right[rows + EXTRA :].astype(F32)
    chips = 2 * kept.shape[0]
    parts = []
    for chip in range(chips):
        lines = []
        for row, extent in ((0, 4 * size), (2, size), (3, 2 * size)):
            each = extent // chips
            at = chip * each
            mine = spot[CORE] == at // (2 * size)
            if row == 0:
                at %= 2 * size
            piece = total[row + at // size : row + at // size + 1, at % size : at % size + each]
            lines.append(jnp.where(mine, piece, 0.0) if row == 0 else piece)
        parts.append(rows_of(lines, size))
    for i in range(chips // 2):
        low, high = parts[2 * i], parts[2 * i + 1]
        kept[i, below:] = jnp.where(spot[NEAR] == 0, low, high).astype(BF16)
        given[i, below:] = jnp.where(spot[NEAR] == 0, high, low).astype(BF16)


def fold_kernel(kept, received, out, given):
    spot = where()
    low = kept[0].astype(F32) + received[0].astype(F32)
    high = kept[1].astype(F32) + received[1].astype(F32)
    out[0] = jnp.where(spot[HIGH] == 0, low, high)
    given[0] = jnp.where(spot[HIGH] == 0, high, low).astype(BF16)


def close_kernel(extra, kept, received, out, given):
    spot = where()
    size = out.shape[0] - extra
    total = kept[0] + received[0].astype(F32)
    low, high = total[:size], total[size : 2 * size]
    out[:size] = jnp.where(spot[CORE] == 0, low, high)
    given[:size] = jnp.where(spot[CORE] == 0, high, low)
    if extra:
        out[size:] = total[2 * size :]
        given[size:] = total[2 * size :]


def attend_out_kernel(mine_a, theirs_a, mine, theirs, out, units, features, gain):
    first = where()[CORE] == 0
    size, half = mine_a.shape
    for at, own, other in ((0, mine_a[...], theirs_a[...]), (2 * half, mine[:size], theirs[:size])):
        out[:, at : at + half] = jnp.where(first, own, other)
        out[:, at + half : at + 2 * half] = jnp.where(first, other, own)
    total = mine[size:] + theirs[size:]
    for row, x in enumerate((units, features, gain)):
        each = x.shape[1]
        x[...] = jnp.where(first, total[row : row + 1, :each], total[row : row + 1, each : 2 * each])


def swap_section(x):
    return lax.ppermute(x, "section", [(i, i ^ 1) for i in range(lax.axis_size("section"))])


def swap_layer(x):
    return lax.ppermute(x, "section", [(i, i ^ 2) for i in range(lax.axis_size("section"))])


def swap_core(x):
    return lax.ppermute(x, "dp", [(i, i ^ 1) for i in range(lax.axis_size("dp"))])


def swap_chip(x, distance):
    return lax.ppermute(x, "dp", [(i, i ^ (2 * distance)) for i in range(lax.axis_size("dp"))])


def after(x, *others):
    return lax.optimization_barrier((x,) + others)[0]


def replica_sum(kept, given, z, chips):
    if chips > LINE:
        pair = jnp.where(z % 2 == 0, jnp.stack([kept, given], 1), jnp.stack([given, kept], 1))
        groups = [[2 * i + c for i in range(chips)] for c in (0, 1)]
        return lax.psum_scatter(
            pair.reshape(chips, *kept.shape[1:]),
            "dp",
            scatter_dimension=0,
            axis_index_groups=groups,
            tiled=False,
        ).astype(F32)
    distance = 1
    while True:
        total = kept.astype(F32) + swap_chip(given, distance).astype(F32)
        if total.shape[0] == 1:
            return total[0]
        distance *= 2
        bit = z // distance % 2
        pairs = total.reshape(total.shape[0] // 2, 2, *total.shape[1:])
        given = lax.dynamic_index_in_dim(pairs, 1 - bit, 1, keepdims=False).astype(given.dtype)
        kept = lax.dynamic_index_in_dim(pairs, bit, 1, keepdims=False)


def rotations(places):
    count = HEAD // 2
    freq = np.power(10000.0, -2.0 * np.arange(count, dtype=np.float32) / HEAD).astype(np.float32)
    angle = np.arange(places, dtype=np.float32)[:, None] * freq[None, :]
    cosine, sine = np.cos(angle), np.sin(angle)
    parts = [cosine] * (LANES // count) + [-sine, sine] * (LANES // HEAD)
    return jnp.asarray(np.concatenate(parts, axis=1).astype(np.float32))


def body(
    hidden_in,
    cotangent,
    doc_lengths,
    attn_weight,
    up_weight,
    down_weight,
    up_bias,
    down_bias,
    norm_gain,
):
    section = lax.axis_index("section")
    replica = lax.axis_index("dp")
    chips = lax.axis_size("dp") // 2
    part, layer = section % 2, section // 2
    core, z = replica % 2, replica // 2
    near = z % 2
    even, lead, first = part == 0, core == part, layer == 0
    micro, rows, width = hidden_in.shape[1:]
    total, half = micro * rows, width // 2
    hidden = up_weight.shape[2]
    blocks = micro * (half // LANES)

    def columns(x, at, size):
        return lax.dynamic_slice_in_dim(x, at, size, axis=1)

    def by_part(mine, theirs, axis):
        return jnp.where(
            even, jnp.concatenate([mine, theirs], axis), jnp.concatenate([theirs, mine], axis)
        )

    def by_core(mine, theirs, axis):
        return jnp.where(
            core == 0, jnp.concatenate([mine, theirs], axis), jnp.concatenate([theirs, mine], axis)
        )

    wide, narrow = ((total, width), BF16), ((total, half), BF16)
    pieces = [((rows, width), BF16)] * micro
    vectors = ((8, width), F32)

    shift_mine = lax.dynamic_slice_in_dim(up_bias[0], core * width, width, axis=0).astype(F32)
    small = jnp.concatenate([shift_mine, down_bias[0].astype(F32), norm_gain[0]])
    def given(at, array, place, shape, name):
        return cut(at, (array,), [(0, place)], [shape], name)[0]

    attn_given = given(
        None,
        attn_weight,
        lambda spot: (0, spot[NEAR] * width + spot[CORE] * half),
        (width, half),
        "cut_attn",
    )
    up_given = given(
        attn_given,
        up_weight,
        lambda spot: (spot[NEAR] * half, spot[CORE] * width),
        (half, width),
        "cut_up",
    )
    attn_near, up_near = swap_section(attn_given), swap_section(up_given)
    hidden_in, cotangent, doc_lengths, small = lax.optimization_barrier(
        (hidden_in, cotangent, doc_lengths, small, up_given)
    )[:4]
    hidden_in, cotangent = hidden_in.reshape(wide[0]), cotangent.reshape(wide[0])
    hidden_other, lengths_other = swap_core((hidden_in, doc_lengths[0]))
    middle_rows = width - 2 * LANES
    down_end, down_given = cut(
        after(hidden_other, small),
        (down_weight,),
        [
            (0, lambda spot: (spot[CORE] * width + spot[NEAR] * (width - LANES), 0)),
            (0, lambda spot: (spot[CORE] * width + LANES, 0)),
        ],
        [(LANES, width), (middle_rows, width)],
        "cut_down",
    )
    down_near, down_middle = swap_section(down_end), swap_section(down_given)
    attn_next, up_next = swap_chip(attn_near, 1), swap_chip(up_near, 1)
    attn_own = cut(
        up_given,
        (attn_weight,),
        [(0, lambda spot, i=i: (0, i * width + spot[CORE] * half)) for i in (0, 1)],
        [(width, half)] * 2,
        "cut_own",
    )
    feed_own = cut(
        down_end,
        (up_weight, down_weight),
        [(0, lambda spot: (0, spot[CORE] * width)), (1, lambda spot: (spot[CORE] * width, 0))],
        [(width, width)] * 2,
        "cut_feed",
    )
    small_theirs = after(swap_section(small), attn_next)
    scalars = pl.BlockSpec(memory_space=pltpu.SMEM)
    table = pl.pallas_call(
        lambda *refs: table_kernel(micro, *refs),
        out_shape=jax.ShapeDtypeStruct((total + 8, max(3 * LANES, total)), F32),
        in_specs=[scalars, scalars, VECTOR],
        out_specs=VECTOR,
        compiler_params=pltpu.CompilerParams(vmem_limit_bytes=8 * 1024 * 1024),
        name="table",
    )(after(doc_lengths[0], attn_near), lengths_other, rotations(rows // 2))
    down_shift = by_part(small[width : width + half], small_theirs[width : width + half], 0)
    gains = [jnp.pad(x[width + half :], (0, width)) for x in (small, small_theirs)]
    params = jnp.stack(
        [
            jnp.where(even, gains[0], gains[1]),
            jnp.where(even, gains[1], gains[0]),
            jnp.pad(down_shift, (0, width)),
            jnp.concatenate([shift_mine, small_theirs[:width]]),
        ]
    )
    params = jnp.pad(params, ((0, 4), (0, 0)))

    def ordered(mine, theirs, *between):
        low, high = jnp.where(near == 0, mine, theirs), jnp.where(near == 0, theirs, mine)
        return jnp.concatenate([low, *between, high], axis=0)

    low, high = jnp.where(near == 0, attn_near, attn_next), jnp.where(near == 0, attn_next, attn_near)
    attn = (
        jnp.where(even, attn_own[0], low),
        jnp.where(even, attn_own[1], high),
        jnp.where(even, low, attn_own[0]),
        jnp.where(even, high, attn_own[1]),
    )

    def attend(streams, keep):
        arrived = len(streams) == 3
        outs, scratch = pieces + [wide], [pltpu.VMEM(*narrow)] * 4
        if keep:
            outs, scratch = outs + [wide] + [narrow] * 4 + [((blocks, 2 * rows, rows), F32), wide], ()
        out = call(
            lambda *refs: attend_kernel(micro, keep, arrived, *refs),
            (*streams, params, table, *attn),
            outs,
            scratch,
            "attend",
        )
        return out[:micro], out[micro:]

    own_part, (stream_0,) = attend((hidden_in, hidden_other), False)
    down_next = swap_chip(after(down_near, own_part[0]), 1)
    middle, *active = call(
        lambda *refs: feed_up_kernel(micro, *refs),
        (
            stream_0,
            *own_part,
            *swap_core(own_part),
            params,
            feed_own[0],
            up_near,
            up_next,
            feed_own[1],
        ),
        [wide] * 2 + [(wide[0], F32)],
        [pltpu.VMEM(*wide)] * 2,
        name="feed_up",
    )
    own_part = call(
        feed_down_kernel, (active[1], active[0], down_near, down_middle, down_next), pieces, name="feed_down"
    )
    arrived = call(
        lambda *refs: finish_kernel(micro, *refs),
        (middle, *own_part, *swap_core(own_part), params),
        [narrow],
        [pltpu.VMEM(*wide)],
        "finish",
    )[0]
    ups = (feed_own[0], ordered(after(up_near, arrived), up_next))
    downs = (feed_own[1], ordered(after(down_near, arrived), down_next, down_middle))
    arrived = after(swap_layer(arrived), ups[1], downs[1])
    own_part, kept = attend((arrived, swap_core(arrived), stream_0), True)
    stream, normed_attn, q, k, v, mixed, chance, pay_attn = kept
    far_attn = swap_section(pay_attn)
    out = call(
        lambda *refs: feed_kernel(micro, *refs),
        (stream, *own_part, *swap_core(own_part), params, *ups, *downs),
        pieces + [wide] * 3 + [((total, 2 * width), BF16), ((total, width + half), BF16)],
        [pltpu.VMEM(*wide)],
        "feed",
    )
    fed, (middle, normed_feed, active_mine, slope, pay) = out[:micro], out[micro:]
    far = swap_section(pay)

    def feed_back(upstreams, arrived, held=()):
        outs, scratch = pieces + [wide], [pltpu.VMEM(*wide)] * 2
        if arrived:
            outs, scratch = outs + [wide, wide, vectors], ()
        out = call(
            lambda *refs: feed_back_kernel(micro, arrived, *refs),
            (*upstreams, slope, *ups, *downs),
            outs,
            scratch,
            "feed_back",
            held,
        )
        return out[:micro], out[micro:]

    def attend_back(upstream, own, other, params, keep, held=()):
        outs = pieces + [wide]
        more = ()
        if keep:
            outs += [((EXTRA, half), F32)] + [narrow] * 3 + [((total + 2 * EXTRA, half), BF16)]
            more = keep
        out = call(
            lambda *refs: attend_back_kernel(micro, bool(keep), *refs),
            (upstream, *own, *other, middle, params, chance, v, k, q, mixed, table, *attn, *more),
            outs,
            [pltpu.VMEM(*narrow)] * 4,
            "attend_back",
            held,
        )
        return out[:micro], out[micro:]

    kept_on = (slope, *fed)
    cotangent_other = swap_core(after(cotangent, arrived))
    own_part, (upstream_0,) = feed_back((cotangent, cotangent_other), False, kept_on)
    own_part, (grad,) = attend_back(
        upstream_0, own_part, swap_core(own_part), params, (), kept_on
    )
    *own_part, far_attn = lax.optimization_barrier((*own_part, far_attn))
    grad_2, arrived = call(
        lambda *refs: norm_back_kernel(micro, *refs),
        (grad, *own_part, *swap_core(own_part), stream, params),
        [wide, narrow],
        name="norm_back",
        held=kept_on,
    )
    arrived = swap_layer(arrived)
    upstream_half = after(columns(upstream_0, core * half, half), grad_2)

    def weight(kernel, args, shape, name, extra=0):
        outs = [((chips // 2, shape[0] // chips + extra, shape[1]), BF16)] * 2
        return call(kernel, args, outs, name=name)

    def folded(grad, token):
        kept, given = grad
        if chips != LINE:
            return replica_sum(kept, given, z, chips)
        received = after(swap_chip(given, 1), token)
        part = (1, *kept.shape[1:])
        return call(fold_kernel, (kept, received), [(part, F32), (part, BF16)], name="fold")

    def closed(fold, token, extra=0):
        if chips != LINE:
            size = (fold.shape[0] - extra) // 2
            mine = lax.dynamic_slice_in_dim(fold, core * size, size, axis=0)
            theirs = lax.dynamic_slice_in_dim(fold, (1 - core) * size, size, axis=0)
            mine, theirs = [jnp.concatenate([x, fold[2 * size :]], axis=0) for x in (mine, theirs)]
            return mine, swap_core(theirs)
        kept, given = fold
        received = after(swap_chip(given, 2), token)
        part = (((kept.shape[-2] + extra) // 2, kept.shape[-1]), F32)
        mine, theirs = call(
            lambda *refs: close_kernel(extra, *refs), (kept, received), [part] * 2, name="close"
        )
        return mine, swap_core(theirs)

    x = types.SimpleNamespace(far=far, far_attn=far_attn)

    def take_upstream(token):
        x.half = jnp.where(first, after(arrived, token), upstream_half)
        x.half_other, x.far_half = swap_core(x.half), swap_section(x.half)
        return x.half

    def take_far(token):
        x.far = after(x.far, token)
        x.far_other = swap_core(x.far)
        return x.far

    def send_active(token):
        x.active_other = swap_core(after(active_mine, token))
        return token

    def feed_step(token):
        x.part, back = feed_back((after(x.half, token), x.half_other), True)
        x.upstream, x.back, theirs, x.sums = back
        x.far_back = swap_section(theirs)
        return x.upstream

    def take_attn(token):
        x.far_attn = after(x.far_attn, token)
        return x.far_attn

    def attend_step(token):
        part = [after(y, token) for y in x.part]
        x.part, back = attend_back(x.upstream, part, swap_core(part), params, (stream, x.sums))
        x.grad, x.vector, x.rhs_a, x.rhs_b, pay_a, pay_b = back
        x.far_rhs_a, x.far_rhs_b = swap_section(pay_a), swap_section(pay_b)
        return x.grad

    def send_attn(token):
        x.far_attn_other = swap_core(after(x.far_attn, token))
        return token

    def take_half(token):
        x.far_half = after(x.far_half, token)
        return x.far_half

    def take_back(token):
        x.far_back = after(x.far_back, token)
        return x.far_back

    def take_rhs_a(token):
        x.far_rhs_a = after(x.far_rhs_a, token)
        return x.far_rhs_a

    def take_rhs_b(token):
        x.far_rhs_b = after(x.far_rhs_b, token)
        x.far_rhs_b_other = swap_core(x.far_rhs_b)
        return x.far_rhs_b

    def down_step(token):
        args = (active_mine, x.active_other, x.far, x.far_other, x.half, after(x.far_half, token))
        x.down = weight(down_weight_kernel, args, (hidden, half), "down_weight")
        return x.down[0]

    def up_step(token):
        args = (normed_feed, x.far, x.far_other, x.back, after(x.far_back, token))
        x.up = weight(up_weight_kernel, args, (width, width), "up_weight")
        return x.up[0]

    def attn_step_a(token):
        args = (normed_attn, x.far_attn, x.far_attn_other, x.rhs_a, after(x.far_rhs_a, token))
        x.attn_a = weight(attend_weight_a_kernel, args, (width, half), "attend_weight_a")
        return x.attn_a[0]

    def attn_step_b(token):
        args = (normed_attn, x.grad, x.far_attn, x.far_attn_other, x.rhs_b)
        args += (after(x.far_rhs_b, token), x.far_rhs_b_other, x.vector)
        x.attn_b = weight(attend_weight_b_kernel, args, (width, half), "attend_weight_b", EXTRA)
        return x.attn_b[0]

    def norm_step(token):
        x.grads, x.grads_given = call(
            lambda *refs: norm_end_kernel(micro, *refs),
            (x.grad, *x.part, *swap_core(x.part), stream, after(params, token)),
            [wide, wide],
            name="norm_end",
        )
        return x.grads

    def send_fed(token):
        x.fed_other = swap_core([after(y, token) for y in fed])
        return token

    def last_step(token):
        x.outputs, x.outputs_given = call(
            lambda *refs: last_kernel(micro, *refs),
            (middle, *fed, *x.fed_other, after(params, token)),
            [wide, wide],
            name="last",
        )
        return x.outputs

    def send_outputs(token):
        x.outputs_far = swap_section(after(x.outputs_given, token))
        return token

    def send_grads(token):
        x.grads_far = swap_section(after(x.grads_given, token))
        return token

    def take_outputs(token):
        x.outputs = jnp.where(lead, x.outputs, after(x.outputs_far, token))
        return x.outputs

    def take_grads(token):
        x.grads = jnp.where(lead, x.grads, after(x.grads_far, token))
        return x.grads

    def down_fold(token):
        x.down = folded(x.down, token)
        return x.down[0]

    def up_fold(token):
        x.up = folded(x.up, token)
        return x.up[0]

    def attn_fold_a(token):
        x.attn_a = folded(x.attn_a, token)
        return x.attn_a[0]

    def attn_fold_b(token):
        x.attn_b = folded(x.attn_b, token)
        return x.attn_b[0]

    def down_close(token):
        x.down = closed(x.down, token)
        return x.down[0]

    def up_close(token):
        x.up = closed(x.up, token)
        return x.up[0]

    def attn_close_a(token):
        x.attn_a = closed(x.attn_a, token)
        return x.attn_a[0]

    def attn_close_b(token):
        x.attn_b = closed(x.attn_b, token, EXTRA)
        return x.attn_b[0]

    token = grad_2
    for step in (
        take_upstream,
        take_far,
        send_active,
        feed_step,
        take_attn,
        attend_step,
        send_attn,
        take_half,
        down_step,
        take_back,
        up_step,
        down_fold,
        norm_step,
        take_rhs_a,
        attn_step_a,
        take_rhs_b,
        attn_step_b,
        send_grads,
        send_fed,
        up_fold,
        attn_fold_a,
        down_close,
        last_step,
        send_outputs,
        attn_fold_b,
        up_close,
        take_grads,
        take_outputs,
        attn_close_a,
        attn_close_b,
    ):
        token = step(token)

    size = width // (2 * chips)
    if chips == LINE:
        attn_out, up_shift_out, down_shift_out, gain_out = call(
            attend_out_kernel,
            (*x.attn_a, *x.attn_b),
            [((size, hidden), F32)] + [((1, y // (2 * chips)), F32) for y in (hidden, half, width)],
            name="attend_out",
        )
    else:
        attn_out = jnp.concatenate(
            [by_core(*x.attn_a, 1), by_core(*[y[:size] for y in x.attn_b], 1)], axis=1
        )
        vector = x.attn_b[0][size:] + x.attn_b[1][size:]
        up_shift_out, down_shift_out, gain_out = [
            columns(vector[i : i + 1], core * (y // (2 * chips)), y // (2 * chips))
            for i, y in enumerate((hidden, half, width))
        ]
    up_out, down_out = by_core(*x.up, 1), by_core(*x.down, 1)

    shape = (1, 1, micro, rows, width)
    return (
        x.outputs.reshape(shape),
        x.grads.reshape(shape),
        attn_out[None],
        up_out[None],
        down_out[None],
        up_shift_out,
        down_shift_out,
        gain_out,
    )


def solution(mesh):
    in_specs = (
        P("dp", None, None, None),
        P("dp", None, None, None),
        P("dp", None, None),
        P("section", None, None),
        P("section", None, None),
        P("section", None, None),
        P("section", None),
        P("section", None),
        P("section", None),
    )
    out_specs = (
        P("section", "dp", None, None, None),
        P("section", "dp", None, None, None),
        P("section", "dp", None),
        P("section", "dp", None),
        P("section", "dp", None),
        P("section", "dp"),
        P("section", "dp"),
        P("section", "dp"),
    )
    return jax.shard_map(body, mesh=mesh, in_specs=in_specs, out_specs=out_specs, check_vma=False)
```

```python
import types

import jax
import jax.numpy as jnp
import numpy as np
from jax import lax
from jax.experimental import pallas as pl
from jax.experimental.pallas import tpu as pltpu
from jax.sharding import PartitionSpec as P

HEAD = 64
BLOCK = 16
EPSILON = 1e-05
MASKED = -1e30
LANES = 128
LINE = 4
EXTRA = 16
F32 = jnp.float32
BF16 = jnp.bfloat16
PART, NEAR, CORE, LEAD, FIRST, HIGH = range(6)


def dot(left, right):
    return lax.dot_general(left, right, (((1,), (0,)), ((), ())), preferred_element_type=F32)


def dot_cols(left, right):
    return lax.dot_general(left, right, (((1,), (1,)), ((), ())), preferred_element_type=F32)


def dot_rows(left, right):
    return lax.dot_general(left, right, (((0,), (0,)), ((), ())), preferred_element_type=F32)


def normalized(values):
    mean = jnp.mean(values, axis=-1, keepdims=True)
    centered = values - mean
    spread = jnp.mean(centered * centered, axis=-1, keepdims=True)
    rstd = lax.rsqrt(spread + EPSILON)
    return centered * rstd, rstd


def norm_backward(values, gain, upstream, grad_normed):
    xhat, rstd = normalized(values)
    scaled = grad_normed * gain
    mean = jnp.mean(scaled, axis=-1, keepdims=True)
    along = jnp.mean(scaled * xhat, axis=-1, keepdims=True)
    grad_gain = jnp.sum(grad_normed * xhat, axis=0, keepdims=True)
    grad = upstream.astype(F32) + rstd * (scaled - mean - xhat * along)
    return grad.astype(BF16), grad_gain


def joined(own, other):
    return jnp.concatenate([a[...].astype(F32) + b[...].astype(F32) for a, b in zip(own, other)], axis=0)


def where():
    section, replica = lax.axis_index("section"), lax.axis_index("dp")
    part, core, z = section % 2, replica % 2, replica // 2
    lead = (part == core).astype(jnp.int32)
    first = (section < 2).astype(jnp.int32)
    return part, z % 2, core, lead, first, z // 2 % 2


def scatter(value, pieces):
    rows = pieces[0].shape[0]
    for index, piece in enumerate(pieces):
        piece[...] = value[index * rows : (index + 1) * rows].astype(BF16)


def lanes_of(spot, half):
    return pl.ds(pl.multiple_of(spot[CORE] * half, LANES), half)


def swap_halves(block):
    lane = lax.broadcasted_iota(jnp.int32, block.shape, 1)
    low = lax.rem(lane, HEAD) < HEAD // 2
    ahead = pltpu.roll(block, LANES - HEAD // 2, 1)
    behind = pltpu.roll(block, HEAD // 2, 1)
    return jnp.where(low, ahead, behind)


def stacked(pair):
    lane = lax.broadcasted_iota(jnp.int32, pair.shape, 1)
    zero = jnp.zeros_like(pair)
    return jnp.concatenate(
        [jnp.where(lane < HEAD, pair, zero), jnp.where(lane < HEAD, zero, pair)], axis=0
    )


def merged(stack, rows):
    lane = lax.broadcasted_iota(jnp.int32, (rows, LANES), 1)
    return jnp.where(lane < HEAD, stack[:rows], stack[rows:])


def visible(table, at, rows, total):
    clean = table[at : at + rows, 2 * LANES : 2 * LANES + 1]
    noisy = table[at : at + rows, 2 * LANES + 1 : 2 * LANES + 2]
    low, high, same = [table[total + i : total + i + 1, at : at + rows] for i in range(3)]
    return ((clean >= low) & (clean <= high)) | (noisy == same)


VECTOR = pl.BlockSpec(memory_space=pltpu.VMEM)
ANYWHERE = pl.BlockSpec(memory_space=pl.ANY)


def call(kernel, args, outs, scratch=(), name=None, held=()):
    count = len(args)

    def wrapped(*refs):
        kernel(*refs[:count], *refs[count + len(held) :])

    return pl.pallas_call(
        wrapped,
        out_shape=[jax.ShapeDtypeStruct(shape, dtype) for shape, dtype in outs],
        in_specs=[VECTOR] * (count + len(held)),
        out_specs=[VECTOR] * len(outs),
        scratch_shapes=list(scratch),
        compiler_params=pltpu.CompilerParams(vmem_limit_bytes=8 * 1024 * 1024),
        name=name,
    )(*args, *held)


GAIN_ATTN, GAIN_FEED, DOWN_SHIFT, SHIFT = range(4)


def cut_kernel(places, *refs):
    spot = where()
    count = len(places)
    refs = refs[1:]
    arrays, outs, sems = refs[: -count - 1], refs[-count - 1 : -1], refs[-1]
    copies = []
    for index, (number, place) in enumerate(places):
        row, column = place(spot)
        rows, columns = outs[index].shape
        lines = pl.ds(pl.multiple_of(row, 16), rows)
        lanes = pl.ds(pl.multiple_of(column, LANES), columns)
        copies.append(
            pltpu.make_async_copy(arrays[number].at[0, lines, lanes], outs[index], sems.at[index])
        )
    for copy in copies:
        copy.start()
    for copy in copies:
        copy.wait()


def cut(before, arrays, places, shapes, name):
    before = arrays[0] if before is None else before
    return pl.pallas_call(
        lambda *refs: cut_kernel(places, *refs),
        out_shape=[jax.ShapeDtypeStruct(shape, BF16) for shape in shapes],
        in_specs=[ANYWHERE] * (1 + len(arrays)),
        out_specs=[VECTOR] * len(shapes),
        scratch_shapes=[pltpu.SemaphoreType.DMA((len(shapes),))],
        compiler_params=pltpu.CompilerParams(vmem_limit_bytes=8 * 1024 * 1024),
        name=name,
    )(before, *arrays)


def table_kernel(micro, mine, theirs, turns, out):
    total = out.shape[0] - 8
    rows = total // micro
    half = rows // 2
    span = half // BLOCK + 1
    lead = where()[LEAD] == 1

    def layout(item, shape, axis):
        place = lax.broadcasted_iota(jnp.int32, shape, axis)
        clean = place >= half
        within = jnp.where(clean, place - half, place)
        document, begin = jnp.zeros(shape, jnp.int32), jnp.zeros(shape, jnp.int32)
        end = jnp.int32(0)
        for j in range(mine.shape[1]):
            length = jnp.where(lead, mine[item, j], theirs[item, j])
            end = end + length
            passed = (within >= end).astype(jnp.int32)
            document = document + passed
            begin = begin + passed * length
        offset = within - begin
        return clean, offset, document * span, document * span + offset // BLOCK

    for item in range(micro):
        at = pl.ds(item * rows, rows)
        clean, offset, _, block = layout(item, (rows, LANES), 0)
        lane = lax.broadcasted_iota(jnp.int32, (rows, LANES), 1)
        chosen = (offset[:, :half] == lane[:, :half]).astype(F32)
        out[at, : 2 * LANES] = lax.dot_general(
            chosen,
            turns[...],
            (((1,), (0,)), ((), ())),
            precision=lax.Precision.HIGHEST,
            preferred_element_type=F32,
        )
        codes = jnp.where(clean == (lane == 0), block, -2)
        out[at, 2 * LANES : 3 * LANES] = codes.astype(F32)
        clean, _, low, block = layout(item, (8, rows), 1)
        row = lax.broadcasted_iota(jnp.int32, (8, rows), 0)
        high, same = jnp.where(clean, block, block - 1), jnp.where(clean, -1, block)
        out[total:, at] = jnp.where(row == 0, low, jnp.where(row == 1, high, same)).astype(F32)


def attend_kernel(micro, keep, arrived, *refs):
    if arrived:
        mine, theirs, before, *refs = refs
    else:
        mine, theirs, *refs = refs
    params, table, *refs = refs
    spot = where()
    held, refs = refs[:4], refs[4:]
    partial, stream, refs = refs[:micro], refs[micro], refs[micro + 1 :]
    if keep:
        normed_out, q, k, v, mixed, chance, pay = refs
    else:
        q, k, v, mixed = refs
    total, width = stream.shape
    half = width // 2
    rows = total // micro
    if arrived:
        low = jnp.where(spot[CORE] == 0, mine[...], theirs[...])
        high = jnp.where(spot[CORE] == 0, theirs[...], mine[...])
        x = jnp.where(spot[FIRST] == 1, before[...], jnp.concatenate([low, high], axis=1))
    else:
        x = jnp.where(spot[LEAD] == 1, mine[...], theirs[...])
    stream[...] = x
    xhat, _ = normalized(x.astype(F32))
    normed = (xhat * params[GAIN_ATTN : GAIN_ATTN + 1, :width]).astype(BF16)
    if keep:
        normed_out[...] = normed
    v[...] = dot(normed, held[2][...]).astype(BF16)
    cos, sin = table[:total, :LANES], table[:total, LANES : 2 * LANES]
    for index, target in ((0, q), (1, k)):
        wide = dot(normed, held[index][...])
        for at in range(0, half, LANES):
            block = wide[:, at : at + LANES]
            target[:, at : at + LANES] = (block * cos + swap_halves(block) * sin).astype(BF16)
    for item in range(micro):
        place = pl.ds(item * rows, rows)
        mask = visible(table, item * rows, rows, total)
        mask = jnp.concatenate([mask, mask], axis=1)
        for pair in range(half // LANES):
            lanes = pl.ds(pair * LANES, LANES)
            scores = dot_cols(k[place, lanes], stacked(q[place, lanes])) * HEAD ** (-0.5)
            scores = jnp.where(mask, scores, MASKED)
            peak = jnp.max(scores, axis=0, keepdims=True)
            powers = jnp.exp(scores - peak)
            weights = powers / jnp.sum(powers, axis=0, keepdims=True)
            if keep:
                chance[item * (half // LANES) + pair] = weights
            result = dot_rows(weights.astype(BF16), v[place, lanes])
            mixed[place, lanes] = merged(result, rows).astype(BF16)
    scatter(dot_cols(mixed[...], held[3][...]), partial)
    if keep:
        pay[:, :half] = normed_out[:, lanes_of(spot, half)]
        pay[:, half:] = mixed[...]


def feed_up(x, own, other, params, held, stream, normed_out, active, slope):
    width = x.shape[1]
    result = (x[...].astype(F32) + joined(own, other)).astype(BF16)
    stream[...] = result
    xhat, _ = normalized(result.astype(F32))
    normed = (xhat * params[GAIN_FEED : GAIN_FEED + 1, :width]).astype(BF16)
    normed_out[...] = normed
    scale = (2.0 / jnp.pi) ** 0.5
    piece = 2 * LANES
    for index in (0, 1):
        for at in range(0, width, piece):
            wide = pl.ds(index * width + at, piece)
            lanes = pl.ds(at, piece)
            if index == 0 or len(held) == 2:
                before = dot(normed, held[index][:, lanes])
            else:
                first, second = ends(where(), width, width // 2)
                before = dot(normed_out[:, first], held[1][:, lanes])
                before += dot(normed_out[:, second], held[2][:, lanes])
            before = before + params[SHIFT : SHIFT + 1, wide]
            square = before * before
            bend = jnp.tanh(scale * before * (1.0 + 0.044715 * square))
            active[index][:, at : at + piece] = (0.5 * before * (1.0 + bend)).astype(BF16)
            if slope is not None:
                inner = scale * (1.0 + 3 * 0.044715 * square)
                tilt = 0.5 * (1.0 + bend) + 0.5 * before * (1.0 - bend * bend) * inner
                slope[:, wide] = tilt.astype(BF16)


def feed_up_kernel(micro, x, *refs):
    own, other, refs = refs[:micro], refs[micro : 2 * micro], refs[2 * micro :]
    params, up_mine, up_near, up_next, down_mine, stream, theirs, total, mine, normed = refs
    ups = (up_mine, up_near, up_next)
    feed_up(x, own, other, params, ups, stream, normed, (mine, theirs), None)
    total[...] = dot(mine[...], down_mine[...])


def ends(spot, width, size):
    return [pl.ds(pl.multiple_of(at * (width - size), LANES), size) for at in (spot[NEAR], 1 - spot[NEAR])]


def feed_down_kernel(total, theirs, near, middle, following, *partial):
    size, width = near.shape
    first, second = ends(where(), width, size)
    result = total[...] + dot(theirs[:, size : width - size], middle[...])
    result += dot(theirs[:, first], near[...]) + dot(theirs[:, second], following[...])
    scatter(result, partial)


def feed_kernel(micro, x, *refs):
    own, other, refs = refs[:micro], refs[micro : 2 * micro], refs[2 * micro :]
    params, up_mine, up_theirs, down_mine, down_theirs, *refs = refs
    spot = where()
    partial, refs = refs[:micro], refs[micro:]
    stream, normed, mine, slope, pay, theirs = refs
    width = x.shape[1]
    half = width // 2
    feed_up(x, own, other, params, (up_mine, up_theirs), stream, normed, (mine, theirs), slope)
    scatter(dot(mine[...], down_mine[...]) + dot(theirs[...], down_theirs[...]), partial)
    lanes = lanes_of(spot, half)
    pay[:, :half] = normed[:, lanes]
    pay[:, half:] = theirs[...]


def finish_kernel(micro, stream, *refs):
    own, other, refs = refs[:micro], refs[micro : 2 * micro], refs[2 * micro :]
    params, part, result = refs
    spot = where()
    width = stream.shape[1]
    shift = params[DOWN_SHIFT : DOWN_SHIFT + 1, :width]
    result[...] = (stream[...].astype(F32) + (joined(own, other) + shift)).astype(BF16)
    part[...] = result[:, lanes_of(spot, part.shape[1])]


def last_kernel(micro, stream, *refs):
    own, other, refs = refs[:micro], refs[micro : 2 * micro], refs[2 * micro :]
    params, mine, theirs = refs
    spot = where()
    width = stream.shape[1]
    shift = params[DOWN_SHIFT : DOWN_SHIFT + 1, :width]
    middle = stream[...]
    result = (middle.astype(F32) + (joined(own, other) + shift)).astype(BF16)
    mine[...] = jnp.where(spot[PART] == 0, middle, result)
    theirs[...] = jnp.where(spot[PART] == 0, result, middle)


def feed_back_kernel(micro, arrived, *refs):
    if arrived:
        half_mine, half_theirs, *refs = refs
    else:
        whole_mine, whole_theirs, *refs = refs
    slope, up_mine, up_theirs, down_mine, down_theirs, *refs = refs
    spot = where()
    partial, upstream, refs = refs[:micro], refs[micro], refs[micro + 1 :]
    if arrived:
        mine, theirs, sums = refs
    else:
        mine, theirs = refs
    rows, width = upstream.shape
    if arrived:
        low = jnp.where(spot[CORE] == 0, half_mine[...], half_theirs[...])
        high = jnp.where(spot[CORE] == 0, half_theirs[...], half_mine[...])
        dz = jnp.concatenate([low, high], axis=1)
        sums[2:3, :] = jnp.sum(dz.astype(F32), axis=0, keepdims=True)
        sums[3:, :] = jnp.zeros((sums.shape[0] - 3, width), F32)
    else:
        dz = jnp.where(spot[LEAD] == 1, whole_mine[...], whole_theirs[...])
    upstream[...] = dz
    piece = 2 * LANES
    for index, (down, back) in enumerate(((down_mine, mine), (down_theirs, theirs))):
        for at in range(0, width, piece):
            grad = dot_cols(dz, down[at : at + piece, :])
            grad = grad * slope[:, index * width + at : index * width + at + piece].astype(F32)
            rounded = grad.astype(BF16)
            back[:, at : at + piece] = rounded
            if arrived:
                sums[index : index + 1, at : at + piece] = jnp.sum(
                    rounded.astype(F32), axis=0, keepdims=True
                )
    scatter(dot_cols(mine[...], up_mine[...]) + dot_cols(theirs[...], up_theirs[...]), partial)


def attend_back_kernel(micro, keep, dz, *refs):
    own, other, refs = refs[:micro], refs[micro : 2 * micro], refs[2 * micro :]
    x, params, chance, v, k, q, mixed, table, *refs = refs
    spot = where()
    held, refs = refs[:4], refs[4:]
    given = micro + 2 if keep else micro
    partial, refs = refs[:given], refs[given:]
    grad, *refs = refs
    if keep:
        vector, rhs_a, rhs_b, pay_a, pay_b, *refs = refs
        stream, sums, *partial = partial
    dq, dk, dv, dmixed = refs
    total, width = x.shape
    half = width // 2
    rows = total // micro
    gain = params[GAIN_FEED : GAIN_FEED + 1, :width]
    result, gain_sum = norm_backward(x[...].astype(F32), gain, dz[...], joined(own, other))
    grad[...] = result
    dmixed[...] = dot(result, held[3][...]).astype(BF16)
    for item in range(micro):
        place = pl.ds(item * rows, rows)
        turn = table[item * rows : (item + 1) * rows, :LANES]
        tilt = table[item * rows : (item + 1) * rows, LANES : 2 * LANES]
        for pair in range(half // LANES):
            lanes = pl.ds(pair * LANES, LANES)
            weights = chance[item * (half // LANES) + pair]
            grads = stacked(dmixed[place, lanes])
            queries = stacked(q[place, lanes])
            dv[place, lanes] = dot(weights.astype(BF16), grads).astype(BF16)
            spread = dot_cols(v[place, lanes], grads)
            inner = jnp.sum(weights * spread, axis=0, keepdims=True)
            scores = (weights * (spread - inner)).astype(BF16)
            query_grad = merged(dot_rows(scores, k[place, lanes]), rows) * HEAD ** (-0.5)
            key_grad = dot(scores, queries) * HEAD ** (-0.5)
            dq[place, lanes] = (query_grad * turn - swap_halves(query_grad) * tilt).astype(BF16)
            dk[place, lanes] = (key_grad * turn - swap_halves(key_grad) * tilt).astype(BF16)
    if keep:
        even = spot[PART] == 0
        rhs_a[...] = jnp.where(even, dq[...], dv[...])
        rhs_b[...] = jnp.where(even, dk[...], mixed[...])
        pay_a[...] = jnp.where(even, dv[...], dq[...])
        pay_b[:total] = jnp.where(even, grad[:, lanes_of(spot, half)], dk[...])
    back = dot_cols(dq[...], held[0][...]) + dot_cols(dk[...], held[1][...])
    back += dot_cols(dv[...], held[2][...])
    scatter(back, partial)
    if keep:
        xhat, _ = normalized(stream[...].astype(F32))
        attn_gain = jnp.sum(back * xhat, axis=0, keepdims=True)
        zero = jnp.zeros((1, half), F32)
        alone = spot[CORE] == 0
        feed_gain = jnp.where(alone, gain_sum, 0.0)
        low = jnp.where(alone, sums[2:3, :half], zero)
        high = jnp.where(alone, sums[2:3, half:], zero)
        mine = (sums[0:1, :], jnp.where(even, low, high), jnp.where(even, attn_gain, feed_gain))
        theirs = (sums[1:2, :], jnp.where(even, high, low), jnp.where(even, feed_gain, attn_gain))
        vector[...] = rows_of(split(mine), half)
        wide = rows_of(split(theirs), half)
        above = wide.astype(BF16)
        pay_b[total : total + EXTRA] = above
        pay_b[total + EXTRA :] = (wide - above.astype(F32)).astype(BF16)


def split(vectors):
    units, features, gain = vectors
    half = features.shape[1]
    return units[:, :half], units[:, half:], features, gain[:, :half], gain[:, half:]


def rows_of(vectors, width):
    rows = [jnp.pad(x, ((0, 0), (0, width - x.shape[1]))) for x in vectors]
    return jnp.concatenate(rows + [jnp.zeros((EXTRA - len(rows), width), F32)], axis=0)


def norm_back_kernel(micro, dz, *refs):
    own, other, refs = refs[:micro], refs[micro : 2 * micro], refs[2 * micro :]
    x, params, grad, part = refs
    spot = where()
    gain = params[GAIN_ATTN : GAIN_ATTN + 1, : x.shape[1]]
    result, _ = norm_backward(x[...].astype(F32), gain, dz[...], joined(own, other))
    grad[...] = result
    part[...] = grad[:, lanes_of(spot, part.shape[1])]


def norm_end_kernel(micro, dz, *refs):
    own, other, refs = refs[:micro], refs[micro : 2 * micro], refs[2 * micro :]
    x, params, mine, theirs = refs
    spot = where()
    gain = params[GAIN_ATTN : GAIN_ATTN + 1, : x.shape[1]]
    upstream = dz[...]
    result, _ = norm_backward(x[...].astype(F32), gain, upstream, joined(own, other))
    even = spot[PART] == 0
    mine[...] = jnp.where(even, result, upstream)
    theirs[...] = jnp.where(even, upstream, result)


def halves(spot, size):
    return [(pl.ds(pl.multiple_of(at * size, LANES), size), at) for at in (spot[CORE], 1 - spot[CORE])]


def deal(grad, half, spot, kept, given):
    pairs, size = kept.shape[0], kept.shape[1]
    for i in range(pairs // 2):
        low = grad[2 * i * size : (2 * i + 1) * size]
        high = grad[(2 * i + 1) * size : (2 * i + 2) * size]
        place = half * (pairs // 2) + i
        kept[place] = jnp.where(spot[NEAR] == 0, low, high).astype(BF16)
        given[place] = jnp.where(spot[NEAR] == 0, high, low).astype(BF16)


def down_weight_kernel(near, near_other, far, far_other, dz, far_dz, *outs):
    spot = where()
    width = near.shape[1]
    at = far.shape[1] - width
    lefts = ((near, far), (near_other, far_other))
    for (left, far_left), (_, half) in zip(lefts, halves(spot, width)):
        grad = dot_rows(left[...], dz[...]) + dot_rows(far_left[:, at:], far_dz[...])
        deal(grad, half, spot, *outs)


def up_weight_kernel(near, far, far_other, back, far_back, kept, given):
    spot = where()
    size = near.shape[1] // 2
    for left, (lines, half) in zip((far, far_other), halves(spot, size)):
        grad = dot_rows(near[:, lines], back[...]) + dot_rows(left[:, :size], far_back[...])
        deal(grad, half, spot, kept, given)


def attend_weight_a_kernel(near, far, far_other, right, far_right, kept, given):
    spot = where()
    size = near.shape[1] // 2
    for left, (lines, half) in zip((far, far_other), halves(spot, size)):
        grad = dot_rows(near[:, lines], right[...]) + dot_rows(left[:, :size], far_right[...])
        deal(grad, half, spot, kept, given)


def attend_weight_b_kernel(
    near, grad_in, far, far_other, right, far_right, far_right_other, vector, kept, given
):
    spot = where()
    size = near.shape[1] // 2
    rows = near.shape[0]
    below = kept.shape[1] - EXTRA
    even = spot[PART] == 0
    rights = jnp.where(even, far_right[:rows], far[:, size:])
    lefts = ((far, far_right), (far_other, far_right_other))
    for (left, back), (lines, half) in zip(lefts, halves(spot, size)):
        grad = dot_rows(jnp.where(even, near[:, lines], grad_in[:, lines]), right[...])
        grad += dot_rows(jnp.where(even, left[:, :size], back[:rows]), rights)
        deal(grad, half, spot, kept.at[:, :below], given.at[:, :below])
    total = vector[...] + far_right[rows : rows + EXTRA].astype(F32) + far_right[rows + EXTRA :].astype(F32)
    chips = 2 * kept.shape[0]
    parts = []
    for chip in range(chips):
        lines = []
        for row, extent in ((0, 4 * size), (2, size), (3, 2 * size)):
            each = extent // chips
            at = chip * each
            mine = spot[CORE] == at // (2 * size)
            if row == 0:
                at %= 2 * size
            piece = total[row + at // size : row + at // size + 1, at % size : at % size + each]
            lines.append(jnp.where(mine, piece, 0.0) if row == 0 else piece)
        parts.append(rows_of(lines, size))
    for i in range(chips // 2):
        low, high = parts[2 * i], parts[2 * i + 1]
        kept[i, below:] = jnp.where(spot[NEAR] == 0, low, high).astype(BF16)
        given[i, below:] = jnp.where(spot[NEAR] == 0, high, low).astype(BF16)


def fold_kernel(kept, received, out, given):
    spot = where()
    low = kept[0].astype(F32) + received[0].astype(F32)
    high = kept[1].astype(F32) + received[1].astype(F32)
    out[0] = jnp.where(spot[HIGH] == 0, low, high)
    given[0] = jnp.where(spot[HIGH] == 0, high, low).astype(BF16)


def close_kernel(extra, kept, received, out, given):
    spot = where()
    size = out.shape[0] - extra
    total = kept[0] + received[0].astype(F32)
    low, high = total[:size], total[size : 2 * size]
    out[:size] = jnp.where(spot[CORE] == 0, low, high)
    given[:size] = jnp.where(spot[CORE] == 0, high, low)
    if extra:
        out[size:] = total[2 * size :]
        given[size:] = total[2 * size :]


def attend_out_kernel(mine_a, theirs_a, mine, theirs, out, units, features, gain):
    first = where()[CORE] == 0
    size, half = mine_a.shape
    for at, own, other in ((0, mine_a[...], theirs_a[...]), (2 * half, mine[:size], theirs[:size])):
        out[:, at : at + half] = jnp.where(first, own, other)
        out[:, at + half : at + 2 * half] = jnp.where(first, other, own)
    total = mine[size:] + theirs[size:]
    for row, x in enumerate((units, features, gain)):
        each = x.shape[1]
        x[...] = jnp.where(first, total[row : row + 1, :each], total[row : row + 1, each : 2 * each])


def swap_section(x):
    return lax.ppermute(x, "section", [(i, i ^ 1) for i in range(lax.axis_size("section"))])


def swap_layer(x):
    return lax.ppermute(x, "section", [(i, i ^ 2) for i in range(lax.axis_size("section"))])


def swap_core(x):
    return lax.ppermute(x, "dp", [(i, i ^ 1) for i in range(lax.axis_size("dp"))])


def swap_chip(x, distance):
    return lax.ppermute(x, "dp", [(i, i ^ (2 * distance)) for i in range(lax.axis_size("dp"))])


def after(x, *others):
    return lax.optimization_barrier((x,) + others)[0]


def replica_sum(kept, given, z, chips):
    if chips > LINE:
        pair = jnp.where(z % 2 == 0, jnp.stack([kept, given], 1), jnp.stack([given, kept], 1))
        groups = [[2 * i + c for i in range(chips)] for c in (0, 1)]
        return lax.psum_scatter(
            pair.reshape(chips, *kept.shape[1:]),
            "dp",
            scatter_dimension=0,
            axis_index_groups=groups,
            tiled=False,
        ).astype(F32)
    distance = 1
    while True:
        total = kept.astype(F32) + swap_chip(given, distance).astype(F32)
        if total.shape[0] == 1:
            return total[0]
        distance *= 2
        bit = z // distance % 2
        pairs = total.reshape(total.shape[0] // 2, 2, *total.shape[1:])
        given = lax.dynamic_index_in_dim(pairs, 1 - bit, 1, keepdims=False).astype(given.dtype)
        kept = lax.dynamic_index_in_dim(pairs, bit, 1, keepdims=False)


def rotations(places):
    count = HEAD // 2
    freq = np.power(10000.0, -2.0 * np.arange(count, dtype=np.float32) / HEAD).astype(np.float32)
    angle = np.arange(places, dtype=np.float32)[:, None] * freq[None, :]
    cosine, sine = np.cos(angle), np.sin(angle)
    parts = [cosine] * (LANES // count) + [-sine, sine] * (LANES // HEAD)
    return jnp.asarray(np.concatenate(parts, axis=1).astype(np.float32))


def body(
    hidden_in,
    cotangent,
    doc_lengths,
    attn_weight,
    up_weight,
    down_weight,
    up_bias,
    down_bias,
    norm_gain,
):
    section = lax.axis_index("section")
    replica = lax.axis_index("dp")
    chips = lax.axis_size("dp") // 2
    part, layer = section % 2, section // 2
    core, z = replica % 2, replica // 2
    near = z % 2
    even, lead, first = part == 0, core == part, layer == 0
    micro, rows, width = hidden_in.shape[1:]
    total, half = micro * rows, width // 2
    hidden = up_weight.shape[2]
    blocks = micro * (half // LANES)

    def columns(x, at, size):
        return lax.dynamic_slice_in_dim(x, at, size, axis=1)

    def by_part(mine, theirs, axis):
        return jnp.where(
            even, jnp.concatenate([mine, theirs], axis), jnp.concatenate([theirs, mine], axis)
        )

    def by_core(mine, theirs, axis):
        return jnp.where(
            core == 0, jnp.concatenate([mine, theirs], axis), jnp.concatenate([theirs, mine], axis)
        )

    wide, narrow = ((total, width), BF16), ((total, half), BF16)
    pieces = [((rows, width), BF16)] * micro
    vectors = ((8, width), F32)

    shift_mine = lax.dynamic_slice_in_dim(up_bias[0], core * width, width, axis=0).astype(F32)
    small = jnp.concatenate([shift_mine, down_bias[0].astype(F32), norm_gain[0]])
    def given(at, array, place, shape, name):
        return cut(at, (array,), [(0, place)], [shape], name)[0]

    attn_given = given(
        None,
        attn_weight,
        lambda spot: (0, spot[NEAR] * width + spot[CORE] * half),
        (width, half),
        "cut_attn",
    )
    up_given = given(
        attn_given,
        up_weight,
        lambda spot: (spot[NEAR] * half, spot[CORE] * width),
        (half, width),
        "cut_up",
    )
    attn_near, up_near = swap_section(attn_given), swap_section(up_given)
    hidden_in, cotangent, doc_lengths, small = lax.optimization_barrier(
        (hidden_in, cotangent, doc_lengths, small, up_given)
    )[:4]
    hidden_in, cotangent = hidden_in.reshape(wide[0]), cotangent.reshape(wide[0])
    hidden_other, lengths_other = swap_core((hidden_in, doc_lengths[0]))
    middle_rows = width - 2 * LANES
    down_end, down_given = cut(
        after(hidden_other, small),
        (down_weight,),
        [
            (0, lambda spot: (spot[CORE] * width + spot[NEAR] * (width - LANES), 0)),
            (0, lambda spot: (spot[CORE] * width + LANES, 0)),
        ],
        [(LANES, width), (middle_rows, width)],
        "cut_down",
    )
    down_near, down_middle = swap_section(down_end), swap_section(down_given)
    attn_next, up_next = swap_chip(attn_near, 1), swap_chip(up_near, 1)
    attn_own = cut(
        up_given,
        (attn_weight,),
        [(0, lambda spot, i=i: (0, i * width + spot[CORE] * half)) for i in (0, 1)],
        [(width, half)] * 2,
        "cut_own",
    )
    feed_own = cut(
        down_end,
        (up_weight, down_weight),
        [(0, lambda spot: (0, spot[CORE] * width)), (1, lambda spot: (spot[CORE] * width, 0))],
        [(width, width)] * 2,
        "cut_feed",
    )
    small_theirs = after(swap_section(small), attn_next)
    scalars = pl.BlockSpec(memory_space=pltpu.SMEM)
    table = pl.pallas_call(
        lambda *refs: table_kernel(micro, *refs),
        out_shape=jax.ShapeDtypeStruct((total + 8, max(3 * LANES, total)), F32),
        in_specs=[scalars, scalars, VECTOR],
        out_specs=VECTOR,
        compiler_params=pltpu.CompilerParams(vmem_limit_bytes=8 * 1024 * 1024),
        name="table",
    )(after(doc_lengths[0], attn_near), lengths_other, rotations(rows // 2))
    down_shift = by_part(small[width : width + half], small_theirs[width : width + half], 0)
    gains = [jnp.pad(x[width + half :], (0, width)) for x in (small, small_theirs)]
    params = jnp.stack(
        [
            jnp.where(even, gains[0], gains[1]),
            jnp.where(even, gains[1], gains[0]),
            jnp.pad(down_shift, (0, width)),
            jnp.concatenate([shift_mine, small_theirs[:width]]),
        ]
    )
    params = jnp.pad(params, ((0, 4), (0, 0)))

    def ordered(mine, theirs, *between):
        low, high = jnp.where(near == 0, mine, theirs), jnp.where(near == 0, theirs, mine)
        return jnp.concatenate([low, *between, high], axis=0)

    low, high = jnp.where(near == 0, attn_near, attn_next), jnp.where(near == 0, attn_next, attn_near)
    attn = (
        jnp.where(even, attn_own[0], low),
        jnp.where(even, attn_own[1], high),
        jnp.where(even, low, attn_own[0]),
        jnp.where(even, high, attn_own[1]),
    )

    def attend(streams, keep):
        arrived = len(streams) == 3
        outs, scratch = pieces + [wide], [pltpu.VMEM(*narrow)] * 4
        if keep:
            outs, scratch = outs + [wide] + [narrow] * 4 + [((blocks, rows, 2 * rows), F32), wide], ()
        out = call(
            lambda *refs: attend_kernel(micro, keep, arrived, *refs),
            (*streams, params, table, *attn),
            outs,
            scratch,
            "attend",
        )
        return out[:micro], out[micro:]

    own_part, (stream_0,) = attend((hidden_in, hidden_other), False)
    down_next = swap_chip(after(down_near, own_part[0]), 1)
    middle, *active = call(
        lambda *refs: feed_up_kernel(micro, *refs),
        (
            stream_0,
            *own_part,
            *swap_core(own_part),
            params,
            feed_own[0],
            up_near,
            up_next,
            feed_own[1],
        ),
        [wide] * 2 + [(wide[0], F32)],
        [pltpu.VMEM(*wide)] * 2,
        name="feed_up",
    )
    own_part = call(
        feed_down_kernel, (active[1], active[0], down_near, down_middle, down_next), pieces, name="feed_down"
    )
    arrived = call(
        lambda *refs: finish_kernel(micro, *refs),
        (middle, *own_part, *swap_core(own_part), params),
        [narrow],
        [pltpu.VMEM(*wide)],
        "finish",
    )[0]
    ups = (feed_own[0], ordered(after(up_near, arrived), up_next))
    downs = (feed_own[1], ordered(after(down_near, arrived), down_next, down_middle))
    arrived = after(swap_layer(arrived), ups[1], downs[1])
    own_part, kept = attend((arrived, swap_core(arrived), stream_0), True)
    stream, normed_attn, q, k, v, mixed, chance, pay_attn = kept
    far_attn = swap_section(pay_attn)
    out = call(
        lambda *refs: feed_kernel(micro, *refs),
        (stream, *own_part, *swap_core(own_part), params, *ups, *downs),
        pieces + [wide] * 3 + [((total, 2 * width), BF16), ((total, width + half), BF16)],
        [pltpu.VMEM(*wide)],
        "feed",
    )
    fed, (middle, normed_feed, active_mine, slope, pay) = out[:micro], out[micro:]
    far = swap_section(pay)

    def feed_back(upstreams, arrived, held=()):
        outs, scratch = pieces + [wide], [pltpu.VMEM(*wide)] * 2
        if arrived:
            outs, scratch = outs + [wide, wide, vectors], ()
        out = call(
            lambda *refs: feed_back_kernel(micro, arrived, *refs),
            (*upstreams, slope, *ups, *downs),
            outs,
            scratch,
            "feed_back",
            held,
        )
        return out[:micro], out[micro:]

    def attend_back(upstream, own, other, params, keep, held=()):
        outs = pieces + [wide]
        more = ()
        if keep:
            outs += [((EXTRA, half), F32)] + [narrow] * 3 + [((total + 2 * EXTRA, half), BF16)]
            more = keep
        out = call(
            lambda *refs: attend_back_kernel(micro, bool(keep), *refs),
            (upstream, *own, *other, middle, params, chance, v, k, q, mixed, table, *attn, *more),
            outs,
            [pltpu.VMEM(*narrow)] * 4,
            "attend_back",
            held,
        )
        return out[:micro], out[micro:]

    kept_on = (slope, *fed)
    cotangent_other = swap_core(after(cotangent, arrived))
    own_part, (upstream_0,) = feed_back((cotangent, cotangent_other), False, kept_on)
    own_part, (grad,) = attend_back(
        upstream_0, own_part, swap_core(own_part), params, (), kept_on
    )
    *own_part, far_attn = lax.optimization_barrier((*own_part, far_attn))
    grad_2, arrived = call(
        lambda *refs: norm_back_kernel(micro, *refs),
        (grad, *own_part, *swap_core(own_part), stream, params),
        [wide, narrow],
        name="norm_back",
        held=kept_on,
    )
    arrived = swap_layer(arrived)
    upstream_half = after(columns(upstream_0, core * half, half), grad_2)

    def weight(kernel, args, shape, name, extra=0):
        outs = [((chips // 2, shape[0] // chips + extra, shape[1]), BF16)] * 2
        return call(kernel, args, outs, name=name)

    def folded(grad, token):
        kept, given = grad
        if chips != LINE:
            return replica_sum(kept, given, z, chips)
        received = after(swap_chip(given, 1), token)
        part = (1, *kept.shape[1:])
        return call(fold_kernel, (kept, received), [(part, F32), (part, BF16)], name="fold")

    def closed(fold, token, extra=0):
        if chips != LINE:
            size = (fold.shape[0] - extra) // 2
            mine = lax.dynamic_slice_in_dim(fold, core * size, size, axis=0)
            theirs = lax.dynamic_slice_in_dim(fold, (1 - core) * size, size, axis=0)
            mine, theirs = [jnp.concatenate([x, fold[2 * size :]], axis=0) for x in (mine, theirs)]
            return mine, swap_core(theirs)
        kept, given = fold
        received = after(swap_chip(given, 2), token)
        part = (((kept.shape[-2] + extra) // 2, kept.shape[-1]), F32)
        mine, theirs = call(
            lambda *refs: close_kernel(extra, *refs), (kept, received), [part] * 2, name="close"
        )
        return mine, swap_core(theirs)

    x = types.SimpleNamespace(far=far, far_attn=far_attn)

    def take_upstream(token):
        x.half = jnp.where(first, after(arrived, token), upstream_half)
        x.half_other, x.far_half = swap_core(x.half), swap_section(x.half)
        return x.half

    def take_far(token):
        x.far = after(x.far, token)
        x.far_other = swap_core(x.far)
        return x.far

    def send_active(token):
        x.active_other = swap_core(after(active_mine, token))
        return token

    def feed_step(token):
        x.part, back = feed_back((after(x.half, token), x.half_other), True)
        x.upstream, x.back, theirs, x.sums = back
        x.far_back, x.part_other = swap_section(theirs), swap_core(x.part)
        return x.upstream

    def take_attn(token):
        x.far_attn = after(x.far_attn, token)
        return x.far_attn

    def attend_step(token):
        part, other = x.part, x.part_other
        x.part, back = attend_back(x.upstream, part, other, after(params, token), (stream, x.sums))
        x.grad, x.vector, x.rhs_a, x.rhs_b, pay_a, pay_b = back
        x.far_rhs_a, x.far_rhs_b = swap_section(pay_a), swap_section(pay_b)
        return x.grad

    def send_attn(token):
        x.far_attn_other = swap_core(after(x.far_attn, token))
        return token

    def take_half(token):
        x.far_half = after(x.far_half, token)
        return x.far_half

    def take_back(token):
        x.far_back = after(x.far_back, token)
        return x.far_back

    def take_rhs_a(token):
        x.far_rhs_a = after(x.far_rhs_a, token)
        return x.far_rhs_a

    def take_rhs_b(token):
        x.far_rhs_b = after(x.far_rhs_b, token)
        x.far_rhs_b_other = swap_core(x.far_rhs_b)
        return x.far_rhs_b

    def down_step(token):
        args = (active_mine, x.active_other, x.far, x.far_other, x.half, after(x.far_half, token))
        x.down = weight(down_weight_kernel, args, (hidden, half), "down_weight")
        return x.down[0]

    def up_step(token):
        args = (normed_feed, x.far, x.far_other, x.back, after(x.far_back, token))
        x.up = weight(up_weight_kernel, args, (width, width), "up_weight")
        return x.up[0]

    def attn_step_a(token):
        args = (normed_attn, x.far_attn, x.far_attn_other, x.rhs_a, after(x.far_rhs_a, token))
        x.attn_a = weight(attend_weight_a_kernel, args, (width, half), "attend_weight_a")
        return x.attn_a[0]

    def attn_step_b(token):
        args = (normed_attn, x.grad, x.far_attn, x.far_attn_other, x.rhs_b)
        args += (after(x.far_rhs_b, token), x.far_rhs_b_other, x.vector)
        x.attn_b = weight(attend_weight_b_kernel, args, (width, half), "attend_weight_b", EXTRA)
        return x.attn_b[0]

    def norm_step(token):
        x.grads, x.grads_given = call(
            lambda *refs: norm_end_kernel(micro, *refs),
            (x.grad, *x.part, *swap_core(x.part), stream, after(params, token)),
            [wide, wide],
            name="norm_end",
        )
        return x.grads

    def send_fed(token):
        x.fed_other = swap_core([after(y, token) for y in fed])
        return token

    def last_step(token):
        x.outputs, x.outputs_given = call(
            lambda *refs: last_kernel(micro, *refs),
            (middle, *fed, *x.fed_other, after(params, token)),
            [wide, wide],
            name="last",
        )
        return x.outputs

    def send_outputs(token):
        x.outputs_far = swap_section(after(x.outputs_given, token))
        return token

    def send_grads(token):
        x.grads_far = swap_section(after(x.grads_given, token))
        return token

    def take_outputs(token):
        x.outputs = jnp.where(lead, x.outputs, after(x.outputs_far, token))
        return x.outputs

    def take_grads(token):
        x.grads = jnp.where(lead, x.grads, after(x.grads_far, token))
        return x.grads

    def down_fold(token):
        x.down = folded(x.down, token)
        return x.down[0]

    def up_fold(token):
        x.up = folded(x.up, token)
        return x.up[0]

    def attn_fold_a(token):
        x.attn_a = folded(x.attn_a, token)
        return x.attn_a[0]

    def attn_fold_b(token):
        x.attn_b = folded(x.attn_b, token)
        return x.attn_b[0]

    def down_close(token):
        x.down = closed(x.down, token)
        return x.down[0]

    def up_close(token):
        x.up = closed(x.up, token)
        return x.up[0]

    def attn_close_a(token):
        x.attn_a = closed(x.attn_a, token)
        return x.attn_a[0]

    def attn_close_b(token):
        x.attn_b = closed(x.attn_b, token, EXTRA)
        return x.attn_b[0]

    token = grad_2
    for step in (
        take_upstream,
        take_far,
        send_active,
        feed_step,
        take_half,
        down_step,
        take_attn,
        attend_step,
        send_attn,
        take_back,
        up_step,
        down_fold,
        norm_step,
        take_rhs_a,
        attn_step_a,
        take_rhs_b,
        attn_step_b,
        send_grads,
        send_fed,
        up_fold,
        attn_fold_a,
        down_close,
        last_step,
        send_outputs,
        attn_fold_b,
        up_close,
        take_grads,
        take_outputs,
        attn_close_a,
        attn_close_b,
    ):
        token = step(token)

    size = width // (2 * chips)
    if chips == LINE:
        attn_out, up_shift_out, down_shift_out, gain_out = call(
            attend_out_kernel,
            (*x.attn_a, *x.attn_b),
            [((size, hidden), F32)] + [((1, y // (2 * chips)), F32) for y in (hidden, half, width)],
            name="attend_out",
        )
    else:
        attn_out = jnp.concatenate(
            [by_core(*x.attn_a, 1), by_core(*[y[:size] for y in x.attn_b], 1)], axis=1
        )
        vector = x.attn_b[0][size:] + x.attn_b[1][size:]
        up_shift_out, down_shift_out, gain_out = [
            columns(vector[i : i + 1], core * (y // (2 * chips)), y // (2 * chips))
            for i, y in enumerate((hidden, half, width))
        ]
    up_out, down_out = by_core(*x.up, 1), by_core(*x.down, 1)

    shape = (1, 1, micro, rows, width)
    return (
        x.outputs.reshape(shape),
        x.grads.reshape(shape),
        attn_out[None],
        up_out[None],
        down_out[None],
        up_shift_out,
        down_shift_out,
        gain_out,
    )


def solution(mesh):
    in_specs = (
        P("dp", None, None, None),
        P("dp", None, None, None),
        P("dp", None, None),
        P("section", None, None),
        P("section", None, None),
        P("section", None, None),
        P("section", None),
        P("section", None),
        P("section", None),
    )
    out_specs = (
        P("section", "dp", None, None, None),
        P("section", "dp", None, None, None),
        P("section", "dp", None),
        P("section", "dp", None),
        P("section", "dp", None),
        P("section", "dp"),
        P("section", "dp"),
        P("section", "dp"),
    )
    return jax.shard_map(body, mesh=mesh, in_specs=in_specs, out_specs=out_specs, check_vma=False)
```

```python
import types

import jax
import jax.numpy as jnp
import numpy as np
from jax import lax
from jax.experimental import pallas as pl
from jax.experimental.pallas import tpu as pltpu
from jax.sharding import PartitionSpec as P

HEAD = 64
BLOCK = 16
EPSILON = 1e-05
MASKED = -1e30
LANES = 128
LINE = 4
EXTRA = 16
F32 = jnp.float32
BF16 = jnp.bfloat16
PART, NEAR, CORE, LEAD, FIRST, HIGH = range(6)


def dot(left, right):
    return lax.dot_general(left, right, (((1,), (0,)), ((), ())), preferred_element_type=F32)


def dot_cols(left, right):
    return lax.dot_general(left, right, (((1,), (1,)), ((), ())), preferred_element_type=F32)


def dot_rows(left, right):
    return lax.dot_general(left, right, (((0,), (0,)), ((), ())), preferred_element_type=F32)


def normalized(values):
    mean = jnp.mean(values, axis=-1, keepdims=True)
    centered = values - mean
    spread = jnp.mean(centered * centered, axis=-1, keepdims=True)
    rstd = lax.rsqrt(spread + EPSILON)
    return centered * rstd, rstd


def norm_backward(values, gain, upstream, grad_normed):
    xhat, rstd = normalized(values)
    scaled = grad_normed * gain
    mean = jnp.mean(scaled, axis=-1, keepdims=True)
    along = jnp.mean(scaled * xhat, axis=-1, keepdims=True)
    grad_gain = jnp.sum(grad_normed * xhat, axis=0, keepdims=True)
    grad = upstream.astype(F32) + rstd * (scaled - mean - xhat * along)
    return grad.astype(BF16), grad_gain


def joined(own, other):
    return jnp.concatenate([a[...].astype(F32) + b[...].astype(F32) for a, b in zip(own, other)], axis=0)


def where():
    section, replica = lax.axis_index("section"), lax.axis_index("dp")
    part, core, z = section % 2, replica % 2, replica // 2
    lead = (part == core).astype(jnp.int32)
    first = (section < 2).astype(jnp.int32)
    return part, z % 2, core, lead, first, z // 2 % 2


def scatter(value, pieces):
    rows = pieces[0].shape[0]
    for index, piece in enumerate(pieces):
        piece[...] = value[index * rows : (index + 1) * rows].astype(BF16)


def lanes_of(spot, half):
    return pl.ds(pl.multiple_of(spot[CORE] * half, LANES), half)


def swap_halves(block):
    lane = lax.broadcasted_iota(jnp.int32, block.shape, 1)
    low = lax.rem(lane, HEAD) < HEAD // 2
    ahead = pltpu.roll(block, LANES - HEAD // 2, 1)
    behind = pltpu.roll(block, HEAD // 2, 1)
    return jnp.where(low, ahead, behind)


def stacked(pair):
    lane = lax.broadcasted_iota(jnp.int32, pair.shape, 1)
    zero = jnp.zeros_like(pair)
    return jnp.concatenate(
        [jnp.where(lane < HEAD, pair, zero), jnp.where(lane < HEAD, zero, pair)], axis=0
    )


def merged(stack, rows):
    lane = lax.broadcasted_iota(jnp.int32, (rows, LANES), 1)
    return jnp.where(lane < HEAD, stack[:rows], stack[rows:])


def visible(table, at, rows, total):
    clean = table[at : at + rows, 2 * LANES : 2 * LANES + 1]
    noisy = table[at : at + rows, 2 * LANES + 1 : 2 * LANES + 2]
    low, high, same = [table[total + i : total + i + 1, at : at + rows] for i in range(3)]
    return ((clean >= low) & (clean <= high)) | (noisy == same)


VECTOR = pl.BlockSpec(memory_space=pltpu.VMEM)
ANYWHERE = pl.BlockSpec(memory_space=pl.ANY)


def call(kernel, args, outs, scratch=(), name=None, held=()):
    count = len(args)

    def wrapped(*refs):
        kernel(*refs[:count], *refs[count + len(held) :])

    return pl.pallas_call(
        wrapped,
        out_shape=[jax.ShapeDtypeStruct(shape, dtype) for shape, dtype in outs],
        in_specs=[VECTOR] * (count + len(held)),
        out_specs=[VECTOR] * len(outs),
        scratch_shapes=list(scratch),
        compiler_params=pltpu.CompilerParams(vmem_limit_bytes=8 * 1024 * 1024),
        name=name,
    )(*args, *held)


GAIN_ATTN, GAIN_FEED, DOWN_SHIFT, SHIFT = range(4)


def cut_kernel(places, *refs):
    spot = where()
    count = len(places)
    refs = refs[1:]
    arrays, outs, sems = refs[: -count - 1], refs[-count - 1 : -1], refs[-1]
    copies = []
    for index, (number, place) in enumerate(places):
        row, column = place(spot)
        rows, columns = outs[index].shape
        lines = pl.ds(pl.multiple_of(row, 16), rows)
        lanes = pl.ds(pl.multiple_of(column, LANES), columns)
        copies.append(
            pltpu.make_async_copy(arrays[number].at[0, lines, lanes], outs[index], sems.at[index])
        )
    for copy in copies:
        copy.start()
    for copy in copies:
        copy.wait()


def cut(before, arrays, places, shapes, name):
    before = arrays[0] if before is None else before
    return pl.pallas_call(
        lambda *refs: cut_kernel(places, *refs),
        out_shape=[jax.ShapeDtypeStruct(shape, BF16) for shape in shapes],
        in_specs=[ANYWHERE] * (1 + len(arrays)),
        out_specs=[VECTOR] * len(shapes),
        scratch_shapes=[pltpu.SemaphoreType.DMA((len(shapes),))],
        compiler_params=pltpu.CompilerParams(vmem_limit_bytes=8 * 1024 * 1024),
        name=name,
    )(before, *arrays)


def table_kernel(micro, mine, theirs, turns, out):
    total = out.shape[0] - 8
    rows = total // micro
    half = rows // 2
    span = half // BLOCK + 1
    lead = where()[LEAD] == 1

    def layout(item, shape, axis):
        place = lax.broadcasted_iota(jnp.int32, shape, axis)
        clean = place >= half
        within = jnp.where(clean, place - half, place)
        document, begin = jnp.zeros(shape, jnp.int32), jnp.zeros(shape, jnp.int32)
        end = jnp.int32(0)
        for j in range(mine.shape[1]):
            length = jnp.where(lead, mine[item, j], theirs[item, j])
            end = end + length
            passed = (within >= end).astype(jnp.int32)
            document = document + passed
            begin = begin + passed * length
        offset = within - begin
        return clean, offset, document * span, document * span + offset // BLOCK

    for item in range(micro):
        at = pl.ds(item * rows, rows)
        clean, offset, _, block = layout(item, (rows, LANES), 0)
        lane = lax.broadcasted_iota(jnp.int32, (rows, LANES), 1)
        chosen = (offset[:, :half] == lane[:, :half]).astype(F32)
        out[at, : 2 * LANES] = lax.dot_general(
            chosen,
            turns[...],
            (((1,), (0,)), ((), ())),
            precision=lax.Precision.HIGHEST,
            preferred_element_type=F32,
        )
        codes = jnp.where(clean == (lane == 0), block, -2)
        out[at, 2 * LANES : 3 * LANES] = codes.astype(F32)
        clean, _, low, block = layout(item, (8, rows), 1)
        row = lax.broadcasted_iota(jnp.int32, (8, rows), 0)
        high, same = jnp.where(clean, block, block - 1), jnp.where(clean, -1, block)
        out[total:, at] = jnp.where(row == 0, low, jnp.where(row == 1, high, same)).astype(F32)


def attend_kernel(micro, keep, arrived, *refs):
    if arrived:
        mine, theirs, before, *refs = refs
    else:
        mine, theirs, *refs = refs
    params, table, *refs = refs
    spot = where()
    held, refs = refs[:4], refs[4:]
    partial, stream, refs = refs[:micro], refs[micro], refs[micro + 1 :]
    if keep:
        normed_out, q, k, v, mixed, chance, pay = refs
    else:
        q, k, v, mixed = refs
    total, width = stream.shape
    half = width // 2
    rows = total // micro
    if arrived:
        low = jnp.where(spot[CORE] == 0, mine[...], theirs[...])
        high = jnp.where(spot[CORE] == 0, theirs[...], mine[...])
        x = jnp.where(spot[FIRST] == 1, before[...], jnp.concatenate([low, high], axis=1))
    else:
        x = jnp.where(spot[LEAD] == 1, mine[...], theirs[...])
    stream[...] = x
    xhat, _ = normalized(x.astype(F32))
    normed = (xhat * params[GAIN_ATTN : GAIN_ATTN + 1, :width]).astype(BF16)
    if keep:
        normed_out[...] = normed
    v[...] = dot(normed, held[2][...]).astype(BF16)
    cos, sin = table[:total, :LANES], table[:total, LANES : 2 * LANES]
    for index, target in ((0, q), (1, k)):
        wide = dot(normed, held[index][...])
        for at in range(0, half, LANES):
            block = wide[:, at : at + LANES]
            target[:, at : at + LANES] = (block * cos + swap_halves(block) * sin).astype(BF16)
    for item in range(micro):
        place = pl.ds(item * rows, rows)
        mask = visible(table, item * rows, rows, total)
        mask = jnp.concatenate([mask, mask], axis=1)
        for pair in range(half // LANES):
            lanes = pl.ds(pair * LANES, LANES)
            scores = dot_cols(k[place, lanes], stacked(q[place, lanes])) * HEAD ** (-0.5)
            scores = jnp.where(mask, scores, MASKED)
            peak = jnp.max(scores, axis=0, keepdims=True)
            powers = jnp.exp(scores - peak)
            weights = powers / jnp.sum(powers, axis=0, keepdims=True)
            if keep:
                chance[item * (half // LANES) + pair] = weights
            result = dot_rows(weights.astype(BF16), v[place, lanes])
            mixed[place, lanes] = merged(result, rows).astype(BF16)
    scatter(dot_cols(mixed[...], held[3][...]), partial)
    if keep:
        pay[:, :half] = normed_out[:, lanes_of(spot, half)]
        pay[:, half:] = mixed[...]


def feed_up(x, own, other, params, held, stream, normed_out, active, slope):
    width = x.shape[1]
    result = (x[...].astype(F32) + joined(own, other)).astype(BF16)
    stream[...] = result
    xhat, _ = normalized(result.astype(F32))
    normed = (xhat * params[GAIN_FEED : GAIN_FEED + 1, :width]).astype(BF16)
    normed_out[...] = normed
    scale = (2.0 / jnp.pi) ** 0.5
    piece = 2 * LANES
    for index in (0, 1):
        for at in range(0, width, piece):
            wide = pl.ds(index * width + at, piece)
            lanes = pl.ds(at, piece)
            if index == 0 or len(held) == 2:
                before = dot(normed, held[index][:, lanes])
            else:
                first, second = ends(where(), width, width // 2)
                before = dot(normed_out[:, first], held[1][:, lanes])
                before += dot(normed_out[:, second], held[2][:, lanes])
            before = before + params[SHIFT : SHIFT + 1, wide]
            square = before * before
            bend = jnp.tanh(scale * before * (1.0 + 0.044715 * square))
            active[index][:, at : at + piece] = (0.5 * before * (1.0 + bend)).astype(BF16)
            if slope is not None:
                inner = scale * (1.0 + 3 * 0.044715 * square)
                tilt = 0.5 * (1.0 + bend) + 0.5 * before * (1.0 - bend * bend) * inner
                slope[:, wide] = tilt.astype(BF16)


def feed_up_kernel(micro, x, *refs):
    own, other, refs = refs[:micro], refs[micro : 2 * micro], refs[2 * micro :]
    params, up_mine, up_near, up_next, down_mine, stream, theirs, total, mine, normed = refs
    ups = (up_mine, up_near, up_next)
    feed_up(x, own, other, params, ups, stream, normed, (mine, theirs), None)
    total[...] = dot(mine[...], down_mine[...])


def ends(spot, width, size):
    return [pl.ds(pl.multiple_of(at * (width - size), LANES), size) for at in (spot[NEAR], 1 - spot[NEAR])]


def feed_down_kernel(total, theirs, near, middle, following, *partial):
    size, width = near.shape
    first, second = ends(where(), width, size)
    result = total[...] + dot(theirs[:, size : width - size], middle[...])
    result += dot(theirs[:, first], near[...]) + dot(theirs[:, second], following[...])
    scatter(result, partial)


def feed_kernel(micro, x, *refs):
    own, other, refs = refs[:micro], refs[micro : 2 * micro], refs[2 * micro :]
    params, up_mine, up_theirs, down_mine, down_theirs, *refs = refs
    spot = where()
    partial, refs = refs[:micro], refs[micro:]
    stream, normed, mine, slope, pay, theirs = refs
    width = x.shape[1]
    half = width // 2
    feed_up(x, own, other, params, (up_mine, up_theirs), stream, normed, (mine, theirs), slope)
    scatter(dot(mine[...], down_mine[...]) + dot(theirs[...], down_theirs[...]), partial)
    lanes = lanes_of(spot, half)
    pay[:, :half] = normed[:, lanes]
    pay[:, half:] = theirs[...]


def finish_kernel(micro, stream, *refs):
    own, other, refs = refs[:micro], refs[micro : 2 * micro], refs[2 * micro :]
    params, part, result = refs
    spot = where()
    width = stream.shape[1]
    shift = params[DOWN_SHIFT : DOWN_SHIFT + 1, :width]
    result[...] = (stream[...].astype(F32) + (joined(own, other) + shift)).astype(BF16)
    part[...] = result[:, lanes_of(spot, part.shape[1])]


def last_kernel(micro, stream, *refs):
    own, other, refs = refs[:micro], refs[micro : 2 * micro], refs[2 * micro :]
    params, mine, theirs = refs
    spot = where()
    width = stream.shape[1]
    shift = params[DOWN_SHIFT : DOWN_SHIFT + 1, :width]
    middle = stream[...]
    result = (middle.astype(F32) + (joined(own, other) + shift)).astype(BF16)
    mine[...] = jnp.where(spot[PART] == 0, middle, result)
    theirs[...] = jnp.where(spot[PART] == 0, result, middle)


def feed_back_kernel(micro, arrived, *refs):
    if arrived:
        half_mine, half_theirs, *refs = refs
    else:
        whole_mine, whole_theirs, *refs = refs
    slope, up_mine, up_theirs, down_mine, down_theirs, *refs = refs
    spot = where()
    partial, upstream, refs = refs[:micro], refs[micro], refs[micro + 1 :]
    if arrived:
        mine, theirs, sums = refs
    else:
        mine, theirs = refs
    rows, width = upstream.shape
    if arrived:
        low = jnp.where(spot[CORE] == 0, half_mine[...], half_theirs[...])
        high = jnp.where(spot[CORE] == 0, half_theirs[...], half_mine[...])
        dz = jnp.concatenate([low, high], axis=1)
        sums[2:3, :] = jnp.sum(dz.astype(F32), axis=0, keepdims=True)
        sums[3:, :] = jnp.zeros((sums.shape[0] - 3, width), F32)
    else:
        dz = jnp.where(spot[LEAD] == 1, whole_mine[...], whole_theirs[...])
    upstream[...] = dz
    piece = 2 * LANES
    for index, (down, back) in enumerate(((down_mine, mine), (down_theirs, theirs))):
        for at in range(0, width, piece):
            grad = dot_cols(dz, down[at : at + piece, :])
            grad = grad * slope[:, index * width + at : index * width + at + piece].astype(F32)
            rounded = grad.astype(BF16)
            back[:, at : at + piece] = rounded
            if arrived:
                sums[index : index + 1, at : at + piece] = jnp.sum(
                    rounded.astype(F32), axis=0, keepdims=True
                )
    scatter(dot_cols(mine[...], up_mine[...]) + dot_cols(theirs[...], up_theirs[...]), partial)


def attend_back_kernel(micro, keep, dz, *refs):
    own, other, refs = refs[:micro], refs[micro : 2 * micro], refs[2 * micro :]
    x, params, chance, v, k, q, mixed, table, *refs = refs
    spot = where()
    held, refs = refs[:4], refs[4:]
    given = micro + 2 if keep else micro
    partial, refs = refs[:given], refs[given:]
    grad, *refs = refs
    if keep:
        vector, rhs_a, rhs_b, pay_a, pay_b, *refs = refs
        stream, sums, *partial = partial
    dq, dk, dv, dmixed = refs
    total, width = x.shape
    half = width // 2
    rows = total // micro
    gain = params[GAIN_FEED : GAIN_FEED + 1, :width]
    result, gain_sum = norm_backward(x[...].astype(F32), gain, dz[...], joined(own, other))
    grad[...] = result
    dmixed[...] = dot(result, held[3][...]).astype(BF16)
    for item in range(micro):
        place = pl.ds(item * rows, rows)
        turn = table[item * rows : (item + 1) * rows, :LANES]
        tilt = table[item * rows : (item + 1) * rows, LANES : 2 * LANES]
        for pair in range(half // LANES):
            lanes = pl.ds(pair * LANES, LANES)
            weights = chance[item * (half // LANES) + pair]
            grads = stacked(dmixed[place, lanes])
            queries = stacked(q[place, lanes])
            dv[place, lanes] = dot(weights.astype(BF16), grads).astype(BF16)
            spread = dot_cols(v[place, lanes], grads)
            inner = jnp.sum(weights * spread, axis=0, keepdims=True)
            scores = (weights * (spread - inner)).astype(BF16)
            query_grad = merged(dot_rows(scores, k[place, lanes]), rows) * HEAD ** (-0.5)
            key_grad = dot(scores, queries) * HEAD ** (-0.5)
            dq[place, lanes] = (query_grad * turn - swap_halves(query_grad) * tilt).astype(BF16)
            dk[place, lanes] = (key_grad * turn - swap_halves(key_grad) * tilt).astype(BF16)
    if keep:
        even = spot[PART] == 0
        rhs_a[...] = jnp.where(even, dq[...], dv[...])
        rhs_b[...] = jnp.where(even, dk[...], mixed[...])
        pay_a[...] = jnp.where(even, dv[...], dq[...])
        pay_b[:total] = jnp.where(even, grad[:, lanes_of(spot, half)], dk[...])
    back = dot_cols(dq[...], held[0][...]) + dot_cols(dk[...], held[1][...])
    back += dot_cols(dv[...], held[2][...])
    scatter(back, partial)
    if keep:
        xhat, _ = normalized(stream[...].astype(F32))
        attn_gain = jnp.sum(back * xhat, axis=0, keepdims=True)
        zero = jnp.zeros((1, half), F32)
        alone = spot[CORE] == 0
        feed_gain = jnp.where(alone, gain_sum, 0.0)
        low = jnp.where(alone, sums[2:3, :half], zero)
        high = jnp.where(alone, sums[2:3, half:], zero)
        mine = (sums[0:1, :], jnp.where(even, low, high), jnp.where(even, attn_gain, feed_gain))
        theirs = (sums[1:2, :], jnp.where(even, high, low), jnp.where(even, feed_gain, attn_gain))
        vector[...] = rows_of(split(mine), half)
        wide = rows_of(split(theirs), half)
        above = wide.astype(BF16)
        pay_b[total : total + EXTRA] = above
        pay_b[total + EXTRA :] = (wide - above.astype(F32)).astype(BF16)


def split(vectors):
    units, features, gain = vectors
    half = features.shape[1]
    return units[:, :half], units[:, half:], features, gain[:, :half], gain[:, half:]


def rows_of(vectors, width):
    rows = [jnp.pad(x, ((0, 0), (0, width - x.shape[1]))) for x in vectors]
    return jnp.concatenate(rows + [jnp.zeros((EXTRA - len(rows), width), F32)], axis=0)


def norm_back_kernel(micro, dz, *refs):
    own, other, refs = refs[:micro], refs[micro : 2 * micro], refs[2 * micro :]
    x, params, grad, part = refs
    spot = where()
    gain = params[GAIN_ATTN : GAIN_ATTN + 1, : x.shape[1]]
    result, _ = norm_backward(x[...].astype(F32), gain, dz[...], joined(own, other))
    grad[...] = result
    part[...] = grad[:, lanes_of(spot, part.shape[1])]


def norm_end_kernel(micro, dz, *refs):
    own, other, refs = refs[:micro], refs[micro : 2 * micro], refs[2 * micro :]
    x, params, mine, theirs = refs
    spot = where()
    gain = params[GAIN_ATTN : GAIN_ATTN + 1, : x.shape[1]]
    upstream = dz[...]
    result, _ = norm_backward(x[...].astype(F32), gain, upstream, joined(own, other))
    even = spot[PART] == 0
    mine[...] = jnp.where(even, result, upstream)
    theirs[...] = jnp.where(even, upstream, result)


def halves(spot, size):
    return [(pl.ds(pl.multiple_of(at * size, LANES), size), at) for at in (spot[CORE], 1 - spot[CORE])]


def deal(grad, half, spot, kept, given):
    pairs, size = kept.shape[0], kept.shape[1]
    for i in range(pairs // 2):
        low = grad[2 * i * size : (2 * i + 1) * size]
        high = grad[(2 * i + 1) * size : (2 * i + 2) * size]
        place = half * (pairs // 2) + i
        kept[place] = jnp.where(spot[NEAR] == 0, low, high).astype(BF16)
        given[place] = jnp.where(spot[NEAR] == 0, high, low).astype(BF16)


def down_weight_kernel(near, near_other, far, far_other, dz, far_dz, *outs):
    spot = where()
    width = near.shape[1]
    at = far.shape[1] - width
    lefts = ((near, far), (near_other, far_other))
    for (left, far_left), (_, half) in zip(lefts, halves(spot, width)):
        grad = dot_rows(left[...], dz[...]) + dot_rows(far_left[:, at:], far_dz[...])
        deal(grad, half, spot, *outs)


def up_weight_kernel(near, far, far_other, back, far_back, kept, given):
    spot = where()
    size = near.shape[1] // 2
    for left, (lines, half) in zip((far, far_other), halves(spot, size)):
        grad = dot_rows(near[:, lines], back[...]) + dot_rows(left[:, :size], far_back[...])
        deal(grad, half, spot, kept, given)


def attend_weight_a_kernel(near, far, far_other, right, far_right, kept, given):
    spot = where()
    size = near.shape[1] // 2
    for left, (lines, half) in zip((far, far_other), halves(spot, size)):
        grad = dot_rows(near[:, lines], right[...]) + dot_rows(left[:, :size], far_right[...])
        deal(grad, half, spot, kept, given)


def attend_weight_b_kernel(
    near, grad_in, far, far_other, right, far_right, far_right_other, vector, kept, given
):
    spot = where()
    size = near.shape[1] // 2
    rows = near.shape[0]
    below = kept.shape[1] - EXTRA
    even = spot[PART] == 0
    rights = jnp.where(even, far_right[:rows], far[:, size:])
    lefts = ((far, far_right), (far_other, far_right_other))
    for (left, back), (lines, half) in zip(lefts, halves(spot, size)):
        grad = dot_rows(jnp.where(even, near[:, lines], grad_in[:, lines]), right[...])
        grad += dot_rows(jnp.where(even, left[:, :size], back[:rows]), rights)
        deal(grad, half, spot, kept.at[:, :below], given.at[:, :below])
    total = vector[...] + far_right[rows : rows + EXTRA].astype(F32) + far_right[rows + EXTRA :].astype(F32)
    chips = 2 * kept.shape[0]
    parts = []
    for chip in range(chips):
        lines = []
        for row, extent in ((0, 4 * size), (2, size), (3, 2 * size)):
            each = extent // chips
            at = chip * each
            mine = spot[CORE] == at // (2 * size)
            if row == 0:
                at %= 2 * size
            piece = total[row + at // size : row + at // size + 1, at % size : at % size + each]
            lines.append(jnp.where(mine, piece, 0.0) if row == 0 else piece)
        parts.append(rows_of(lines, size))
    for i in range(chips // 2):
        low, high = parts[2 * i], parts[2 * i + 1]
        kept[i, below:] = jnp.where(spot[NEAR] == 0, low, high).astype(BF16)
        given[i, below:] = jnp.where(spot[NEAR] == 0, high, low).astype(BF16)


def fold_kernel(kept, received, out, given):
    spot = where()
    low = kept[0].astype(F32) + received[0].astype(F32)
    high = kept[1].astype(F32) + received[1].astype(F32)
    out[0] = jnp.where(spot[HIGH] == 0, low, high)
    given[0] = jnp.where(spot[HIGH] == 0, high, low).astype(BF16)


def close_kernel(extra, kept, received, out, given):
    spot = where()
    size = out.shape[0] - extra
    total = kept[0] + received[0].astype(F32)
    low, high = total[:size], total[size : 2 * size]
    out[:size] = jnp.where(spot[CORE] == 0, low, high)
    given[:size] = jnp.where(spot[CORE] == 0, high, low)
    if extra:
        out[size:] = total[2 * size :]
        given[size:] = total[2 * size :]


def attend_out_kernel(mine_a, theirs_a, mine, theirs, out, units, features, gain):
    first = where()[CORE] == 0
    size, half = mine_a.shape
    for at, own, other in ((0, mine_a[...], theirs_a[...]), (2 * half, mine[:size], theirs[:size])):
        out[:, at : at + half] = jnp.where(first, own, other)
        out[:, at + half : at + 2 * half] = jnp.where(first, other, own)
    total = mine[size:] + theirs[size:]
    for row, x in enumerate((units, features, gain)):
        each = x.shape[1]
        x[...] = jnp.where(first, total[row : row + 1, :each], total[row : row + 1, each : 2 * each])


def swap_section(x):
    return lax.ppermute(x, "section", [(i, i ^ 1) for i in range(lax.axis_size("section"))])


def swap_layer(x):
    return lax.ppermute(x, "section", [(i, i ^ 2) for i in range(lax.axis_size("section"))])


def swap_core(x):
    return lax.ppermute(x, "dp", [(i, i ^ 1) for i in range(lax.axis_size("dp"))])


def swap_chip(x, distance):
    return lax.ppermute(x, "dp", [(i, i ^ (2 * distance)) for i in range(lax.axis_size("dp"))])


def after(x, *others):
    return lax.optimization_barrier((x,) + others)[0]


def replica_sum(kept, given, z, chips):
    if chips > LINE:
        pair = jnp.where(z % 2 == 0, jnp.stack([kept, given], 1), jnp.stack([given, kept], 1))
        groups = [[2 * i + c for i in range(chips)] for c in (0, 1)]
        return lax.psum_scatter(
            pair.reshape(chips, *kept.shape[1:]),
            "dp",
            scatter_dimension=0,
            axis_index_groups=groups,
            tiled=False,
        ).astype(F32)
    distance = 1
    while True:
        total = kept.astype(F32) + swap_chip(given, distance).astype(F32)
        if total.shape[0] == 1:
            return total[0]
        distance *= 2
        bit = z // distance % 2
        pairs = total.reshape(total.shape[0] // 2, 2, *total.shape[1:])
        given = lax.dynamic_index_in_dim(pairs, 1 - bit, 1, keepdims=False).astype(given.dtype)
        kept = lax.dynamic_index_in_dim(pairs, bit, 1, keepdims=False)


def rotations(places):
    count = HEAD // 2
    freq = np.power(10000.0, -2.0 * np.arange(count, dtype=np.float32) / HEAD).astype(np.float32)
    angle = np.arange(places, dtype=np.float32)[:, None] * freq[None, :]
    cosine, sine = np.cos(angle), np.sin(angle)
    parts = [cosine] * (LANES // count) + [-sine, sine] * (LANES // HEAD)
    return jnp.asarray(np.concatenate(parts, axis=1).astype(np.float32))


def body(
    hidden_in,
    cotangent,
    doc_lengths,
    attn_weight,
    up_weight,
    down_weight,
    up_bias,
    down_bias,
    norm_gain,
):
    section = lax.axis_index("section")
    replica = lax.axis_index("dp")
    chips = lax.axis_size("dp") // 2
    part, layer = section % 2, section // 2
    core, z = replica % 2, replica // 2
    near = z % 2
    even, lead, first = part == 0, core == part, layer == 0
    micro, rows, width = hidden_in.shape[1:]
    total, half = micro * rows, width // 2
    hidden = up_weight.shape[2]
    blocks = micro * (half // LANES)

    def columns(x, at, size):
        return lax.dynamic_slice_in_dim(x, at, size, axis=1)

    def by_part(mine, theirs, axis):
        return jnp.where(
            even, jnp.concatenate([mine, theirs], axis), jnp.concatenate([theirs, mine], axis)
        )

    def by_core(mine, theirs, axis):
        return jnp.where(
            core == 0, jnp.concatenate([mine, theirs], axis), jnp.concatenate([theirs, mine], axis)
        )

    wide, narrow = ((total, width), BF16), ((total, half), BF16)
    pieces = [((rows, width), BF16)] * micro
    vectors = ((8, width), F32)

    shift_mine = lax.dynamic_slice_in_dim(up_bias[0], core * width, width, axis=0).astype(F32)
    small = jnp.concatenate([shift_mine, down_bias[0].astype(F32), norm_gain[0]])
    def given(at, array, place, shape, name):
        return cut(at, (array,), [(0, place)], [shape], name)[0]

    attn_given = given(
        None,
        attn_weight,
        lambda spot: (0, spot[NEAR] * width + spot[CORE] * half),
        (width, half),
        "cut_attn",
    )
    up_given = given(
        attn_given,
        up_weight,
        lambda spot: (spot[NEAR] * half, spot[CORE] * width),
        (half, width),
        "cut_up",
    )
    attn_near, up_near = swap_section(attn_given), swap_section(up_given)
    hidden_in, cotangent, doc_lengths, small = lax.optimization_barrier(
        (hidden_in, cotangent, doc_lengths, small, up_given)
    )[:4]
    hidden_in, cotangent = hidden_in.reshape(wide[0]), cotangent.reshape(wide[0])
    hidden_other, lengths_other = swap_core((hidden_in, doc_lengths[0]))
    middle_rows = width - 2 * LANES
    down_end, down_given = cut(
        after(hidden_other, small),
        (down_weight,),
        [
            (0, lambda spot: (spot[CORE] * width + spot[NEAR] * (width - LANES), 0)),
            (0, lambda spot: (spot[CORE] * width + LANES, 0)),
        ],
        [(LANES, width), (middle_rows, width)],
        "cut_down",
    )
    down_near, down_middle = swap_section(down_end), swap_section(down_given)
    attn_next, up_next = swap_chip(attn_near, 1), swap_chip(up_near, 1)
    attn_own = cut(
        up_given,
        (attn_weight,),
        [(0, lambda spot, i=i: (0, i * width + spot[CORE] * half)) for i in (0, 1)],
        [(width, half)] * 2,
        "cut_own",
    )
    feed_own = cut(
        down_end,
        (up_weight, down_weight),
        [(0, lambda spot: (0, spot[CORE] * width)), (1, lambda spot: (spot[CORE] * width, 0))],
        [(width, width)] * 2,
        "cut_feed",
    )
    small_theirs = after(swap_section(small), attn_next)
    scalars = pl.BlockSpec(memory_space=pltpu.SMEM)
    table = pl.pallas_call(
        lambda *refs: table_kernel(micro, *refs),
        out_shape=jax.ShapeDtypeStruct((total + 8, max(3 * LANES, total)), F32),
        in_specs=[scalars, scalars, VECTOR],
        out_specs=VECTOR,
        compiler_params=pltpu.CompilerParams(vmem_limit_bytes=8 * 1024 * 1024),
        name="table",
    )(after(doc_lengths[0], attn_near), lengths_other, rotations(rows // 2))
    down_shift = by_part(small[width : width + half], small_theirs[width : width + half], 0)
    gains = [jnp.pad(x[width + half :], (0, width)) for x in (small, small_theirs)]
    params = jnp.stack(
        [
            jnp.where(even, gains[0], gains[1]),
            jnp.where(even, gains[1], gains[0]),
            jnp.pad(down_shift, (0, width)),
            jnp.concatenate([shift_mine, small_theirs[:width]]),
        ]
    )
    params = jnp.pad(params, ((0, 4), (0, 0)))

    def ordered(mine, theirs, *between):
        low, high = jnp.where(near == 0, mine, theirs), jnp.where(near == 0, theirs, mine)
        return jnp.concatenate([low, *between, high], axis=0)

    low, high = jnp.where(near == 0, attn_near, attn_next), jnp.where(near == 0, attn_next, attn_near)
    attn = (
        jnp.where(even, attn_own[0], low),
        jnp.where(even, attn_own[1], high),
        jnp.where(even, low, attn_own[0]),
        jnp.where(even, high, attn_own[1]),
    )

    def attend(streams, keep):
        arrived = len(streams) == 3
        outs, scratch = pieces + [wide], [pltpu.VMEM(*narrow)] * 4
        if keep:
            outs, scratch = outs + [wide] + [narrow] * 4 + [((blocks, rows, 2 * rows), F32), wide], ()
        out = call(
            lambda *refs: attend_kernel(micro, keep, arrived, *refs),
            (*streams, params, table, *attn),
            outs,
            scratch,
            "attend",
        )
        return out[:micro], out[micro:]

    own_part, (stream_0,) = attend((hidden_in, hidden_other), False)
    down_next = swap_chip(after(down_near, own_part[0]), 1)
    middle, *active = call(
        lambda *refs: feed_up_kernel(micro, *refs),
        (
            stream_0,
            *own_part,
            *swap_core(own_part),
            params,
            feed_own[0],
            up_near,
            up_next,
            feed_own[1],
        ),
        [wide] * 2 + [(wide[0], F32)],
        [pltpu.VMEM(*wide)] * 2,
        name="feed_up",
    )
    own_part = call(
        feed_down_kernel, (active[1], active[0], down_near, down_middle, down_next), pieces, name="feed_down"
    )
    arrived = call(
        lambda *refs: finish_kernel(micro, *refs),
        (middle, *own_part, *swap_core(own_part), params),
        [narrow],
        [pltpu.VMEM(*wide)],
        "finish",
    )[0]
    ups = (feed_own[0], ordered(after(up_near, arrived), up_next))
    downs = (feed_own[1], ordered(after(down_near, arrived), down_next, down_middle))
    arrived = after(swap_layer(arrived), ups[1], downs[1])
    own_part, kept = attend((arrived, swap_core(arrived), stream_0), True)
    stream, normed_attn, q, k, v, mixed, chance, pay_attn = kept
    far_attn = swap_section(pay_attn)
    out = call(
        lambda *refs: feed_kernel(micro, *refs),
        (stream, *own_part, *swap_core(own_part), params, *ups, *downs),
        pieces + [wide] * 3 + [((total, 2 * width), BF16), ((total, width + half), BF16)],
        [pltpu.VMEM(*wide)],
        "feed",
    )
    fed, (middle, normed_feed, active_mine, slope, pay) = out[:micro], out[micro:]
    far = swap_section(pay)

    def feed_back(upstreams, arrived, held=()):
        outs, scratch = pieces + [wide], [pltpu.VMEM(*wide)] * 2
        if arrived:
            outs, scratch = outs + [wide, wide, vectors], ()
        out = call(
            lambda *refs: feed_back_kernel(micro, arrived, *refs),
            (*upstreams, slope, *ups, *downs),
            outs,
            scratch,
            "feed_back",
            held,
        )
        return out[:micro], out[micro:]

    def attend_back(upstream, own, other, params, keep, held=()):
        outs = pieces + [wide]
        more = ()
        if keep:
            outs += [((EXTRA, half), F32)] + [narrow] * 3 + [((total + 2 * EXTRA, half), BF16)]
            more = keep
        out = call(
            lambda *refs: attend_back_kernel(micro, bool(keep), *refs),
            (upstream, *own, *other, middle, params, chance, v, k, q, mixed, table, *attn, *more),
            outs,
            [pltpu.VMEM(*narrow)] * 4,
            "attend_back",
            held,
        )
        return out[:micro], out[micro:]

    kept_on = (slope, *fed, *ups, *downs, active_mine)
    cotangent_other = swap_core(after(cotangent, arrived))
    own_part, (upstream_0,) = feed_back((cotangent, cotangent_other), False, kept_on)
    own_part, (grad,) = attend_back(
        upstream_0, own_part, swap_core(own_part), params, (), kept_on
    )
    *own_part, far_attn = lax.optimization_barrier((*own_part, far_attn))
    grad_2, arrived = call(
        lambda *refs: norm_back_kernel(micro, *refs),
        (grad, *own_part, *swap_core(own_part), stream, params),
        [wide, narrow],
        name="norm_back",
        held=kept_on,
    )
    arrived = swap_layer(arrived)
    upstream_half = after(columns(upstream_0, core * half, half), grad_2)

    def weight(kernel, args, shape, name, extra=0):
        outs = [((chips // 2, shape[0] // chips + extra, shape[1]), BF16)] * 2
        return call(kernel, args, outs, name=name)

    def folded(grad, token):
        kept, given = grad
        if chips != LINE:
            return replica_sum(kept, given, z, chips)
        received = after(swap_chip(given, 1), token)
        part = (1, *kept.shape[1:])
        return call(fold_kernel, (kept, received), [(part, F32), (part, BF16)], name="fold")

    def closed(fold, token, extra=0):
        if chips != LINE:
            size = (fold.shape[0] - extra) // 2
            mine = lax.dynamic_slice_in_dim(fold, core * size, size, axis=0)
            theirs = lax.dynamic_slice_in_dim(fold, (1 - core) * size, size, axis=0)
            mine, theirs = [jnp.concatenate([x, fold[2 * size :]], axis=0) for x in (mine, theirs)]
            return mine, swap_core(theirs)
        kept, given = fold
        received = after(swap_chip(given, 2), token)
        part = (((kept.shape[-2] + extra) // 2, kept.shape[-1]), F32)
        mine, theirs = call(
            lambda *refs: close_kernel(extra, *refs), (kept, received), [part] * 2, name="close"
        )
        return mine, swap_core(theirs)

    x = types.SimpleNamespace(far=far, far_attn=far_attn)

    def take_upstream(token):
        x.half = jnp.where(first, after(arrived, token), upstream_half)
        x.half_other, x.far_half = swap_core(x.half), swap_section(x.half)
        return x.half

    def take_far(token):
        x.far = after(x.far, token)
        x.far_other = swap_core(x.far)
        return x.far

    def send_active(token):
        x.active_other = swap_core(after(active_mine, token))
        return token

    def feed_step(token):
        x.part, back = feed_back((after(x.half, token), x.half_other), True)
        x.upstream, x.back, theirs, x.sums = back
        x.far_back, x.part_other = swap_section(theirs), swap_core(x.part)
        return x.upstream

    def take_attn(token):
        x.far_attn = after(x.far_attn, token)
        return x.far_attn

    def attend_step(token):
        part, other = x.part, x.part_other
        x.part, back = attend_back(x.upstream, part, other, after(params, token), (stream, x.sums))
        x.grad, x.vector, x.rhs_a, x.rhs_b, pay_a, pay_b = back
        x.far_rhs_a, x.far_rhs_b = swap_section(pay_a), swap_section(pay_b)
        return x.grad

    def send_attn(token):
        x.far_attn_other = swap_core(after(x.far_attn, token))
        return token

    def take_half(token):
        x.far_half = after(x.far_half, token)
        return x.far_half

    def take_back(token):
        x.far_back = after(x.far_back, token)
        return x.far_back

    def take_rhs_a(token):
        x.far_rhs_a = after(x.far_rhs_a, token)
        return x.far_rhs_a

    def take_rhs_b(token):
        x.far_rhs_b = after(x.far_rhs_b, token)
        x.far_rhs_b_other = swap_core(x.far_rhs_b)
        return x.far_rhs_b

    def down_step(token):
        args = (active_mine, x.active_other, x.far, x.far_other, x.half, after(x.far_half, token))
        x.down = weight(down_weight_kernel, args, (hidden, half), "down_weight")
        return x.down[0]

    def up_step(token):
        args = (normed_feed, x.far, x.far_other, x.back, after(x.far_back, token))
        x.up = weight(up_weight_kernel, args, (width, width), "up_weight")
        return x.up[0]

    def attn_step_a(token):
        args = (normed_attn, x.far_attn, x.far_attn_other, x.rhs_a, after(x.far_rhs_a, token))
        x.attn_a = weight(attend_weight_a_kernel, args, (width, half), "attend_weight_a")
        return x.attn_a[0]

    def attn_step_b(token):
        args = (normed_attn, x.grad, x.far_attn, x.far_attn_other, x.rhs_b)
        args += (after(x.far_rhs_b, token), x.far_rhs_b_other, x.vector)
        x.attn_b = weight(attend_weight_b_kernel, args, (width, half), "attend_weight_b", EXTRA)
        return x.attn_b[0]

    def norm_step(token):
        x.grads, x.grads_given = call(
            lambda *refs: norm_end_kernel(micro, *refs),
            (x.grad, *x.part, *swap_core(x.part), stream, after(params, token)),
            [wide, wide],
            name="norm_end",
        )
        return x.grads

    def send_fed(token):
        x.fed_other = swap_core([after(y, token) for y in fed])
        return token

    def last_step(token):
        x.outputs, x.outputs_given = call(
            lambda *refs: last_kernel(micro, *refs),
            (middle, *fed, *x.fed_other, after(params, token)),
            [wide, wide],
            name="last",
        )
        return x.outputs

    def send_outputs(token):
        x.outputs_far = swap_section(after(x.outputs_given, token))
        return token

    def send_grads(token):
        x.grads_far = swap_section(after(x.grads_given, token))
        return token

    def take_outputs(token):
        x.outputs = jnp.where(lead, x.outputs, after(x.outputs_far, token))
        return x.outputs

    def take_grads(token):
        x.grads = jnp.where(lead, x.grads, after(x.grads_far, token))
        return x.grads

    def down_fold(token):
        x.down = folded(x.down, token)
        return x.down[0]

    def up_fold(token):
        x.up = folded(x.up, token)
        return x.up[0]

    def attn_fold_a(token):
        x.attn_a = folded(x.attn_a, token)
        return x.attn_a[0]

    def attn_fold_b(token):
        x.attn_b = folded(x.attn_b, token)
        return x.attn_b[0]

    def down_close(token):
        x.down = closed(x.down, token)
        return x.down[0]

    def up_close(token):
        x.up = closed(x.up, token)
        return x.up[0]

    def attn_close_a(token):
        x.attn_a = closed(x.attn_a, token)
        return x.attn_a[0]

    def attn_close_b(token):
        x.attn_b = closed(x.attn_b, token, EXTRA)
        return x.attn_b[0]

    token = grad_2
    for step in (
        take_upstream,
        take_far,
        send_active,
        feed_step,
        take_half,
        down_step,
        take_attn,
        attend_step,
        send_attn,
        take_back,
        up_step,
        down_fold,
        norm_step,
        take_rhs_a,
        attn_step_a,
        take_rhs_b,
        attn_step_b,
        send_grads,
        send_fed,
        up_fold,
        attn_fold_a,
        down_close,
        last_step,
        send_outputs,
        attn_fold_b,
        up_close,
        take_grads,
        take_outputs,
        attn_close_a,
        attn_close_b,
    ):
        token = step(token)

    size = width // (2 * chips)
    if chips == LINE:
        attn_out, up_shift_out, down_shift_out, gain_out = call(
            attend_out_kernel,
            (*x.attn_a, *x.attn_b),
            [((size, hidden), F32)] + [((1, y // (2 * chips)), F32) for y in (hidden, half, width)],
            name="attend_out",
        )
    else:
        attn_out = jnp.concatenate(
            [by_core(*x.attn_a, 1), by_core(*[y[:size] for y in x.attn_b], 1)], axis=1
        )
        vector = x.attn_b[0][size:] + x.attn_b[1][size:]
        up_shift_out, down_shift_out, gain_out = [
            columns(vector[i : i + 1], core * (y // (2 * chips)), y // (2 * chips))
            for i, y in enumerate((hidden, half, width))
        ]
    up_out, down_out = by_core(*x.up, 1), by_core(*x.down, 1)

    shape = (1, 1, micro, rows, width)
    return (
        x.outputs.reshape(shape),
        x.grads.reshape(shape),
        attn_out[None],
        up_out[None],
        down_out[None],
        up_shift_out,
        down_shift_out,
        gain_out,
    )


def solution(mesh):
    in_specs = (
        P("dp", None, None, None),
        P("dp", None, None, None),
        P("dp", None, None),
        P("section", None, None),
        P("section", None, None),
        P("section", None, None),
        P("section", None),
        P("section", None),
        P("section", None),
    )
    out_specs = (
        P("section", "dp", None, None, None),
        P("section", "dp", None, None, None),
        P("section", "dp", None),
        P("section", "dp", None),
        P("section", "dp", None),
        P("section", "dp"),
        P("section", "dp"),
        P("section", "dp"),
    )
    return jax.shard_map(body, mesh=mesh, in_specs=in_specs, out_specs=out_specs, check_vma=False)
```

```python
import types

import jax
import jax.numpy as jnp
import numpy as np
from jax import lax
from jax.experimental import pallas as pl
from jax.experimental.pallas import tpu as pltpu
from jax.sharding import PartitionSpec as P

HEAD = 64
BLOCK = 16
EPSILON = 1e-05
MASKED = -1e30
LANES = 128
LINE = 4
EXTRA = 16
F32 = jnp.float32
BF16 = jnp.bfloat16
PART, NEAR, CORE, LEAD, FIRST, HIGH = range(6)


def dot(left, right):
    return lax.dot_general(left, right, (((1,), (0,)), ((), ())), preferred_element_type=F32)


def dot_cols(left, right):
    return lax.dot_general(left, right, (((1,), (1,)), ((), ())), preferred_element_type=F32)


def dot_rows(left, right):
    return lax.dot_general(left, right, (((0,), (0,)), ((), ())), preferred_element_type=F32)


def normalized(values):
    mean = jnp.mean(values, axis=-1, keepdims=True)
    centered = values - mean
    spread = jnp.mean(centered * centered, axis=-1, keepdims=True)
    rstd = lax.rsqrt(spread + EPSILON)
    return centered * rstd, rstd


def norm_backward(values, gain, upstream, grad_normed):
    xhat, rstd = normalized(values)
    scaled = grad_normed * gain
    mean = jnp.mean(scaled, axis=-1, keepdims=True)
    along = jnp.mean(scaled * xhat, axis=-1, keepdims=True)
    grad_gain = jnp.sum(grad_normed * xhat, axis=0, keepdims=True)
    grad = upstream.astype(F32) + rstd * (scaled - mean - xhat * along)
    return grad.astype(BF16), grad_gain


def joined(own, other):
    return jnp.concatenate([a[...].astype(F32) + b[...].astype(F32) for a, b in zip(own, other)], axis=0)


def where():
    section, replica = lax.axis_index("section"), lax.axis_index("dp")
    part, core, z = section % 2, replica % 2, replica // 2
    lead = (part == core).astype(jnp.int32)
    first = (section < 2).astype(jnp.int32)
    return part, z % 2, core, lead, first, z // 2 % 2


def scatter(value, pieces):
    rows = pieces[0].shape[0]
    for index, piece in enumerate(pieces):
        piece[...] = value[index * rows : (index + 1) * rows].astype(BF16)


def lanes_of(spot, half):
    return pl.ds(pl.multiple_of(spot[CORE] * half, LANES), half)


def swap_halves(block):
    lane = lax.broadcasted_iota(jnp.int32, block.shape, 1)
    low = lax.rem(lane, HEAD) < HEAD // 2
    ahead = pltpu.roll(block, LANES - HEAD // 2, 1)
    behind = pltpu.roll(block, HEAD // 2, 1)
    return jnp.where(low, ahead, behind)


def stacked(pair):
    lane = lax.broadcasted_iota(jnp.int32, pair.shape, 1)
    zero = jnp.zeros_like(pair)
    return jnp.concatenate(
        [jnp.where(lane < HEAD, pair, zero), jnp.where(lane < HEAD, zero, pair)], axis=0
    )


def merged(stack, rows):
    lane = lax.broadcasted_iota(jnp.int32, (rows, LANES), 1)
    return jnp.where(lane < HEAD, stack[:rows], stack[rows:])


def visible(table, at, rows, total):
    clean = table[at : at + rows, 2 * LANES : 2 * LANES + 1]
    noisy = table[at : at + rows, 2 * LANES + 1 : 2 * LANES + 2]
    low, high, same = [table[total + i : total + i + 1, at : at + rows] for i in range(3)]
    return ((clean >= low) & (clean <= high)) | (noisy == same)


VECTOR = pl.BlockSpec(memory_space=pltpu.VMEM)
ANYWHERE = pl.BlockSpec(memory_space=pl.ANY)


def call(kernel, args, outs, scratch=(), name=None, held=()):
    count = len(args)

    def wrapped(*refs):
        kernel(*refs[:count], *refs[count + len(held) :])

    return pl.pallas_call(
        wrapped,
        out_shape=[jax.ShapeDtypeStruct(shape, dtype) for shape, dtype in outs],
        in_specs=[VECTOR] * (count + len(held)),
        out_specs=[VECTOR] * len(outs),
        scratch_shapes=list(scratch),
        compiler_params=pltpu.CompilerParams(vmem_limit_bytes=8 * 1024 * 1024),
        name=name,
    )(*args, *held)


GAIN_ATTN, GAIN_FEED, DOWN_SHIFT, SHIFT = range(4)


def cut_kernel(places, *refs):
    spot = where()
    count = len(places)
    refs = refs[1:]
    arrays, outs, sems = refs[: -count - 1], refs[-count - 1 : -1], refs[-1]
    copies = []
    for index, (number, place) in enumerate(places):
        row, column = place(spot)
        rows, columns = outs[index].shape
        lines = pl.ds(pl.multiple_of(row, 16), rows)
        lanes = pl.ds(pl.multiple_of(column, LANES), columns)
        copies.append(
            pltpu.make_async_copy(arrays[number].at[0, lines, lanes], outs[index], sems.at[index])
        )
    for copy in copies:
        copy.start()
    for copy in copies:
        copy.wait()


def cut(before, arrays, places, shapes, name):
    before = arrays[0] if before is None else before
    return pl.pallas_call(
        lambda *refs: cut_kernel(places, *refs),
        out_shape=[jax.ShapeDtypeStruct(shape, BF16) for shape in shapes],
        in_specs=[ANYWHERE] * (1 + len(arrays)),
        out_specs=[VECTOR] * len(shapes),
        scratch_shapes=[pltpu.SemaphoreType.DMA((len(shapes),))],
        compiler_params=pltpu.CompilerParams(vmem_limit_bytes=8 * 1024 * 1024),
        name=name,
    )(before, *arrays)


def table_kernel(micro, mine, theirs, turns, out):
    total = out.shape[0] - 8
    rows = total // micro
    half = rows // 2
    span = half // BLOCK + 1
    lead = where()[LEAD] == 1

    def layout(item, shape, axis):
        place = lax.broadcasted_iota(jnp.int32, shape, axis)
        clean = place >= half
        within = jnp.where(clean, place - half, place)
        document, begin = jnp.zeros(shape, jnp.int32), jnp.zeros(shape, jnp.int32)
        end = jnp.int32(0)
        for j in range(mine.shape[1]):
            length = jnp.where(lead, mine[item, j], theirs[item, j])
            end = end + length
            passed = (within >= end).astype(jnp.int32)
            document = document + passed
            begin = begin + passed * length
        offset = within - begin
        return clean, offset, document * span, document * span + offset // BLOCK

    for item in range(micro):
        at = pl.ds(item * rows, rows)
        clean, offset, _, block = layout(item, (rows, LANES), 0)
        lane = lax.broadcasted_iota(jnp.int32, (rows, LANES), 1)
        chosen = (offset[:, :half] == lane[:, :half]).astype(F32)
        out[at, : 2 * LANES] = lax.dot_general(
            chosen,
            turns[...],
            (((1,), (0,)), ((), ())),
            precision=lax.Precision.HIGHEST,
            preferred_element_type=F32,
        )
        codes = jnp.where(clean == (lane == 0), block, -2)
        out[at, 2 * LANES : 3 * LANES] = codes.astype(F32)
        clean, _, low, block = layout(item, (8, rows), 1)
        row = lax.broadcasted_iota(jnp.int32, (8, rows), 0)
        high, same = jnp.where(clean, block, block - 1), jnp.where(clean, -1, block)
        out[total:, at] = jnp.where(row == 0, low, jnp.where(row == 1, high, same)).astype(F32)


def attend_kernel(micro, keep, arrived, *refs):
    if arrived:
        mine, theirs, before, *refs = refs
    else:
        mine, theirs, *refs = refs
    params, table, *refs = refs
    spot = where()
    held, refs = refs[:4], refs[4:]
    partial, stream, refs = refs[:micro], refs[micro], refs[micro + 1 :]
    if keep:
        normed_out, q, k, v, mixed, chance, pay = refs
    else:
        q, k, v, mixed = refs
    total, width = stream.shape
    half = width // 2
    rows = total // micro
    if arrived:
        low = jnp.where(spot[CORE] == 0, mine[...], theirs[...])
        high = jnp.where(spot[CORE] == 0, theirs[...], mine[...])
        x = jnp.where(spot[FIRST] == 1, before[...], jnp.concatenate([low, high], axis=1))
    else:
        x = jnp.where(spot[LEAD] == 1, mine[...], theirs[...])
    stream[...] = x
    xhat, _ = normalized(x.astype(F32))
    normed = (xhat * params[GAIN_ATTN : GAIN_ATTN + 1, :width]).astype(BF16)
    if keep:
        normed_out[...] = normed
    v[...] = dot(normed, held[2][...]).astype(BF16)
    cos, sin = table[:total, :LANES], table[:total, LANES : 2 * LANES]
    for index, target in ((0, q), (1, k)):
        wide = dot(normed, held[index][...])
        for at in range(0, half, LANES):
            block = wide[:, at : at + LANES]
            target[:, at : at + LANES] = (block * cos + swap_halves(block) * sin).astype(BF16)
    for item in range(micro):
        place = pl.ds(item * rows, rows)
        mask = visible(table, item * rows, rows, total)
        mask = jnp.concatenate([mask, mask], axis=1)
        for pair in range(half // LANES):
            lanes = pl.ds(pair * LANES, LANES)
            scores = dot_cols(k[place, lanes], stacked(q[place, lanes])) * HEAD ** (-0.5)
            scores = jnp.where(mask, scores, MASKED)
            peak = jnp.max(scores, axis=0, keepdims=True)
            powers = jnp.exp(scores - peak)
            weights = powers / jnp.sum(powers, axis=0, keepdims=True)
            if keep:
                chance[item * (half // LANES) + pair] = weights
            result = dot_rows(weights.astype(BF16), v[place, lanes])
            mixed[place, lanes] = merged(result, rows).astype(BF16)
    scatter(dot_cols(mixed[...], held[3][...]), partial)
    if keep:
        pay[:, :half] = normed_out[:, lanes_of(spot, half)]
        pay[:, half:] = mixed[...]


def feed_up(x, own, other, params, held, stream, normed_out, active, slope):
    width = x.shape[1]
    result = (x[...].astype(F32) + joined(own, other)).astype(BF16)
    stream[...] = result
    xhat, _ = normalized(result.astype(F32))
    normed = (xhat * params[GAIN_FEED : GAIN_FEED + 1, :width]).astype(BF16)
    normed_out[...] = normed
    scale = (2.0 / jnp.pi) ** 0.5
    piece = 2 * LANES
    for index in (0, 1):
        for at in range(0, width, piece):
            wide = pl.ds(index * width + at, piece)
            lanes = pl.ds(at, piece)
            if index == 0 or len(held) == 2:
                before = dot(normed, held[index][:, lanes])
            else:
                first, second = ends(where(), width, width // 2)
                before = dot(normed_out[:, first], held[1][:, lanes])
                before += dot(normed_out[:, second], held[2][:, lanes])
            before = before + params[SHIFT : SHIFT + 1, wide]
            square = before * before
            bend = jnp.tanh(scale * before * (1.0 + 0.044715 * square))
            active[index][:, at : at + piece] = (0.5 * before * (1.0 + bend)).astype(BF16)
            if slope is not None:
                inner = scale * (1.0 + 3 * 0.044715 * square)
                tilt = 0.5 * (1.0 + bend) + 0.5 * before * (1.0 - bend * bend) * inner
                slope[:, wide] = tilt.astype(BF16)


def feed_up_kernel(micro, x, *refs):
    own, other, refs = refs[:micro], refs[micro : 2 * micro], refs[2 * micro :]
    params, up_mine, up_near, up_next, down_mine, stream, theirs, total, mine, normed = refs
    ups = (up_mine, up_near, up_next)
    feed_up(x, own, other, params, ups, stream, normed, (mine, theirs), None)
    total[...] = dot(mine[...], down_mine[...])


def ends(spot, width, size):
    return [pl.ds(pl.multiple_of(at * (width - size), LANES), size) for at in (spot[NEAR], 1 - spot[NEAR])]


def feed_down_kernel(total, theirs, near, middle, following, *partial):
    size, width = near.shape
    first, second = ends(where(), width, size)
    result = total[...] + dot(theirs[:, size : width - size], middle[...])
    result += dot(theirs[:, first], near[...]) + dot(theirs[:, second], following[...])
    scatter(result, partial)


def feed_kernel(micro, x, *refs):
    own, other, refs = refs[:micro], refs[micro : 2 * micro], refs[2 * micro :]
    params, up_mine, up_theirs, down_mine, down_theirs, *refs = refs
    spot = where()
    partial, refs = refs[:micro], refs[micro:]
    stream, normed, mine, slope, pay, theirs = refs
    width = x.shape[1]
    half = width // 2
    feed_up(x, own, other, params, (up_mine, up_theirs), stream, normed, (mine, theirs), slope)
    scatter(dot(mine[...], down_mine[...]) + dot(theirs[...], down_theirs[...]), partial)
    lanes = lanes_of(spot, half)
    pay[:, :half] = normed[:, lanes]
    pay[:, half:] = theirs[...]


def finish_kernel(micro, stream, *refs):
    own, other, refs = refs[:micro], refs[micro : 2 * micro], refs[2 * micro :]
    params, part, result = refs
    spot = where()
    width = stream.shape[1]
    shift = params[DOWN_SHIFT : DOWN_SHIFT + 1, :width]
    result[...] = (stream[...].astype(F32) + (joined(own, other) + shift)).astype(BF16)
    part[...] = result[:, lanes_of(spot, part.shape[1])]


def last_kernel(micro, stream, *refs):
    own, other, refs = refs[:micro], refs[micro : 2 * micro], refs[2 * micro :]
    params, mine, theirs = refs
    spot = where()
    width = stream.shape[1]
    shift = params[DOWN_SHIFT : DOWN_SHIFT + 1, :width]
    middle = stream[...]
    result = (middle.astype(F32) + (joined(own, other) + shift)).astype(BF16)
    mine[...] = jnp.where(spot[PART] == 0, middle, result)
    theirs[...] = jnp.where(spot[PART] == 0, result, middle)


def feed_back_kernel(micro, arrived, *refs):
    if arrived:
        half_mine, half_theirs, *refs = refs
    else:
        whole_mine, whole_theirs, *refs = refs
    slope, up_mine, up_theirs, down_mine, down_theirs, *refs = refs
    spot = where()
    partial, upstream, refs = refs[:micro], refs[micro], refs[micro + 1 :]
    if arrived:
        mine, theirs, sums = refs
    else:
        mine, theirs = refs
    rows, width = upstream.shape
    if arrived:
        low = jnp.where(spot[CORE] == 0, half_mine[...], half_theirs[...])
        high = jnp.where(spot[CORE] == 0, half_theirs[...], half_mine[...])
        dz = jnp.concatenate([low, high], axis=1)
        sums[2:3, :] = jnp.sum(dz.astype(F32), axis=0, keepdims=True)
        sums[3:, :] = jnp.zeros((sums.shape[0] - 3, width), F32)
    else:
        dz = jnp.where(spot[LEAD] == 1, whole_mine[...], whole_theirs[...])
    upstream[...] = dz
    piece = 2 * LANES
    for index, (down, back) in enumerate(((down_mine, mine), (down_theirs, theirs))):
        for at in range(0, width, piece):
            grad = dot_cols(dz, down[at : at + piece, :])
            grad = grad * slope[:, index * width + at : index * width + at + piece].astype(F32)
            rounded = grad.astype(BF16)
            back[:, at : at + piece] = rounded
            if arrived:
                sums[index : index + 1, at : at + piece] = jnp.sum(
                    rounded.astype(F32), axis=0, keepdims=True
                )
    scatter(dot_cols(mine[...], up_mine[...]) + dot_cols(theirs[...], up_theirs[...]), partial)


def attend_back_kernel(micro, keep, dz, *refs):
    own, other, refs = refs[:micro], refs[micro : 2 * micro], refs[2 * micro :]
    x, params, chance, v, k, q, mixed, table, *refs = refs
    spot = where()
    held, refs = refs[:4], refs[4:]
    given = micro + 2 if keep else micro
    partial, refs = refs[:given], refs[given:]
    grad, *refs = refs
    if keep:
        vector, rhs_a, rhs_b, pay_a, pay_b, *refs = refs
        stream, sums, *partial = partial
    dq, dk, dv, dmixed = refs
    total, width = x.shape
    half = width // 2
    rows = total // micro
    gain = params[GAIN_FEED : GAIN_FEED + 1, :width]
    result, gain_sum = norm_backward(x[...].astype(F32), gain, dz[...], joined(own, other))
    grad[...] = result
    dmixed[...] = dot(result, held[3][...]).astype(BF16)
    for item in range(micro):
        place = pl.ds(item * rows, rows)
        turn = table[item * rows : (item + 1) * rows, :LANES]
        tilt = table[item * rows : (item + 1) * rows, LANES : 2 * LANES]
        for pair in range(half // LANES):
            lanes = pl.ds(pair * LANES, LANES)
            weights = chance[item * (half // LANES) + pair]
            grads = stacked(dmixed[place, lanes])
            queries = stacked(q[place, lanes])
            dv[place, lanes] = dot(weights.astype(BF16), grads).astype(BF16)
            spread = dot_cols(v[place, lanes], grads)
            inner = jnp.sum(weights * spread, axis=0, keepdims=True)
            scores = (weights * (spread - inner)).astype(BF16)
            query_grad = merged(dot_rows(scores, k[place, lanes]), rows) * HEAD ** (-0.5)
            key_grad = dot(scores, queries) * HEAD ** (-0.5)
            dq[place, lanes] = (query_grad * turn - swap_halves(query_grad) * tilt).astype(BF16)
            dk[place, lanes] = (key_grad * turn - swap_halves(key_grad) * tilt).astype(BF16)
    if keep:
        even = spot[PART] == 0
        rhs_a[...] = jnp.where(even, dq[...], dv[...])
        rhs_b[...] = jnp.where(even, dk[...], mixed[...])
        pay_a[...] = jnp.where(even, dv[...], dq[...])
        pay_b[:total] = jnp.where(even, grad[:, lanes_of(spot, half)], dk[...])
    back = dot_cols(dq[...], held[0][...]) + dot_cols(dk[...], held[1][...])
    back += dot_cols(dv[...], held[2][...])
    scatter(back, partial)
    if keep:
        xhat, _ = normalized(stream[...].astype(F32))
        attn_gain = jnp.sum(back * xhat, axis=0, keepdims=True)
        zero = jnp.zeros((1, half), F32)
        alone = spot[CORE] == 0
        feed_gain = jnp.where(alone, gain_sum, 0.0)
        low = jnp.where(alone, sums[2:3, :half], zero)
        high = jnp.where(alone, sums[2:3, half:], zero)
        mine = (sums[0:1, :], jnp.where(even, low, high), jnp.where(even, attn_gain, feed_gain))
        theirs = (sums[1:2, :], jnp.where(even, high, low), jnp.where(even, feed_gain, attn_gain))
        vector[...] = rows_of(split(mine), half)
        wide = rows_of(split(theirs), half)
        above = wide.astype(BF16)
        pay_b[total : total + EXTRA] = above
        pay_b[total + EXTRA :] = (wide - above.astype(F32)).astype(BF16)


def split(vectors):
    units, features, gain = vectors
    half = features.shape[1]
    return units[:, :half], units[:, half:], features, gain[:, :half], gain[:, half:]


def rows_of(vectors, width):
    rows = [jnp.pad(x, ((0, 0), (0, width - x.shape[1]))) for x in vectors]
    return jnp.concatenate(rows + [jnp.zeros((EXTRA - len(rows), width), F32)], axis=0)


def norm_back_kernel(micro, dz, *refs):
    own, other, refs = refs[:micro], refs[micro : 2 * micro], refs[2 * micro :]
    x, params, grad, part = refs
    spot = where()
    gain = params[GAIN_ATTN : GAIN_ATTN + 1, : x.shape[1]]
    result, _ = norm_backward(x[...].astype(F32), gain, dz[...], joined(own, other))
    grad[...] = result
    part[...] = grad[:, lanes_of(spot, part.shape[1])]


def norm_end_kernel(micro, dz, *refs):
    own, other, refs = refs[:micro], refs[micro : 2 * micro], refs[2 * micro :]
    x, params, mine, theirs = refs
    spot = where()
    gain = params[GAIN_ATTN : GAIN_ATTN + 1, : x.shape[1]]
    upstream = dz[...]
    result, _ = norm_backward(x[...].astype(F32), gain, upstream, joined(own, other))
    even = spot[PART] == 0
    mine[...] = jnp.where(even, result, upstream)
    theirs[...] = jnp.where(even, upstream, result)


def halves(spot, size):
    return [(pl.ds(pl.multiple_of(at * size, LANES), size), at) for at in (spot[CORE], 1 - spot[CORE])]


def deal(grad, half, spot, kept, given):
    pairs, size = kept.shape[0], kept.shape[1]
    for i in range(pairs // 2):
        low = grad[2 * i * size : (2 * i + 1) * size]
        high = grad[(2 * i + 1) * size : (2 * i + 2) * size]
        place = half * (pairs // 2) + i
        kept[place] = jnp.where(spot[NEAR] == 0, low, high).astype(BF16)
        given[place] = jnp.where(spot[NEAR] == 0, high, low).astype(BF16)


def down_near_kernel(near, near_other, dz, out):
    out[0] = dot_rows(near[...], dz[...])
    out[1] = dot_rows(near_other[...], dz[...])


def down_weight_kernel(part, far, far_other, far_dz, kept, given):
    spot = where()
    width = part.shape[1]
    at = far.shape[1] - width
    for i, (far_left, (_, half)) in enumerate(zip((far, far_other), halves(spot, width))):
        grad = part[i] + dot_rows(far_left[:, at:], far_dz[...])
        deal(grad, half, spot, kept, given)


def up_weight_kernel(near, far, far_other, back, far_back, kept, given):
    spot = where()
    size = near.shape[1] // 2
    for left, (lines, half) in zip((far, far_other), halves(spot, size)):
        grad = dot_rows(near[:, lines], back[...]) + dot_rows(left[:, :size], far_back[...])
        deal(grad, half, spot, kept, given)


def attend_weight_a_kernel(near, far, far_other, right, far_right, kept, given):
    spot = where()
    size = near.shape[1] // 2
    for left, (lines, half) in zip((far, far_other), halves(spot, size)):
        grad = dot_rows(near[:, lines], right[...]) + dot_rows(left[:, :size], far_right[...])
        deal(grad, half, spot, kept, given)


def attend_weight_b_kernel(
    near, grad_in, far, far_other, right, far_right, far_right_other, vector, kept, given
):
    spot = where()
    size = near.shape[1] // 2
    rows = near.shape[0]
    below = kept.shape[1] - EXTRA
    even = spot[PART] == 0
    rights = jnp.where(even, far_right[:rows], far[:, size:])
    lefts = ((far, far_right), (far_other, far_right_other))
    for (left, back), (lines, half) in zip(lefts, halves(spot, size)):
        grad = dot_rows(jnp.where(even, near[:, lines], grad_in[:, lines]), right[...])
        grad += dot_rows(jnp.where(even, left[:, :size], back[:rows]), rights)
        deal(grad, half, spot, kept.at[:, :below], given.at[:, :below])
    total = vector[...] + far_right[rows : rows + EXTRA].astype(F32) + far_right[rows + EXTRA :].astype(F32)
    chips = 2 * kept.shape[0]
    parts = []
    for chip in range(chips):
        lines = []
        for row, extent in ((0, 4 * size), (2, size), (3, 2 * size)):
            each = extent // chips
            at = chip * each
            mine = spot[CORE] == at // (2 * size)
            if row == 0:
                at %= 2 * size
            piece = total[row + at // size : row + at // size + 1, at % size : at % size + each]
            lines.append(jnp.where(mine, piece, 0.0) if row == 0 else piece)
        parts.append(rows_of(lines, size))
    for i in range(chips // 2):
        low, high = parts[2 * i], parts[2 * i + 1]
        kept[i, below:] = jnp.where(spot[NEAR] == 0, low, high).astype(BF16)
        given[i, below:] = jnp.where(spot[NEAR] == 0, high, low).astype(BF16)


def fold_kernel(kept, received, out, given):
    spot = where()
    low = kept[0].astype(F32) + received[0].astype(F32)
    high = kept[1].astype(F32) + received[1].astype(F32)
    out[0] = jnp.where(spot[HIGH] == 0, low, high)
    given[0] = jnp.where(spot[HIGH] == 0, high, low).astype(BF16)


def close_kernel(extra, kept, received, out, given):
    spot = where()
    size = out.shape[0] - extra
    total = kept[0] + received[0].astype(F32)
    low, high = total[:size], total[size : 2 * size]
    out[:size] = jnp.where(spot[CORE] == 0, low, high)
    given[:size] = jnp.where(spot[CORE] == 0, high, low)
    if extra:
        out[size:] = total[2 * size :]
        given[size:] = total[2 * size :]


def attend_out_kernel(mine_a, theirs_a, mine, theirs, out, units, features, gain):
    first = where()[CORE] == 0
    size, half = mine_a.shape
    for at, own, other in ((0, mine_a[...], theirs_a[...]), (2 * half, mine[:size], theirs[:size])):
        out[:, at : at + half] = jnp.where(first, own, other)
        out[:, at + half : at + 2 * half] = jnp.where(first, other, own)
    total = mine[size:] + theirs[size:]
    for row, x in enumerate((units, features, gain)):
        each = x.shape[1]
        x[...] = jnp.where(first, total[row : row + 1, :each], total[row : row + 1, each : 2 * each])


def swap_section(x):
    return lax.ppermute(x, "section", [(i, i ^ 1) for i in range(lax.axis_size("section"))])


def swap_layer(x):
    return lax.ppermute(x, "section", [(i, i ^ 2) for i in range(lax.axis_size("section"))])


def swap_core(x):
    return lax.ppermute(x, "dp", [(i, i ^ 1) for i in range(lax.axis_size("dp"))])


def swap_chip(x, distance):
    return lax.ppermute(x, "dp", [(i, i ^ (2 * distance)) for i in range(lax.axis_size("dp"))])


def after(x, *others):
    return lax.optimization_barrier((x,) + others)[0]


def replica_sum(kept, given, z, chips):
    if chips > LINE:
        pair = jnp.where(z % 2 == 0, jnp.stack([kept, given], 1), jnp.stack([given, kept], 1))
        groups = [[2 * i + c for i in range(chips)] for c in (0, 1)]
        return lax.psum_scatter(
            pair.reshape(chips, *kept.shape[1:]),
            "dp",
            scatter_dimension=0,
            axis_index_groups=groups,
            tiled=False,
        ).astype(F32)
    distance = 1
    while True:
        total = kept.astype(F32) + swap_chip(given, distance).astype(F32)
        if total.shape[0] == 1:
            return total[0]
        distance *= 2
        bit = z // distance % 2
        pairs = total.reshape(total.shape[0] // 2, 2, *total.shape[1:])
        given = lax.dynamic_index_in_dim(pairs, 1 - bit, 1, keepdims=False).astype(given.dtype)
        kept = lax.dynamic_index_in_dim(pairs, bit, 1, keepdims=False)


def rotations(places):
    count = HEAD // 2
    freq = np.power(10000.0, -2.0 * np.arange(count, dtype=np.float32) / HEAD).astype(np.float32)
    angle = np.arange(places, dtype=np.float32)[:, None] * freq[None, :]
    cosine, sine = np.cos(angle), np.sin(angle)
    parts = [cosine] * (LANES // count) + [-sine, sine] * (LANES // HEAD)
    return jnp.asarray(np.concatenate(parts, axis=1).astype(np.float32))


def body(
    hidden_in,
    cotangent,
    doc_lengths,
    attn_weight,
    up_weight,
    down_weight,
    up_bias,
    down_bias,
    norm_gain,
):
    section = lax.axis_index("section")
    replica = lax.axis_index("dp")
    chips = lax.axis_size("dp") // 2
    part, layer = section % 2, section // 2
    core, z = replica % 2, replica // 2
    near = z % 2
    even, lead, first = part == 0, core == part, layer == 0
    micro, rows, width = hidden_in.shape[1:]
    total, half = micro * rows, width // 2
    hidden = up_weight.shape[2]
    blocks = micro * (half // LANES)

    def columns(x, at, size):
        return lax.dynamic_slice_in_dim(x, at, size, axis=1)

    def by_part(mine, theirs, axis):
        return jnp.where(
            even, jnp.concatenate([mine, theirs], axis), jnp.concatenate([theirs, mine], axis)
        )

    def by_core(mine, theirs, axis):
        return jnp.where(
            core == 0, jnp.concatenate([mine, theirs], axis), jnp.concatenate([theirs, mine], axis)
        )

    wide, narrow = ((total, width), BF16), ((total, half), BF16)
    pieces = [((rows, width), BF16)] * micro
    vectors = ((8, width), F32)

    shift_mine = lax.dynamic_slice_in_dim(up_bias[0], core * width, width, axis=0).astype(F32)
    small = jnp.concatenate([shift_mine, down_bias[0].astype(F32), norm_gain[0]])
    def given(at, array, place, shape, name):
        return cut(at, (array,), [(0, place)], [shape], name)[0]

    attn_given = given(
        None,
        attn_weight,
        lambda spot: (0, spot[NEAR] * width + spot[CORE] * half),
        (width, half),
        "cut_attn",
    )
    up_given = given(
        attn_given,
        up_weight,
        lambda spot: (spot[NEAR] * half, spot[CORE] * width),
        (half, width),
        "cut_up",
    )
    attn_near, up_near = swap_section(attn_given), swap_section(up_given)
    hidden_in, cotangent, doc_lengths, small = lax.optimization_barrier(
        (hidden_in, cotangent, doc_lengths, small, up_given)
    )[:4]
    hidden_in, cotangent = hidden_in.reshape(wide[0]), cotangent.reshape(wide[0])
    hidden_other, lengths_other = swap_core((hidden_in, doc_lengths[0]))
    middle_rows = width - 2 * LANES
    down_end, down_given = cut(
        after(hidden_other, small),
        (down_weight,),
        [
            (0, lambda spot: (spot[CORE] * width + spot[NEAR] * (width - LANES), 0)),
            (0, lambda spot: (spot[CORE] * width + LANES, 0)),
        ],
        [(LANES, width), (middle_rows, width)],
        "cut_down",
    )
    down_near, down_middle = swap_section(down_end), swap_section(down_given)
    attn_next, up_next = swap_chip(attn_near, 1), swap_chip(up_near, 1)
    attn_own = cut(
        up_given,
        (attn_weight,),
        [(0, lambda spot, i=i: (0, i * width + spot[CORE] * half)) for i in (0, 1)],
        [(width, half)] * 2,
        "cut_own",
    )
    feed_own = cut(
        down_end,
        (up_weight, down_weight),
        [(0, lambda spot: (0, spot[CORE] * width)), (1, lambda spot: (spot[CORE] * width, 0))],
        [(width, width)] * 2,
        "cut_feed",
    )
    small_theirs = after(swap_section(small), attn_next)
    scalars = pl.BlockSpec(memory_space=pltpu.SMEM)
    table = pl.pallas_call(
        lambda *refs: table_kernel(micro, *refs),
        out_shape=jax.ShapeDtypeStruct((total + 8, max(3 * LANES, total)), F32),
        in_specs=[scalars, scalars, VECTOR],
        out_specs=VECTOR,
        compiler_params=pltpu.CompilerParams(vmem_limit_bytes=8 * 1024 * 1024),
        name="table",
    )(after(doc_lengths[0], attn_near), lengths_other, rotations(rows // 2))
    down_shift = by_part(small[width : width + half], small_theirs[width : width + half], 0)
    gains = [jnp.pad(x[width + half :], (0, width)) for x in (small, small_theirs)]
    params = jnp.stack(
        [
            jnp.where(even, gains[0], gains[1]),
            jnp.where(even, gains[1], gains[0]),
            jnp.pad(down_shift, (0, width)),
            jnp.concatenate([shift_mine, small_theirs[:width]]),
        ]
    )
    params = jnp.pad(params, ((0, 4), (0, 0)))

    def ordered(mine, theirs, *between):
        low, high = jnp.where(near == 0, mine, theirs), jnp.where(near == 0, theirs, mine)
        return jnp.concatenate([low, *between, high], axis=0)

    low, high = jnp.where(near == 0, attn_near, attn_next), jnp.where(near == 0, attn_next, attn_near)
    attn = (
        jnp.where(even, attn_own[0], low),
        jnp.where(even, attn_own[1], high),
        jnp.where(even, low, attn_own[0]),
        jnp.where(even, high, attn_own[1]),
    )

    def attend(streams, keep):
        arrived = len(streams) == 3
        outs, scratch = pieces + [wide], [pltpu.VMEM(*narrow)] * 4
        if keep:
            outs, scratch = outs + [wide] + [narrow] * 4 + [((blocks, rows, 2 * rows), F32), wide], ()
        out = call(
            lambda *refs: attend_kernel(micro, keep, arrived, *refs),
            (*streams, params, table, *attn),
            outs,
            scratch,
            "attend",
        )
        return out[:micro], out[micro:]

    own_part, (stream_0,) = attend((hidden_in, hidden_other), False)
    down_next = swap_chip(after(down_near, own_part[0]), 1)
    middle, *active = call(
        lambda *refs: feed_up_kernel(micro, *refs),
        (
            stream_0,
            *own_part,
            *swap_core(own_part),
            params,
            feed_own[0],
            up_near,
            up_next,
            feed_own[1],
        ),
        [wide] * 2 + [(wide[0], F32)],
        [pltpu.VMEM(*wide)] * 2,
        name="feed_up",
    )
    own_part = call(
        feed_down_kernel, (active[1], active[0], down_near, down_middle, down_next), pieces, name="feed_down"
    )
    arrived = call(
        lambda *refs: finish_kernel(micro, *refs),
        (middle, *own_part, *swap_core(own_part), params),
        [narrow],
        [pltpu.VMEM(*wide)],
        "finish",
    )[0]
    ups = (feed_own[0], ordered(after(up_near, arrived), up_next))
    downs = (feed_own[1], ordered(after(down_near, arrived), down_next, down_middle))
    arrived = after(swap_layer(arrived), ups[1], downs[1])
    own_part, kept = attend((arrived, swap_core(arrived), stream_0), True)
    stream, normed_attn, q, k, v, mixed, chance, pay_attn = kept
    far_attn = swap_section(pay_attn)
    out = call(
        lambda *refs: feed_kernel(micro, *refs),
        (stream, *own_part, *swap_core(own_part), params, *ups, *downs),
        pieces + [wide] * 3 + [((total, 2 * width), BF16), ((total, width + half), BF16)],
        [pltpu.VMEM(*wide)],
        "feed",
    )
    fed, (middle, normed_feed, active_mine, slope, pay) = out[:micro], out[micro:]
    far = swap_section(pay)

    def feed_back(upstreams, arrived, held=()):
        outs, scratch = pieces + [wide], [pltpu.VMEM(*wide)] * 2
        if arrived:
            outs, scratch = outs + [wide, wide, vectors], ()
        out = call(
            lambda *refs: feed_back_kernel(micro, arrived, *refs),
            (*upstreams, slope, *ups, *downs),
            outs,
            scratch,
            "feed_back",
            held,
        )
        return out[:micro], out[micro:]

    def attend_back(upstream, own, other, params, keep, held=()):
        outs = pieces + [wide]
        more = ()
        if keep:
            outs += [((EXTRA, half), F32)] + [narrow] * 3 + [((total + 2 * EXTRA, half), BF16)]
            more = keep
        out = call(
            lambda *refs: attend_back_kernel(micro, bool(keep), *refs),
            (upstream, *own, *other, middle, params, chance, v, k, q, mixed, table, *attn, *more),
            outs,
            [pltpu.VMEM(*narrow)] * 4,
            "attend_back",
            held,
        )
        return out[:micro], out[micro:]

    kept_on = (slope, *fed, *ups, *downs, active_mine)
    cotangent_other = swap_core(after(cotangent, arrived))
    own_part, (upstream_0,) = feed_back((cotangent, cotangent_other), False, kept_on)
    own_part, (grad,) = attend_back(
        upstream_0, own_part, swap_core(own_part), params, (), kept_on
    )
    *own_part, far_attn = lax.optimization_barrier((*own_part, far_attn))
    grad_2, arrived = call(
        lambda *refs: norm_back_kernel(micro, *refs),
        (grad, *own_part, *swap_core(own_part), stream, params),
        [wide, narrow],
        name="norm_back",
        held=kept_on,
    )
    arrived = swap_layer(arrived)
    upstream_half = after(columns(upstream_0, core * half, half), grad_2)

    def weight(kernel, args, shape, name, extra=0):
        outs = [((chips // 2, shape[0] // chips + extra, shape[1]), BF16)] * 2
        return call(kernel, args, outs, name=name)

    def folded(grad, token):
        kept, given = grad
        if chips != LINE:
            return replica_sum(kept, given, z, chips)
        received = after(swap_chip(given, 1), token)
        part = (1, *kept.shape[1:])
        return call(fold_kernel, (kept, received), [(part, F32), (part, BF16)], name="fold")

    def closed(fold, token, extra=0):
        if chips != LINE:
            size = (fold.shape[0] - extra) // 2
            mine = lax.dynamic_slice_in_dim(fold, core * size, size, axis=0)
            theirs = lax.dynamic_slice_in_dim(fold, (1 - core) * size, size, axis=0)
            mine, theirs = [jnp.concatenate([x, fold[2 * size :]], axis=0) for x in (mine, theirs)]
            return mine, swap_core(theirs)
        kept, given = fold
        received = after(swap_chip(given, 2), token)
        part = (((kept.shape[-2] + extra) // 2, kept.shape[-1]), F32)
        mine, theirs = call(
            lambda *refs: close_kernel(extra, *refs), (kept, received), [part] * 2, name="close"
        )
        return mine, swap_core(theirs)

    x = types.SimpleNamespace(far=far, far_attn=far_attn)

    def take_upstream(token):
        x.half = jnp.where(first, after(arrived, token), upstream_half)
        x.half_other, x.far_half = swap_core(x.half), swap_section(x.half)
        return x.half

    def take_far(token):
        x.far = after(x.far, token)
        x.far_other = swap_core(x.far)
        return x.far

    def send_active(token):
        x.active_other = swap_core(after(active_mine, token))
        return token

    def feed_step(token):
        x.part, back = feed_back((after(x.half, token), x.half_other), True)
        x.upstream, x.back, theirs, x.sums = back
        x.far_back, x.part_other = swap_section(theirs), swap_core(x.part)
        return x.upstream

    def take_attn(token):
        x.far_attn = after(x.far_attn, token)
        return x.far_attn

    def attend_step(token):
        part, other = x.part, x.part_other
        x.part, back = attend_back(x.upstream, part, other, after(params, token), (stream, x.sums))
        x.grad, x.vector, x.rhs_a, x.rhs_b, pay_a, pay_b = back
        x.far_rhs_a, x.far_rhs_b = swap_section(pay_a), swap_section(pay_b)
        return x.grad

    def send_attn(token):
        x.far_attn_other = swap_core(after(x.far_attn, token))
        return token

    def take_half(token):
        x.far_half = after(x.far_half, token)
        return x.far_half

    def take_back(token):
        x.far_back = after(x.far_back, token)
        return x.far_back

    def take_rhs_a(token):
        x.far_rhs_a = after(x.far_rhs_a, token)
        return x.far_rhs_a

    def take_rhs_b(token):
        x.far_rhs_b = after(x.far_rhs_b, token)
        x.far_rhs_b_other = swap_core(x.far_rhs_b)
        return x.far_rhs_b

    def down_near_step(token):
        args = (active_mine, x.active_other, after(x.half, token))
        x.down = call(down_near_kernel, args, [((2, width, half), F32)], name="down_near")[0]
        return x.down

    def down_step(token):
        args = (x.down, x.far, x.far_other, after(x.far_half, token))
        x.down = weight(down_weight_kernel, args, (hidden, half), "down_weight")
        return x.down[0]

    def up_step(token):
        args = (normed_feed, x.far, x.far_other, x.back, after(x.far_back, token))
        x.up = weight(up_weight_kernel, args, (width, width), "up_weight")
        return x.up[0]

    def attn_step_a(token):
        args = (normed_attn, x.far_attn, x.far_attn_other, x.rhs_a, after(x.far_rhs_a, token))
        x.attn_a = weight(attend_weight_a_kernel, args, (width, half), "attend_weight_a")
        return x.attn_a[0]

    def attn_step_b(token):
        args = (normed_attn, x.grad, x.far_attn, x.far_attn_other, x.rhs_b)
        args += (after(x.far_rhs_b, token), x.far_rhs_b_other, x.vector)
        x.attn_b = weight(attend_weight_b_kernel, args, (width, half), "attend_weight_b", EXTRA)
        return x.attn_b[0]

    def norm_step(token):
        x.grads, x.grads_given = call(
            lambda *refs: norm_end_kernel(micro, *refs),
            (x.grad, *x.part, *swap_core(x.part), stream, after(params, token)),
            [wide, wide],
            name="norm_end",
        )
        return x.grads

    def send_fed(token):
        x.fed_other = swap_core([after(y, token) for y in fed])
        return token

    def last_step(token):
        x.outputs, x.outputs_given = call(
            lambda *refs: last_kernel(micro, *refs),
            (middle, *fed, *x.fed_other, after(params, token)),
            [wide, wide],
            name="last",
        )
        return x.outputs

    def send_outputs(token):
        x.outputs_far = swap_section(after(x.outputs_given, token))
        return token

    def send_grads(token):
        x.grads_far = swap_section(after(x.grads_given, token))
        return token

    def take_outputs(token):
        x.outputs = jnp.where(lead, x.outputs, after(x.outputs_far, token))
        return x.outputs

    def take_grads(token):
        x.grads = jnp.where(lead, x.grads, after(x.grads_far, token))
        return x.grads

    def down_fold(token):
        x.down = folded(x.down, token)
        return x.down[0]

    def up_fold(token):
        x.up = folded(x.up, token)
        return x.up[0]

    def attn_fold_a(token):
        x.attn_a = folded(x.attn_a, token)
        return x.attn_a[0]

    def attn_fold_b(token):
        x.attn_b = folded(x.attn_b, token)
        return x.attn_b[0]

    def down_close(token):
        x.down = closed(x.down, token)
        return x.down[0]

    def up_close(token):
        x.up = closed(x.up, token)
        return x.up[0]

    def attn_close_a(token):
        x.attn_a = closed(x.attn_a, token)
        return x.attn_a[0]

    def attn_close_b(token):
        x.attn_b = closed(x.attn_b, token, EXTRA)
        return x.attn_b[0]

    token = grad_2
    for step in (
        take_upstream,
        take_far,
        send_active,
        feed_step,
        down_near_step,
        take_half,
        down_step,
        take_attn,
        attend_step,
        send_attn,
        take_back,
        up_step,
        down_fold,
        norm_step,
        take_rhs_a,
        attn_step_a,
        take_rhs_b,
        attn_step_b,
        send_grads,
        send_fed,
        up_fold,
        attn_fold_a,
        down_close,
        last_step,
        send_outputs,
        attn_fold_b,
        up_close,
        take_grads,
        take_outputs,
        attn_close_a,
        attn_close_b,
    ):
        token = step(token)

    size = width // (2 * chips)
    if chips == LINE:
        attn_out, up_shift_out, down_shift_out, gain_out = call(
            attend_out_kernel,
            (*x.attn_a, *x.attn_b),
            [((size, hidden), F32)] + [((1, y // (2 * chips)), F32) for y in (hidden, half, width)],
            name="attend_out",
        )
    else:
        attn_out = jnp.concatenate(
            [by_core(*x.attn_a, 1), by_core(*[y[:size] for y in x.attn_b], 1)], axis=1
        )
        vector = x.attn_b[0][size:] + x.attn_b[1][size:]
        up_shift_out, down_shift_out, gain_out = [
            columns(vector[i : i + 1], core * (y // (2 * chips)), y // (2 * chips))
            for i, y in enumerate((hidden, half, width))
        ]
    up_out, down_out = by_core(*x.up, 1), by_core(*x.down, 1)

    shape = (1, 1, micro, rows, width)
    return (
        x.outputs.reshape(shape),
        x.grads.reshape(shape),
        attn_out[None],
        up_out[None],
        down_out[None],
        up_shift_out,
        down_shift_out,
        gain_out,
    )


def solution(mesh):
    in_specs = (
        P("dp", None, None, None),
        P("dp", None, None, None),
        P("dp", None, None),
        P("section", None, None),
        P("section", None, None),
        P("section", None, None),
        P("section", None),
        P("section", None),
        P("section", None),
    )
    out_specs = (
        P("section", "dp", None, None, None),
        P("section", "dp", None, None, None),
        P("section", "dp", None),
        P("section", "dp", None),
        P("section", "dp", None),
        P("section", "dp"),
        P("section", "dp"),
        P("section", "dp"),
    )
    return jax.shard_map(body, mesh=mesh, in_specs=in_specs, out_specs=out_specs, check_vma=False)
```
